128 devices in a mesh: tm: 32 (over x, z, core), state: 4 (over y).
Axes of the slice: x: 4, y: 4, z: 4, core: 2. Of those that a mesh axis runs over, the one named last changes fastest.
Arguments:
- dyn_cols: int32 [1024, 8, 3], P('tm', 'state'), may hold values from 0 to 7, as said below
- dyn_vals: bfloat16 [1024, 8, 64, 192], P('tm', 'state'), may hold values from -1 to 1
- obs_blocks: int32 [1024, 2], P('tm'), may hold values from 0 to 7
- obs_op: bfloat16 [1024, 64, 128], P('tm'), may hold values from -0.75 to 0.75
- obs_counts: int32 [1024], P('tm'), may hold values from 32 to 128, as said below
- obs_values: float32 [1024, 128], P('tm'), may hold values from -6 to 6
- gain: bfloat16 [1024, 512, 128], P('tm', 'state'), may hold values from -0.0078125 to 0.0078125
- sources: float32 [1024, 512], P('tm', 'state'), may hold values from -0.625 to 0.625
- prior: float32 [512], replicated, may hold values from -6 to 6
Outputs:
- filtered: float32 [1024, 512], P('tm', 'state')
The draws below stay inside these ranges and needn't reach their ends.
Inputs may be any that keep to these rules, and one draw needn't show every extreme that they name: `dyn_cols`: for every step and block row i, the first entry is i itself and the 3 entries are distinct block columns. `obs_counts`: some step has all 128 observations present.
All inputs are finite; a program needn't handle non-finite values.
Results may differ from the reference program's by a relative error of at most 0.0003.
The reference program's roundings to bfloat16 on the way count: a program that leaves them out, or rounds other values in their place, can miss the bound.
Values may be sent and summed in bfloat16 or wider, within the bound.
A program may use at most 128 MiB of HBM per device.

```python
import math
import jax
import jax.numpy as jnp
from jax import lax

NS = 512
BS = 64
KF = 3
OBS = 128
NB = 8
OB = 2
HORIZON_LENGTH = 1024


def draw_dyn_cols(key, part):
    scores = jax.random.randint(key, (HORIZON_LENGTH, NB, NB - 1), 0, 1 << 20) * NB + jnp.arange(NB - 1)
    picked = lax.top_k(scores, KF - 1)[1] + 1
    row_index = jnp.arange(NB)[None, :, None]
    others = (row_index + picked) % NB
    leading = jnp.broadcast_to(row_index, (HORIZON_LENGTH, NB, 1))
    return jnp.concatenate([leading, others], axis=2).astype(jnp.int32)


def draw_dyn_vals(key, part):
    quick_decay_seed, speed_seed, layer_level_seed, spike_seed, decay_seed, perturbation_seed = jax.random.split(key, 6)
    share = 0.25
    fast = jax.random.uniform(quick_decay_seed, (NB, BS)) < share
    fast_rate = jnp.exp(-jax.random.uniform(speed_seed, (NB, BS), minval=1.0 / 50.0, maxval=1.0 / 30.0))
    depth = jax.random.uniform(layer_level_seed, (HORIZON_LENGTH, NB, BS), minval=0.25, maxval=1.25)
    gradual_decay_speed = 1.0 - 0.002 * depth
    spike_location = jax.random.randint(spike_seed, (2,), 0, HORIZON_LENGTH)
    spike_struck_flags = jnp.any(jnp.arange(HORIZON_LENGTH)[:, None] == spike_location[None, :], axis=1)
    decay_factor = jax.random.uniform(decay_seed, (HORIZON_LENGTH, NB, BS), minval=0.5, maxval=0.8)
    gradual_decay_speed = jnp.where(spike_struck_flags[:, None, None], gradual_decay_speed * decay_factor, gradual_decay_speed)
    rate = jnp.where(fast[None, :, :], fast_rate[None, :, :], gradual_decay_speed)
    diagonal = rate[..., None] * jnp.eye(BS, dtype=jnp.float32)
    padding = jnp.zeros((HORIZON_LENGTH, NB, BS, (KF - 1) * BS), jnp.float32)
    leading = jnp.concatenate([diagonal, padding], axis=3)
    off_diag = 1.0 - jnp.concatenate([jnp.eye(BS, dtype=jnp.float32), jnp.zeros((BS, (KF - 1) * BS), jnp.float32)], axis=1)
    noise = jax.random.truncated_normal(perturbation_seed, -4.0, 4.0, (HORIZON_LENGTH, NB, BS, KF * BS)) * (0.014 / math.sqrt(KF * BS))
    return (leading + noise * off_diag).astype(jnp.bfloat16)


def draw_obs_counts(key, part):
    key_count, key_where = jax.random.split(key, 2)
    counts = jax.random.randint(key_count, (HORIZON_LENGTH,), OBS // 4, OBS + 1)
    where_full = jax.random.randint(key_where, (), 0, HORIZON_LENGTH)
    return jnp.where(jnp.arange(HORIZON_LENGTH) == where_full, OBS, counts).astype(jnp.int32)


def plant(drawn, own_key, low, top_value):
    dims = drawn.shape
    index_at = [jax.random.randint(jax.random.fold_in(own_key, axis), (), 0, dims[axis]) for axis in range(len(dims))]
    drawn = drawn.at[tuple(index_at)].set(low)
    longest = dims.index(max(dims))
    index_at[longest] = (index_at[longest] + 1) % dims[longest]
    return drawn.at[tuple(index_at)].set(top_value)


def block_levels(key, extent, shards, smallest, high):
    level, own = 1.0, jax.random.fold_in(key, 6)
    for position, shards_of in shards:
        steps = jnp.exp(jax.random.uniform(jax.random.fold_in(own, position), (shards_of,), jnp.float32, smallest / len(shards), high / len(shards)))
        level = level * jnp.repeat(steps, extent[position] // shards_of).reshape([-1 if axis == position else 1 for axis in range(len(extent))])
    return level


def scatter_about(own_key, shape, deviation, most, shards=(), kind=jnp.bfloat16):
    result = jax.random.normal(own_key, shape, jnp.float32) * deviation
    if len(shards) > 0:
        result = block_levels(own_key, shape, shards, -0.22, 0.18) * result
    return jnp.clip(result, min=-most, max=most).astype(kind)


def setup_inputs(seed: int = 0) -> dict:
    key_of = jax.random.split(jax.random.key(seed), 10)
    return {
        "dyn_cols": draw_dyn_cols(jax.random.fold_in(key_of[9], 71), 0),
        "dyn_vals": draw_dyn_vals(jax.random.fold_in(key_of[9], 71), 0),
        "obs_blocks": plant(jax.random.randint(key_of[2], (HORIZON_LENGTH, OB), 0, NB), jax.random.fold_in(key_of[2], 1), 0, NB - 1).astype(jnp.int32),
        "obs_op": scatter_about(key_of[3], (HORIZON_LENGTH, BS, OBS), BS ** -0.5, 0.75, ((0, 32),)),
        "obs_counts": draw_obs_counts(jax.random.fold_in(key_of[9], 71), 0),
        "obs_values": scatter_about(key_of[5], (HORIZON_LENGTH, OBS), 1.0, 6.0, ((0, 32),), jnp.float32),
        "gain": scatter_about(key_of[6], (HORIZON_LENGTH, NS, OBS), (4000 * OBS) ** -0.5, 0.0078125, ((0, 32), (1, 4))),
        "sources": scatter_about(key_of[7], (HORIZON_LENGTH, NS), 0.04, 0.625, ((0, 32), (1, 4)), jnp.float32),
        "prior": scatter_about(key_of[8], (NS,), 1.0, 6.0, (), jnp.float32),
    }


HIGHEST = lax.Precision.HIGHEST


def assemble(columns, values):
    count_rows = columns.shape[0]
    onehot = (columns[:, :, None] == jnp.arange(NB)[None, None, :]).astype(jnp.float32)
    blocks = values.reshape(count_rows, BS, KF, BS).astype(jnp.float32)
    assembled = jnp.einsum('rkc,rakb->racb', onehot, blocks, precision=HIGHEST)
    return assembled.reshape(count_rows * BS, NS)


def reference(dyn_cols, dyn_vals, obs_blocks, obs_op, obs_counts, obs_values, gain, sources, prior):
    def advance(state_mean, inputs):
        columns, values, observed, operator, count, measured, gain_step, source = inputs
        forward = assemble(columns, values)
        selected = forward.reshape(NB, BS, NS)[observed]
        source_blocks = source.reshape(NB, BS)[observed]
        operator_blocks = operator.reshape(BS, OB, BS).astype(jnp.float32)
        image = jnp.einsum('boa,obn->oan', operator_blocks, selected, precision=HIGHEST)
        image = image.reshape(OBS, NS).astype(jnp.bfloat16)
        source_image = jnp.einsum('boa,ob->oa', operator_blocks, source_blocks, precision=HIGHEST)
        source_image = source_image.reshape(OBS).astype(jnp.bfloat16)
        active = jnp.arange(OBS) < count
        masked = jnp.where(active[:, None], image, jnp.zeros((), jnp.bfloat16))
        innovation = jnp.where(active, measured - lax.optimization_barrier(source_image).astype(jnp.float32), 0.0)
        correction = jnp.dot(gain_step, masked, preferred_element_type=jnp.float32)
        element = (forward - correction).astype(jnp.bfloat16)
        offset = source + jnp.dot(gain_step.astype(jnp.float32), innovation, precision=HIGHEST)
        new_mean = jnp.dot(element.astype(jnp.float32), state_mean, precision=HIGHEST) + offset
        return new_mean, new_mean

    _, filtered = lax.scan(advance, prior, (dyn_cols, dyn_vals, obs_blocks, obs_op, obs_counts, obs_values, gain, sources))
    return filtered
```

```python
import jax
import jax.numpy as jnp
from jax import lax
from jax.experimental import pallas as pl
from jax.experimental.pallas import tpu as pltpu
from jax.sharding import PartitionSpec as P

MESH = pl.DeviceIdType.MESH
F32 = jnp.float32
BF16 = jnp.bfloat16
NS = 512
HALF = 256
STEPS = 8
CHUNK = 2
NCHUNK = STEPS // CHUNK


def split(value):
    high = value.astype(BF16)
    low = (value - high.astype(F32)).astype(BF16)
    return high, low


def column_to_row(column):
    rows = lax.broadcasted_iota(jnp.int32, (128, 128), 0)
    lanes = lax.broadcasted_iota(jnp.int32, (128, 128), 1)
    return jnp.sum(jnp.where(rows == lanes, column, 0.0), axis=0, keepdims=True)


def matvec(load, vector):
    out = []
    for g in range(4):
        total = load(g, 0) * vector[0]
        for j in range(1, 4):
            total = total + load(g, j) * vector[j]
        out.append(column_to_row(jnp.sum(total, axis=1, keepdims=True)))
    return out


def rows_of(ref):
    return [ref[g : g + 1, :] for g in range(4)]


def put_rows(ref, rows):
    for g in range(4):
        ref[g : g + 1, :] = rows[g]


def block_of_map(ref):
    def load(g, j):
        rows, lanes = pl.ds(g * 128, 128), pl.ds((j % 2) * 128, 128)
        return ref[j // 2, 0, rows, lanes].astype(F32) + ref[j // 2, 1, rows, lanes].astype(F32)

    return load


def block_of_plain(ref):
    def load(g, j):
        return ref[pl.ds(g * 128, 128), pl.ds(j * 128, 128)].astype(F32)

    return load


def product(left, right):
    total = None
    for h in range(2):
        rows = pl.ds(h * HALF, HALF)
        for a, b in ((0, 0), (0, 1), (1, 0)):
            term = jnp.dot(left[h, a], right[b, rows, :], preferred_element_type=F32)
            total = term if total is None else total + term
    return total


def to_plain(ref, out):
    for h in range(2):
        out[:, h * HALF : (h + 1) * HALF] = ref[h, 0].astype(F32) + ref[h, 1].astype(F32)


def kernel(
    columns_count,
    vals_ref, gain_ref, obs_op_ref, meta_ref, obs_values_ref, sources_ref, prior_ref,
    out_ref,
    packed, a_buf, b_buf, gain_buf, src_buf, meta_buf, meta_smem, op_buf, ov_buf,
    f_buf, fn_buf, e_buf, off_buf,
    maps, maps_q, chip, chip_q, partial, partial_q, before, before_q, whole,
    plain_a, plain_b, plain_c, x_in, x_out, x_work, sweep_buf,
    send_in, recv_in, send_small, recv_small, send_obs, recv_obs, smem_sem,
    send_map, recv_map, send_chip, recv_chip, send_y, recv_y, send_yq, recv_yq,
    send_left, recv_left, send_x, recv_x, send_out, recv_out, send_full, recv_full,
):
    tm, y = lax.axis_index("tm"), lax.axis_index("state")
    core = lax.rem(tm, 2)
    column = tm // 2
    first_tm = tm - core
    other = 1 - core
    sibling = (first_tm + other, y)
    last = columns_count - 1

    barrier = pltpu.get_barrier_semaphore()
    for c in range(2):
        for j in range(4):
            @pl.when(jnp.logical_or(c != core, j != y))
            def _():
                pl.semaphore_signal(barrier, inc=1, device_id=(first_tm + c, j), device_id_type=MESH)

    @pl.when(column > 0)
    def _():
        pl.semaphore_signal(barrier, inc=1, device_id=(tm - 2, 3), device_id_type=MESH)

    def pack(s, carry):
        left = vals_ref[s, 0, :, 128:192]
        right = vals_ref[s, 1, :, 128:192]
        packed[s] = jnp.concatenate([left, right], axis=1)
        return carry

    lax.fori_loop(0, 4 * STEPS, pack, 0)

    sends_on = jnp.logical_and(y == 3, column < last)

    @pl.when(sends_on)
    def _():
        pl.semaphore_wait(barrier, 11)

    @pl.when(jnp.logical_not(sends_on))
    def _():
        pl.semaphore_wait(barrier, 7)

    def target_of(b):
        return first_tm + b % 2, 2 * core + b // 2

    def is_me(b):
        dest_tm, dest_y = target_of(b)
        return jnp.logical_and(dest_tm == tm, dest_y == y)

    def remote(src, dst, send, recv, device):
        return pltpu.make_async_remote_copy(
            src_ref=src, dst_ref=dst, send_sem=send, recv_sem=recv, device_id=device, device_id_type=MESH
        )

    def small_pairs(b):
        start = pl.ds(8 * b, STEPS)
        return (
            (sources_ref.at[start], src_buf.at[y], 0),
            (meta_ref.at[start], meta_buf.at[y], 1),
        )

    def big_pairs(b, q):
        start, there = pl.ds(8 * b + CHUNK * q, CHUNK), pl.ds(CHUNK * q, CHUNK)
        return (
            (vals_ref.at[start, :, :, pl.ds(0, 128)], a_buf.at[y, there], 0),
            (packed.at[start], b_buf.at[y, there], 1),
            (gain_ref.at[start], gain_buf.at[y, there], 2),
        )

    def send_pair(b, src, dst, send, recv):
        @pl.when(jnp.logical_not(is_me(b)))
        def _():
            remote(src, dst, send, recv, target_of(b)).start()

        @pl.when(is_me(b))
        def _():
            pltpu.make_async_copy(src, dst, recv).start()

    for b in range(4):
        for src, dst, kind in small_pairs(b):
            send_pair(b, src, dst, send_small.at[b, kind], recv_small.at[y, kind])

    holds = core == y // 2
    mine_at = pl.ds(16 * lax.rem(y, 2) + 8 * core, STEPS)
    other_at = pl.ds(16 * lax.rem(y, 2) + 8 * other, STEPS)
    obs_arrays = ((obs_op_ref, op_buf, 0), (obs_values_ref, ov_buf, 1))

    @pl.when(holds)
    def _():
        for src, dst, kind in obs_arrays:
            remote(src.at[other_at], dst, send_obs.at[kind], recv_obs.at[kind], sibling).start()
            pltpu.make_async_copy(src.at[mine_at], dst, recv_obs.at[kind]).start()

    def start_chunk(q, carry):
        for b in range(4):
            for src, dst, kind in big_pairs(b, q):
                send_pair(b, src, dst, send_in.at[b, kind, q], recv_in.at[y, kind, q])
        return carry

    lax.fori_loop(0, NCHUNK, start_chunk, 0)

    def arrived(dst, sem):
        pltpu.make_async_copy(dst, dst, sem).wait()

    for j in range(4):
        arrived(src_buf.at[j], recv_small.at[j, 0])
        arrived(meta_buf.at[j], recv_small.at[j, 1])
    for src, dst, kind in obs_arrays:
        arrived(dst, recv_obs.at[kind])
    to_smem = pltpu.make_async_copy(meta_buf, meta_smem, smem_sem)
    to_smem.start()
    to_smem.wait()

    lane64 = lax.broadcasted_iota(jnp.int32, (64, 128), 1)
    row64 = lax.broadcasted_iota(jnp.int32, (64, 128), 0)
    left64 = lane64 < 64
    half64 = lane64 // 64
    lane1 = lax.broadcasted_iota(jnp.int32, (1, 128), 1)

    maps_q[core] = jnp.zeros((8, 128), F32)

    def step(s, carry):
        @pl.when(lax.rem(s, CHUNK) == 0)
        def _():
            q = s // CHUNK
            there = pl.ds(CHUNK * q, CHUNK)
            for j in range(4):
                arrived(a_buf.at[j, there], recv_in.at[j, 0, q])
                arrived(b_buf.at[j, there], recv_in.at[j, 1, q])
                arrived(gain_buf.at[j, there], recv_in.at[j, 2, q])

        for j in range(4):
            third = b_buf[j, s].astype(F32)
            third_turned = pltpu.roll(third, 64, 1)
            for il in range(2):
                i = 2 * j + il
                pair = a_buf[j, s, il].astype(F32)
                turned = pltpu.roll(pair, 64, 1)
                block0 = jnp.where(left64, pair, turned)
                block1 = jnp.where(left64, turned, pair)
                block2 = jnp.where(left64 if il == 0 else jnp.logical_not(left64), third, third_turned)
                col1 = meta_smem[j, s, 3 * il + 1]
                col2 = meta_smem[j, s, 3 * il + 2]
                for p in range(4):
                    index = half64 + 2 * p
                    value = jnp.where(index == col1, block1, jnp.where(index == col2, block2, 0.0))
                    if p == j:
                        value = jnp.where(half64 == il, block0, value)
                    f_buf[i, :, p * 128 : (p + 1) * 128] = value
                    fn_buf[i, :, p * 128 : (p + 1) * 128] = value.astype(BF16)

        operator = op_buf[s].astype(F32)
        turned_operator = operator.T.astype(BF16)
        count = meta_smem[0, s, 8]
        images, source_columns = [], []
        for o in range(2):
            block = meta_smem[0, s, 6 + o]
            selected = fn_buf[block]
            images.append(jnp.dot(turned_operator[64 * o : 64 * o + 64], selected, preferred_element_type=F32))
            source_row = src_buf[block // 2, pl.ds(s, 1), :]
            offset = lax.rem(block, 2) * 64
            source_columns.append(
                jnp.sum(jnp.where(lane64 == row64 + offset, source_row, 0.0), axis=1, keepdims=True)
            )
        image = jnp.concatenate(images, axis=0)
        slot = lax.broadcasted_iota(jnp.int32, (128, NS), 0)
        masked = jnp.where(slot < count, image, 0.0).astype(BF16)
        gains = gain_buf[:, s].reshape(NS, 128)
        correction = jnp.dot(gains, masked, preferred_element_type=F32)
        e_buf[s] = (f_buf[...].reshape(NS, NS) - correction).astype(BF16)

        source_image = jnp.sum(
            operator * jnp.where(left64, source_columns[0], source_columns[1]), axis=0, keepdims=True
        )
        source_image = source_image.astype(BF16).astype(F32)
        innovation = jnp.where(lane1 < count, ov_buf[pl.ds(s, 1), :] - source_image, 0.0)
        offsets = []
        for g in range(4):
            moved = jnp.sum(gain_buf[g, s].astype(F32) * innovation, axis=1, keepdims=True)
            offsets.append(column_to_row(moved) + src_buf[g, pl.ds(s, 1), :])
        put_rows(off_buf.at[s], offsets)

        moved = matvec(block_of_plain(e_buf.at[s]), rows_of(maps_q.at[core]))
        put_rows(maps_q.at[core], [m + o for m, o in zip(moved, offsets)])

        @pl.when(s == 0)
        def _():
            for h in range(2):
                maps[core, h, 0] = e_buf[s, :, h * HALF : (h + 1) * HALF]
                maps[core, h, 1] = jnp.zeros((NS, HALF), BF16)

        @pl.when(s > 0)
        def _():
            for h in range(2):
                matrix = e_buf[s]
                value = jnp.dot(matrix, maps[core, h, 0], preferred_element_type=F32)
                value = value + jnp.dot(matrix, maps[core, h, 1], preferred_element_type=F32)
                maps[core, h, 0], maps[core, h, 1] = split(value)

        return carry

    lax.fori_loop(0, STEPS, step, 0)

    map_copy = remote(maps.at[core], maps.at[core], send_map.at[0], recv_map.at[0], sibling)
    q_copy = remote(maps_q.at[core], maps_q.at[core], send_map.at[1], recv_map.at[1], sibling)
    map_copy.start()
    q_copy.start()
    arrived(maps_q.at[other], recv_map.at[1])
    arrived(maps.at[other], recv_map.at[0])
    chip[y, core, 0], chip[y, core, 1] = split(product(maps.at[1], maps.at[0, core]))
    moved = matvec(block_of_map(maps.at[1]), rows_of(maps_q.at[0]))
    put_rows(chip_q.at[y], [m + o for m, o in zip(moved, rows_of(maps_q.at[1]))])

    def y_copies(d):
        there = (tm, lax.rem(y + d, 4))
        return (
            remote(chip.at[y, core], chip.at[y, core], send_y.at[d], recv_y.at[y], there),
            remote(chip_q.at[y], chip_q.at[y], send_yq.at[d], recv_yq.at[y], there),
        )

    for d in (1, 2, 3):
        @pl.when(y + d <= 3)
        def _():
            for copy in y_copies(d):
                copy.start()

    own_copy = remote(chip.at[y, core], chip.at[y, core], send_chip, recv_chip, sibling)

    @pl.when(y == 3)
    def _():
        own_copy.start()

    to_plain(maps.at[0], plain_c)

    def left_copy(l):
        return remote(chip.at[l, core], chip.at[l, core], send_left.at[l], recv_left.at[l], sibling)

    for l in range(3):
        @pl.when(l < y)
        def _():
            arrived(chip_q.at[l], recv_yq.at[l])
    for l in (2, 1):
        @pl.when(l < y)
        def _():
            arrived(chip.at[l, core], recv_y.at[l])
            left_copy(l).start()

    @pl.when(y > 0)
    def _():
        arrived(chip.at[0, core], recv_y.at[0])
        partial[...] = chip[0, core]
        partial_q[...] = chip_q[0]

    def extend(l):
        high, low = split(product(chip.at[l], partial))
        partial[0], partial[1] = high, low
        moved = matvec(block_of_map(chip.at[l]), rows_of(partial_q))
        put_rows(partial_q, [m + o for m, o in zip(moved, rows_of(chip_q.at[l]))])

    for l in (1, 2):
        @pl.when(l < y)
        def _():
            arrived(chip.at[l, other], recv_left.at[l])
            extend(l)

    @pl.when(y > 0)
    def _():
        before[core] = partial[...]
        before_q[...] = partial_q[...]
        remote(before.at[core], before.at[core], send_full.at[0], recv_full.at[0], sibling).start()

    @pl.when(y == 3)
    def _():
        arrived(chip.at[y, other], recv_chip)
        extend(3)
        whole[core] = partial[...]
        copy = remote(whole.at[core], whole.at[core], send_full.at[1], recv_full.at[1], sibling)
        copy.start()
        arrived(whole.at[other], recv_full.at[1])
        to_plain(whole, plain_a)

    @pl.when(y > 0)
    def _():
        arrived(before.at[other], recv_full.at[0])
        to_plain(before, plain_b)

    def x_copy(j):
        return remote(x_out, x_in, send_x.at[j], recv_x, (tm + 2, j))

    @pl.when(column == 0)
    def _():
        x_in[...] = prior_ref[...]

    @pl.when(column > 0)
    def _():
        arrived(x_in, recv_x)

    @pl.when(jnp.logical_and(y == 3, column < last))
    def _():
        moved = matvec(block_of_plain(plain_a), rows_of(x_in))
        put_rows(x_out, [m + o for m, o in zip(moved, rows_of(partial_q))])
        for j in (3, 2, 1, 0):
            x_copy(j).start()

    @pl.when(y == 0)
    def _():
        x_work[...] = x_in[...]

    @pl.when(y > 0)
    def _():
        moved = matvec(block_of_plain(plain_b), rows_of(x_in))
        put_rows(x_work, [m + o for m, o in zip(moved, rows_of(before_q))])

    @pl.when(core == 1)
    def _():
        moved = matvec(block_of_plain(plain_c), rows_of(x_work))
        put_rows(x_work, [m + o for m, o in zip(moved, rows_of(maps_q.at[0]))])

    def sweep(s, carry):
        moved = matvec(block_of_plain(e_buf.at[s]), list(carry))
        rows = [m + o for m, o in zip(moved, rows_of(off_buf.at[s]))]
        for g in range(4):
            sweep_buf[g, pl.ds(s, 1), :] = rows[g]
        return tuple(rows)

    lax.fori_loop(0, STEPS, sweep, tuple(rows_of(x_work)))

    owner = first_tm + y // 2
    out_block = 2 * lax.rem(y, 2) + core
    here = pl.ds(8 * out_block, STEPS)

    def own_rows(g):
        return jnp.logical_and(owner == tm, g == y)

    for g in range(4):
        src, dst = sweep_buf.at[g], out_ref.at[here]

        @pl.when(jnp.logical_not(own_rows(g)))
        def _():
            remote(src, dst, send_out.at[g], recv_out.at[out_block], (owner, g)).start()

        @pl.when(own_rows(g))
        def _():
            pltpu.make_async_copy(src, dst, recv_out.at[out_block]).start()

    for b in range(4):
        arrived(out_ref.at[pl.ds(8 * b, STEPS)], recv_out.at[b])

    for g in range(4):
        @pl.when(jnp.logical_not(own_rows(g)))
        def _():
            remote(sweep_buf.at[g], out_ref.at[here], send_out.at[g], recv_out.at[out_block], (owner, g)).wait_send()

    for b in range(4):
        @pl.when(jnp.logical_not(is_me(b)))
        def _():
            for src, dst, kind in small_pairs(b):
                remote(src, dst, send_small.at[b, kind], recv_small.at[y, kind], target_of(b)).wait_send()

    def finish_chunk(q, carry):
        for b in range(4):
            @pl.when(jnp.logical_not(is_me(b)))
            def _():
                for src, dst, kind in big_pairs(b, q):
                    remote(src, dst, send_in.at[b, kind, q], recv_in.at[y, kind, q], target_of(b)).wait_send()
        return carry

    lax.fori_loop(0, NCHUNK, finish_chunk, 0)

    @pl.when(holds)
    def _():
        for src, dst, kind in obs_arrays:
            remote(src.at[other_at], dst, send_obs.at[kind], recv_obs.at[kind], sibling).wait_send()

    map_copy.wait_send()
    q_copy.wait_send()
    for d in (1, 2, 3):
        @pl.when(y + d <= 3)
        def _():
            for copy in y_copies(d):
                copy.wait_send()
    for l in (2, 1):
        @pl.when(l < y)
        def _():
            left_copy(l).wait_send()

    @pl.when(y > 0)
    def _():
        remote(before.at[core], before.at[core], send_full.at[0], recv_full.at[0], sibling).wait_send()

    @pl.when(y == 3)
    def _():
        own_copy.wait_send()
        remote(whole.at[core], whole.at[core], send_full.at[1], recv_full.at[1], sibling).wait_send()

    @pl.when(jnp.logical_and(y == 3, column < last))
    def _():
        for j in range(4):
            x_copy(j).wait_send()


def body(dyn_cols, dyn_vals, obs_blocks, obs_op, obs_counts, obs_values, gain, sources, prior):
    count = dyn_vals.shape[0]
    columns_count = lax.axis_size("tm") // 2
    meta = jnp.concatenate(
        [dyn_cols.reshape(count, 6), obs_blocks, obs_counts[:, None], jnp.zeros((count, 119), jnp.int32)], axis=1
    )
    prior_rows = jnp.concatenate([prior.reshape(4, 128), jnp.zeros((4, 128), F32)], axis=0)
    vmem = pl.BlockSpec(memory_space=pltpu.VMEM)
    hbm = pl.BlockSpec(memory_space=pl.ANY)
    dma = pltpu.SemaphoreType.DMA
    a_map = (2, 2, NS, HALF)

    def call(*refs):
        kernel(columns_count, *refs)

    return pl.pallas_call(
        call,
        out_shape=jax.ShapeDtypeStruct((count, 128), F32),
        in_specs=[vmem, hbm, vmem, vmem, vmem, vmem, vmem],
        out_specs=vmem,
        scratch_shapes=[
            pltpu.VMEM((count, 64, 128), BF16),
            pltpu.VMEM((4, STEPS, 2, 64, 128), BF16),
            pltpu.VMEM((4, STEPS, 64, 128), BF16),
            pltpu.VMEM((4, STEPS, 128, 128), BF16),
            pltpu.VMEM((4, STEPS, 128), F32),
            pltpu.VMEM((4, STEPS, 128), jnp.int32),
            pltpu.SMEM((4, STEPS, 128), jnp.int32),
            pltpu.VMEM((STEPS, 64, 128), BF16),
            pltpu.VMEM((STEPS, 128), F32),
            pltpu.VMEM((8, 64, NS), F32),
            pltpu.VMEM((8, 64, NS), BF16),
            pltpu.VMEM((STEPS, NS, NS), BF16),
            pltpu.VMEM((STEPS, 8, 128), F32),
            pltpu.VMEM((2, *a_map), BF16),
            pltpu.VMEM((2, 8, 128), F32),
            pltpu.VMEM((4, *a_map), BF16),
            pltpu.VMEM((4, 8, 128), F32),
            pltpu.VMEM((2, NS, HALF), BF16),
            pltpu.VMEM((8, 128), F32),
            pltpu.VMEM(a_map, BF16),
            pltpu.VMEM((8, 128), F32),
            pltpu.VMEM(a_map, BF16),
            pltpu.VMEM((NS, NS), F32),
            pltpu.VMEM((NS, NS), F32),
            pltpu.VMEM((NS, NS), F32),
            pltpu.VMEM((8, 128), F32),
            pltpu.VMEM((8, 128), F32),
            pltpu.VMEM((8, 128), F32),
            pltpu.VMEM((4, STEPS, 128), F32),
            dma((4, 3, NCHUNK)), dma((4, 3, NCHUNK)),
            dma((4, 2)), dma((4, 2)),
            dma((2,)), dma((2,)), dma,
            dma((2,)), dma((2,)),
            dma, dma,
            dma((4,)), dma((4,)), dma((4,)), dma((4,)),
            dma((4,)), dma((4,)),
            dma((4,)), dma,
            dma((4,)), dma((4,)),
            dma((2,)), dma((2,)),
        ],
        compiler_params=pltpu.CompilerParams(
            collective_id=0, has_side_effects=True, vmem_limit_bytes=58 * 1024 * 1024
        ),
        cost_estimate=pl.CostEstimate(flops=10_000_000_000, bytes_accessed=4_000_000, transcendentals=0),
    )(dyn_vals, gain, obs_op, meta, obs_values, sources, prior_rows)


def solution(mesh):
    return jax.shard_map(
        body,
        mesh=mesh,
        in_specs=(
            P("tm", "state", None),
            P("tm", "state", None, None),
            P("tm", None),
            P("tm", None, None),
            P("tm"),
            P("tm", None),
            P("tm", "state", None),
            P("tm", "state"),
            P(),
        ),
        out_specs=P("tm", "state"),
        check_vma=False,
    )
```

```python
import jax
import jax.numpy as jnp
from jax import lax
from jax.experimental import pallas as pl
from jax.experimental.pallas import tpu as pltpu
from jax.sharding import PartitionSpec as P

MESH = pl.DeviceIdType.MESH
F32 = jnp.float32
BF16 = jnp.bfloat16
NS = 512
HALF = 256
STEPS = 8
CHUNK = 2
NCHUNK = STEPS // CHUNK


def split(value):
    high = value.astype(BF16)
    low = (value - high.astype(F32)).astype(BF16)
    return high, low


def column_to_row(column):
    rows = lax.broadcasted_iota(jnp.int32, (128, 128), 0)
    lanes = lax.broadcasted_iota(jnp.int32, (128, 128), 1)
    return jnp.sum(jnp.where(rows == lanes, column, 0.0), axis=0, keepdims=True)


def matvec(load, vector):
    out = []
    for g in range(4):
        total = load(g, 0) * vector[0]
        for j in range(1, 4):
            total = total + load(g, j) * vector[j]
        out.append(column_to_row(jnp.sum(total, axis=1, keepdims=True)))
    return out


def rows_of(ref):
    return [ref[g : g + 1, :] for g in range(4)]


def put_rows(ref, rows):
    for g in range(4):
        ref[g : g + 1, :] = rows[g]


def block_of_map(ref):
    def load(g, j):
        rows, lanes = pl.ds(g * 128, 128), pl.ds((j % 2) * 128, 128)
        return ref[j // 2, 0, rows, lanes].astype(F32) + ref[j // 2, 1, rows, lanes].astype(F32)

    return load


def block_of_plain(ref):
    def load(g, j):
        return ref[pl.ds(g * 128, 128), pl.ds(j * 128, 128)].astype(F32)

    return load


def product(left, right):
    total = None
    for h in range(2):
        rows = pl.ds(h * HALF, HALF)
        for a, b in ((0, 0), (0, 1), (1, 0)):
            term = jnp.dot(left[h, a], right[b, rows, :], preferred_element_type=F32)
            total = term if total is None else total + term
    return total


def to_plain(ref, out):
    for h in range(2):
        out[:, h * HALF : (h + 1) * HALF] = ref[h, 0].astype(F32) + ref[h, 1].astype(F32)


def kernel(
    columns_count,
    vals_ref, gain_ref, obs_op_ref, cols_ref, blocks_ref, counts_ref, obs_values_ref, sources_ref, prior_ref,
    out_ref,
    third, packed, a_buf, b_buf, gain_buf, src_buf, cols_buf, blocks_buf, counts_buf,
    cols_smem, blocks_smem, counts_smem, op_buf, ov_buf,
    f_buf, fn_buf, e_buf, off_buf,
    maps, maps_q, chip, chip_q, partial, partial_q, before, before_q, whole,
    mate, mate_q, plain_a, plain_b, plain_c, plain_d, x_in, x_pair, x_mid, x_out, x_work, sweep_buf,
    send_in, recv_in, send_small, recv_small, send_obs, recv_obs, smem_sem,
    send_map, recv_map, send_chip, recv_chip, send_y, recv_y, send_yq, recv_yq,
    send_left, recv_left, send_x, recv_x, send_out, recv_out, send_full, recv_full,
    third_sem, send_mate, recv_mate, recv_pair,
):
    tm, y = lax.axis_index("tm"), lax.axis_index("state")
    core = lax.rem(tm, 2)
    column = tm // 2
    first_tm = tm - core
    other = 1 - core
    sibling = (first_tm + other, y)
    pair, second = column // 2, lax.rem(column, 2)
    even_pair = lax.rem(pair, 2) == 0
    last_pair = columns_count // 2 - 1

    def master_column(p):
        return 2 * p + 1 - lax.rem(p, 2)

    def device(c, j):
        return 2 * c + core, j

    in_master = column == master_column(pair)
    is_master = jnp.logical_and(in_master, y == 3)
    is_mate = jnp.logical_and(jnp.logical_not(in_master), y == 3)
    partner = device(column + 1 - 2 * second, 3)

    barrier = pltpu.get_barrier_semaphore()

    def greet(where):
        pl.semaphore_signal(barrier, inc=1, device_id=where, device_id_type=MESH)

    for c in range(2):
        for j in range(4):
            @pl.when(jnp.logical_or(c != core, j != y))
            def _():
                greet((first_tm + c, j))

    third_copy = pltpu.make_async_copy(vals_ref.at[:, :, :, pl.ds(128, 64)], third, third_sem)
    third_copy.start()

    from_earlier = jnp.logical_and(second == 0, pair > 0)
    from_own = jnp.logical_and(second == 1, jnp.logical_not(even_pair))
    earlier_master = device(master_column(pair - 1), 3)

    @pl.when(from_earlier)
    def _():
        greet(earlier_master)

    @pl.when(from_own)
    def _():
        greet(device(column - 1, 3))

    takes_pair = jnp.logical_and(is_master, jnp.logical_and(even_pair, pair > 0))

    @pl.when(takes_pair)
    def _():
        greet(earlier_master)

    @pl.when(is_master)
    def _():
        greet(partner)

    sends_on = jnp.logical_and(is_master, pair < last_pair)
    odd_master = jnp.logical_and(is_master, jnp.logical_not(even_pair))
    peers = (
        7
        + jnp.where(is_mate, 1, 0)
        + jnp.where(odd_master, 4, 0)
        + jnp.where(sends_on, 4, 0)
        + jnp.where(jnp.logical_and(sends_on, odd_master), 1, 0)
    )
    pl.semaphore_wait(barrier, peers)

    def target_of(b):
        return first_tm + b % 2, 2 * core + b // 2

    def is_me(b):
        dest_tm, dest_y = target_of(b)
        return jnp.logical_and(dest_tm == tm, dest_y == y)

    def remote(src, dst, send, recv, device):
        return pltpu.make_async_remote_copy(
            src_ref=src, dst_ref=dst, send_sem=send, recv_sem=recv, device_id=device, device_id_type=MESH
        )

    def small_pairs(b):
        start = pl.ds(8 * b, STEPS)
        return (
            (sources_ref.at[start], src_buf.at[y], 0),
            (cols_ref, cols_buf.at[y], 1),
        )

    def big_pairs(b, q):
        start, there = pl.ds(8 * b + CHUNK * q, CHUNK), pl.ds(CHUNK * q, CHUNK)
        return (
            (vals_ref.at[start, :, :, pl.ds(0, 128)], a_buf.at[y, there], 0),
            (gain_ref.at[start], gain_buf.at[y, there], 2),
            (packed.at[start], b_buf.at[y, there], 1),
        )

    def send_pair(b, src, dst, send, recv):
        @pl.when(jnp.logical_not(is_me(b)))
        def _():
            remote(src, dst, send, recv, target_of(b)).start()

        @pl.when(is_me(b))
        def _():
            pltpu.make_async_copy(src, dst, recv).start()

    for b in range(4):
        for src, dst, kind in small_pairs(b):
            send_pair(b, src, dst, send_small.at[b, kind], recv_small.at[y, kind])

    holds = core == y // 2
    first_step = 16 * lax.rem(y, 2) + 8 * core
    mine_at = pl.ds(first_step, STEPS)
    other_at = pl.ds(16 * lax.rem(y, 2) + 8 * other, STEPS)
    obs_arrays = (
        (obs_op_ref.at[mine_at], obs_op_ref.at[other_at], op_buf, 0),
        (obs_values_ref.at[mine_at], obs_values_ref.at[other_at], ov_buf, 1),
        (blocks_ref, blocks_ref, blocks_buf, 2),
        (counts_ref, counts_ref, counts_buf, 3),
    )

    @pl.when(holds)
    def _():
        for mine, others, dst, kind in obs_arrays:
            remote(others, dst, send_obs.at[kind], recv_obs.at[kind], sibling).start()
            pltpu.make_async_copy(mine, dst, recv_obs.at[kind]).start()

    def start_chunk(q, carry):
        for b in range(4):
            for src, dst, kind in big_pairs(b, q)[:2]:
                send_pair(b, src, dst, send_in.at[b, kind, q], recv_in.at[y, kind, q])

        @pl.when(q == 0)
        def _():
            third_copy.wait()

        for b in range(4):
            for t in range(CHUNK):
                at = 8 * b + CHUNK * q + t
                packed[at] = jnp.concatenate([third[at, 0], third[at, 1]], axis=1)
        for b in range(4):
            src, dst, kind = big_pairs(b, q)[2]
            send_pair(b, src, dst, send_in.at[b, kind, q], recv_in.at[y, kind, q])
        return carry

    lax.fori_loop(0, NCHUNK, start_chunk, 0)

    def arrived(dst, sem):
        pltpu.make_async_copy(dst, dst, sem).wait()

    for j in range(4):
        arrived(src_buf.at[j], recv_small.at[j, 0])
        arrived(cols_buf.at[j], recv_small.at[j, 1])
    for _, _, dst, kind in obs_arrays:
        arrived(dst, recv_obs.at[kind])
    to_smem = [
        pltpu.make_async_copy(src, dst, smem_sem.at[k])
        for k, (src, dst) in enumerate(((cols_buf, cols_smem), (blocks_buf, blocks_smem), (counts_buf, counts_smem)))
    ]
    for copy in to_smem:
        copy.start()
    for copy in to_smem:
        copy.wait()

    lane64 = lax.broadcasted_iota(jnp.int32, (64, 128), 1)
    row64 = lax.broadcasted_iota(jnp.int32, (64, 128), 0)
    left64 = lane64 < 64
    half64 = lane64 // 64
    lane1 = lax.broadcasted_iota(jnp.int32, (1, 128), 1)

    maps_q[core] = jnp.zeros((4, 128), F32)

    def step(s, carry):
        at = first_step + s

        @pl.when(lax.rem(s, CHUNK) == 0)
        def _():
            q = s // CHUNK
            there = pl.ds(CHUNK * q, CHUNK)
            for j in range(4):
                arrived(a_buf.at[j, there], recv_in.at[j, 0, q])
                arrived(b_buf.at[j, there], recv_in.at[j, 1, q])
                arrived(gain_buf.at[j, there], recv_in.at[j, 2, q])

        for j in range(4):
            thirds = b_buf[j, s].astype(F32)
            thirds_turned = pltpu.roll(thirds, 64, 1)
            for il in range(2):
                i = 2 * j + il
                pair = a_buf[j, s, il].astype(F32)
                turned = pltpu.roll(pair, 64, 1)
                block0 = jnp.where(left64, pair, turned)
                block1 = jnp.where(left64, turned, pair)
                block2 = jnp.where(left64 if il == 0 else jnp.logical_not(left64), thirds, thirds_turned)
                col1 = cols_smem[j, 1, il, at]
                col2 = cols_smem[j, 2, il, at]
                for p in range(4):
                    index = half64 + 2 * p
                    value = jnp.where(index == col1, block1, jnp.where(index == col2, block2, 0.0))
                    if p == j:
                        value = jnp.where(half64 == il, block0, value)
                    f_buf[i, :, p * 128 : (p + 1) * 128] = value
                    fn_buf[i, :, p * 128 : (p + 1) * 128] = value.astype(BF16)

        operator = op_buf[s].astype(F32)
        turned_operator = operator.T.astype(BF16)
        count = counts_smem[0, at]
        images, source_columns = [], []
        for o in range(2):
            block = blocks_smem[o, at]
            selected = fn_buf[block]
            images.append(jnp.dot(turned_operator[64 * o : 64 * o + 64], selected, preferred_element_type=F32))
            source_row = src_buf[block // 2, pl.ds(s, 1), :]
            offset = lax.rem(block, 2) * 64
            source_columns.append(
                jnp.sum(jnp.where(lane64 == row64 + offset, source_row, 0.0), axis=1, keepdims=True)
            )
        image = jnp.concatenate(images, axis=0)
        slot = lax.broadcasted_iota(jnp.int32, (128, NS), 0)
        masked = jnp.where(slot < count, image, 0.0).astype(BF16)
        gains = gain_buf[:, s].reshape(NS, 128)
        correction = jnp.dot(gains, masked, preferred_element_type=F32)
        e_buf[s] = (f_buf[...].reshape(NS, NS) - correction).astype(BF16)

        source_image = jnp.sum(
            operator * jnp.where(left64, source_columns[0], source_columns[1]), axis=0, keepdims=True
        )
        source_image = source_image.astype(BF16).astype(F32)
        innovation = jnp.where(lane1 < count, ov_buf[pl.ds(s, 1), :] - source_image, 0.0)
        offsets = []
        for g in range(4):
            moved = jnp.sum(gain_buf[g, s].astype(F32) * innovation, axis=1, keepdims=True)
            offsets.append(column_to_row(moved) + src_buf[g, pl.ds(s, 1), :])
        put_rows(off_buf.at[s], offsets)

        moved = matvec(block_of_plain(e_buf.at[s]), rows_of(maps_q.at[core]))
        put_rows(maps_q.at[core], [m + o for m, o in zip(moved, offsets)])

        @pl.when(s == 0)
        def _():
            for h in range(2):
                maps[core, h, 0] = e_buf[s, :, h * HALF : (h + 1) * HALF]
                maps[core, h, 1] = jnp.zeros((NS, HALF), BF16)

        @pl.when(s > 0)
        def _():
            for h in range(2):
                matrix = e_buf[s]
                value = jnp.dot(matrix, maps[core, h, 0], preferred_element_type=F32)
                value = value + jnp.dot(matrix, maps[core, h, 1], preferred_element_type=F32)
                maps[core, h, 0], maps[core, h, 1] = split(value)

        return carry

    lax.fori_loop(0, STEPS, step, 0)

    map_copy = remote(maps.at[core], maps.at[core], send_map.at[0], recv_map.at[0], sibling)
    q_copy = remote(maps_q.at[core], maps_q.at[core], send_map.at[1], recv_map.at[1], sibling)
    map_copy.start()
    q_copy.start()
    arrived(maps_q.at[other], recv_map.at[1])
    arrived(maps.at[other], recv_map.at[0])
    chip[y, core, 0], chip[y, core, 1] = split(product(maps.at[1], maps.at[0, core]))
    moved = matvec(block_of_map(maps.at[1]), rows_of(maps_q.at[0]))
    put_rows(chip_q.at[y], [m + o for m, o in zip(moved, rows_of(maps_q.at[1]))])

    def y_copies(d):
        there = (tm, lax.rem(y + d, 4))
        return (
            remote(chip.at[y, core], chip.at[y, core], send_y.at[d], recv_y.at[y], there),
            remote(chip_q.at[y], chip_q.at[y], send_yq.at[d], recv_yq.at[y], there),
        )

    for d in (1, 2, 3):
        @pl.when(y + d <= 3)
        def _():
            for copy in y_copies(d):
                copy.start()

    own_copy = remote(chip.at[y, core], chip.at[y, core], send_chip, recv_chip, sibling)

    @pl.when(y == 3)
    def _():
        own_copy.start()

    to_plain(maps.at[0], plain_c)

    def left_copy(l):
        return remote(chip.at[l, core], chip.at[l, core], send_left.at[l], recv_left.at[l], sibling)

    for l in range(3):
        @pl.when(l < y)
        def _():
            arrived(chip_q.at[l], recv_yq.at[l])
    for l in (2, 1):
        @pl.when(l < y)
        def _():
            arrived(chip.at[l, core], recv_y.at[l])
            left_copy(l).start()

    @pl.when(y > 0)
    def _():
        arrived(chip.at[0, core], recv_y.at[0])
        partial[...] = chip[0, core]
        partial_q[...] = chip_q[0]

    def extend(l):
        high, low = split(product(chip.at[l], partial))
        partial[0], partial[1] = high, low
        moved = matvec(block_of_map(chip.at[l]), rows_of(partial_q))
        put_rows(partial_q, [m + o for m, o in zip(moved, rows_of(chip_q.at[l]))])

    for l in (1, 2):
        @pl.when(l < y)
        def _():
            arrived(chip.at[l, other], recv_left.at[l])
            extend(l)

    @pl.when(y > 0)
    def _():
        before[core] = partial[...]
        before_q[...] = partial_q[...]
        remote(before.at[core], before.at[core], send_full.at[0], recv_full.at[0], sibling).start()

    mate_copy = remote(partial, mate.at[core], send_mate.at[0], recv_mate.at[0], partner)
    mate_q_copy = remote(partial_q, mate_q, send_mate.at[1], recv_mate.at[1], partner)
    mate_on = remote(mate.at[core], mate.at[core], send_mate.at[2], recv_mate.at[2], sibling)

    @pl.when(y == 3)
    def _():
        arrived(chip.at[y, other], recv_chip)
        extend(3)

    @pl.when(is_mate)
    def _():
        mate_copy.start()
        mate_q_copy.start()

    @pl.when(is_master)
    def _():
        whole[core] = partial[...]
        copy = remote(whole.at[core], whole.at[core], send_full.at[1], recv_full.at[1], sibling)
        copy.start()
        arrived(mate.at[core], recv_mate.at[0])
        mate_on.start()
        arrived(whole.at[other], recv_full.at[1])
        to_plain(whole, plain_a)
        arrived(mate_q, recv_mate.at[1])
        arrived(mate.at[other], recv_mate.at[2])
        to_plain(mate, plain_d)

    @pl.when(y > 0)
    def _():
        arrived(before.at[other], recv_full.at[0])
        to_plain(before, plain_b)

    def next_pair_copy():
        return remote(x_out, x_pair, send_x.at[8], recv_pair, device(master_column(pair + 1), 3))

    def next_copy(j):
        return remote(x_out, x_in, send_x.at[j], recv_x, device(2 * pair + 2, j))

    def second_copy(j):
        return remote(x_mid, x_in, send_x.at[4 + j], recv_x, device(2 * pair + 1, j))

    def apply(plain, vector, shift, out):
        moved = matvec(block_of_plain(plain), rows_of(vector))
        put_rows(out, [m + o for m, o in zip(moved, rows_of(shift))])

    @pl.when(jnp.logical_and(pair == 0, second == 0))
    def _():
        x_in[...] = prior_ref[...]

    @pl.when(jnp.logical_or(from_earlier, from_own))
    def _():
        arrived(x_in, recv_x)

    @pl.when(is_master)
    def _():
        @pl.when(even_pair)
        def _():
            @pl.when(pair == 0)
            def _():
                x_pair[...] = prior_ref[...]

            @pl.when(pair > 0)
            def _():
                arrived(x_pair, recv_pair)

            apply(plain_d, x_pair, mate_q, x_mid)
            apply(plain_a, x_mid, partial_q, x_out)

            @pl.when(sends_on)
            def _():
                for j in (3, 2, 1, 0):
                    next_copy(j).start()

            for j in range(3):
                second_copy(j).start()
            x_in[...] = x_mid[...]

        @pl.when(jnp.logical_not(even_pair))
        def _():
            apply(plain_a, x_in, partial_q, x_mid)
            apply(plain_d, x_mid, mate_q, x_out)

            @pl.when(sends_on)
            def _():
                next_pair_copy().start()
                for j in range(4):
                    next_copy(j).start()

            for j in range(4):
                second_copy(j).start()

    @pl.when(jnp.logical_and(jnp.logical_and(even_pair, second == 1), y < 3))
    def _():
        arrived(x_in, recv_x)

    @pl.when(y == 0)
    def _():
        x_work[...] = x_in[...]

    @pl.when(y > 0)
    def _():
        moved = matvec(block_of_plain(plain_b), rows_of(x_in))
        put_rows(x_work, [m + o for m, o in zip(moved, rows_of(before_q))])

    @pl.when(core == 1)
    def _():
        moved = matvec(block_of_plain(plain_c), rows_of(x_work))
        put_rows(x_work, [m + o for m, o in zip(moved, rows_of(maps_q.at[0]))])

    def sweep(s, carry):
        moved = matvec(block_of_plain(e_buf.at[s]), list(carry))
        rows = [m + o for m, o in zip(moved, rows_of(off_buf.at[s]))]
        for g in range(4):
            sweep_buf[g, pl.ds(s, 1), :] = rows[g]
        return tuple(rows)

    lax.fori_loop(0, STEPS, sweep, tuple(rows_of(x_work)))

    owner = first_tm + y // 2
    out_block = 2 * lax.rem(y, 2) + core
    here = pl.ds(8 * out_block, STEPS)

    def own_rows(g):
        return jnp.logical_and(owner == tm, g == y)

    for g in range(4):
        src, dst = sweep_buf.at[g], out_ref.at[here]

        @pl.when(jnp.logical_not(own_rows(g)))
        def _():
            remote(src, dst, send_out.at[g], recv_out.at[out_block], (owner, g)).start()

        @pl.when(own_rows(g))
        def _():
            pltpu.make_async_copy(src, dst, recv_out.at[out_block]).start()

    for b in range(4):
        arrived(out_ref.at[pl.ds(8 * b, STEPS)], recv_out.at[b])

    for g in range(4):
        @pl.when(jnp.logical_not(own_rows(g)))
        def _():
            remote(sweep_buf.at[g], out_ref.at[here], send_out.at[g], recv_out.at[out_block], (owner, g)).wait_send()

    for b in range(4):
        @pl.when(jnp.logical_not(is_me(b)))
        def _():
            for src, dst, kind in small_pairs(b):
                remote(src, dst, send_small.at[b, kind], recv_small.at[y, kind], target_of(b)).wait_send()

    def finish_chunk(q, carry):
        for b in range(4):
            @pl.when(jnp.logical_not(is_me(b)))
            def _():
                for src, dst, kind in big_pairs(b, q):
                    remote(src, dst, send_in.at[b, kind, q], recv_in.at[y, kind, q], target_of(b)).wait_send()
        return carry

    lax.fori_loop(0, NCHUNK, finish_chunk, 0)

    @pl.when(holds)
    def _():
        for mine, others, dst, kind in obs_arrays:
            remote(others, dst, send_obs.at[kind], recv_obs.at[kind], sibling).wait_send()

    map_copy.wait_send()
    q_copy.wait_send()
    for d in (1, 2, 3):
        @pl.when(y + d <= 3)
        def _():
            for copy in y_copies(d):
                copy.wait_send()
    for l in (2, 1):
        @pl.when(l < y)
        def _():
            left_copy(l).wait_send()

    @pl.when(y > 0)
    def _():
        remote(before.at[core], before.at[core], send_full.at[0], recv_full.at[0], sibling).wait_send()

    @pl.when(y == 3)
    def _():
        own_copy.wait_send()

    @pl.when(is_mate)
    def _():
        mate_copy.wait_send()
        mate_q_copy.wait_send()

    @pl.when(is_master)
    def _():
        remote(whole.at[core], whole.at[core], send_full.at[1], recv_full.at[1], sibling).wait_send()
        mate_on.wait_send()
        for j in range(3):
            second_copy(j).wait_send()

    @pl.when(odd_master)
    def _():
        second_copy(3).wait_send()

    @pl.when(sends_on)
    def _():
        for j in range(4):
            next_copy(j).wait_send()

    @pl.when(jnp.logical_and(sends_on, odd_master))
    def _():
        next_pair_copy().wait_send()


def body(dyn_cols, dyn_vals, obs_blocks, obs_op, obs_counts, obs_values, gain, sources, prior):
    count = dyn_vals.shape[0]
    columns_count = lax.axis_size("tm") // 2
    cols = jnp.transpose(dyn_cols, (2, 1, 0))
    blocks = jnp.transpose(obs_blocks, (1, 0))
    counts = obs_counts.reshape(1, count)
    prior_rows = prior.reshape(4, 128)
    vmem = pl.BlockSpec(memory_space=pltpu.VMEM)
    hbm = pl.BlockSpec(memory_space=pl.ANY)
    dma = pltpu.SemaphoreType.DMA
    a_map = (2, 2, NS, HALF)

    def call(*refs):
        kernel(columns_count, *refs)

    return pl.pallas_call(
        call,
        out_shape=jax.ShapeDtypeStruct((count, 128), F32),
        in_specs=[hbm, hbm, hbm, vmem, vmem, vmem, vmem, vmem, vmem],
        out_specs=vmem,
        scratch_shapes=[
            pltpu.VMEM((count, 2, 64, 64), BF16),
            pltpu.VMEM((count, 64, 128), BF16),
            pltpu.VMEM((4, STEPS, 2, 64, 128), BF16),
            pltpu.VMEM((4, STEPS, 64, 128), BF16),
            pltpu.VMEM((4, STEPS, 128, 128), BF16),
            pltpu.VMEM((4, STEPS, 128), F32),
            pltpu.VMEM((4, *cols.shape), jnp.int32),
            pltpu.VMEM(blocks.shape, jnp.int32),
            pltpu.VMEM(counts.shape, jnp.int32),
            pltpu.SMEM((4, *cols.shape), jnp.int32),
            pltpu.SMEM(blocks.shape, jnp.int32),
            pltpu.SMEM(counts.shape, jnp.int32),
            pltpu.VMEM((STEPS, 64, 128), BF16),
            pltpu.VMEM((STEPS, 128), F32),
            pltpu.VMEM((8, 64, NS), F32),
            pltpu.VMEM((8, 64, NS), BF16),
            pltpu.VMEM((STEPS, NS, NS), BF16),
            pltpu.VMEM((STEPS, 4, 128), F32),
            pltpu.VMEM((2, *a_map), BF16),
            pltpu.VMEM((2, 4, 128), F32),
            pltpu.VMEM((4, *a_map), BF16),
            pltpu.VMEM((4, 4, 128), F32),
            pltpu.VMEM((2, NS, HALF), BF16),
            pltpu.VMEM((4, 128), F32),
            pltpu.VMEM(a_map, BF16),
            pltpu.VMEM((4, 128), F32),
            pltpu.VMEM(a_map, BF16),
            pltpu.VMEM(a_map, BF16),
            pltpu.VMEM((4, 128), F32),
            pltpu.VMEM((NS, NS), F32),
            pltpu.VMEM((NS, NS), F32),
            pltpu.VMEM((NS, NS), F32),
            pltpu.VMEM((NS, NS), F32),
            pltpu.VMEM((4, 128), F32),
            pltpu.VMEM((4, 128), F32),
            pltpu.VMEM((4, 128), F32),
            pltpu.VMEM((4, 128), F32),
            pltpu.VMEM((4, 128), F32),
            pltpu.VMEM((4, STEPS, 128), F32),
            dma((4, 3, NCHUNK)), dma((4, 3, NCHUNK)),
            dma((4, 2)), dma((4, 2)),
            dma((4,)), dma((4,)), dma((3,)),
            dma((2,)), dma((2,)),
            dma, dma,
            dma((4,)), dma((4,)), dma((4,)), dma((4,)),
            dma((4,)), dma((4,)),
            dma((9,)), dma,
            dma((4,)), dma((4,)),
            dma((2,)), dma((2,)),
            dma, dma((3,)), dma((3,)), dma,
        ],
        compiler_params=pltpu.CompilerParams(
            collective_id=0, has_side_effects=True, vmem_limit_bytes=58 * 1024 * 1024
        ),
        cost_estimate=pl.CostEstimate(flops=10_000_000_000, bytes_accessed=4_000_000, transcendentals=0),
    )(dyn_vals, gain, obs_op, cols, blocks, counts, obs_values, sources, prior_rows)


def solution(mesh):
    return jax.shard_map(
        body,
        mesh=mesh,
        in_specs=(
            P("tm", "state", None),
            P("tm", "state", None, None),
            P("tm", None),
            P("tm", None, None),
            P("tm"),
            P("tm", None),
            P("tm", "state", None),
            P("tm", "state"),
            P(),
        ),
        out_specs=P("tm", "state"),
        check_vma=False,
    )
```

```python
import jax
import jax.numpy as jnp
from jax import lax
from jax.experimental import pallas as pl
from jax.experimental.pallas import tpu as pltpu
from jax.sharding import PartitionSpec as P

MESH = pl.DeviceIdType.MESH
F32 = jnp.float32
BF16 = jnp.bfloat16
NS = 512
HALF = 256
STEPS = 8
CHUNK = 2
NCHUNK = STEPS // CHUNK


def split(value):
    high = value.astype(BF16)
    low = (value - high.astype(F32)).astype(BF16)
    return high, low


def column_to_row(column):
    rows = lax.broadcasted_iota(jnp.int32, (128, 128), 0)
    lanes = lax.broadcasted_iota(jnp.int32, (128, 128), 1)
    return jnp.sum(jnp.where(rows == lanes, column, 0.0), axis=0, keepdims=True)


def matvec(load, vector):
    out = []
    for g in range(4):
        total = load(g, 0) * vector[0]
        for j in range(1, 4):
            total = total + load(g, j) * vector[j]
        out.append(column_to_row(jnp.sum(total, axis=1, keepdims=True)))
    return out


def rows_of(ref):
    return [ref[g : g + 1, :] for g in range(4)]


def put_rows(ref, rows):
    for g in range(4):
        ref[g : g + 1, :] = rows[g]


def block_of_plain(ref):
    def load(g, j):
        return ref[pl.ds(g * 128, 128), pl.ds(j * 128, 128)].astype(F32)

    return load


def product(left, right):
    total = None
    for h in range(2):
        rows = pl.ds(h * HALF, HALF)
        for a, b in ((0, 0), (0, 1), (1, 0)):
            term = jnp.dot(left[h, a], right[b, rows, :], preferred_element_type=F32)
            total = term if total is None else total + term
    return total


def half_map(maps_ref, out):
    for h in range(2):
        out[:, h * HALF : (h + 1) * HALF] = maps_ref[h, 0].astype(F32) + maps_ref[h, 1].astype(F32)


def left_lanes(shape):
    return lax.broadcasted_iota(jnp.int32, shape, 1) < 64


def pack_chunk(doubled):
    low = doubled - doubled.astype(BF16).astype(F32)
    return jnp.where(left_lanes(doubled.shape), doubled, low).astype(BF16)


def pack_pair(pair):
    turned = pltpu.roll(pair, 64, 1)
    left = left_lanes(pair.shape)
    return pack_chunk(jnp.where(left, pair, turned)), pack_chunk(jnp.where(left, turned, pair))


def chunk_product(left, right):
    rows = right.reshape(8, 64, 128)
    rows = jnp.concatenate([rows, rows], axis=1).reshape(2 * NS, 128)
    lanes = jnp.concatenate([left[n] for n in range(8)], axis=1)
    parts = jnp.dot(lanes, rows, preferred_element_type=F32)
    return pack_chunk(parts + pltpu.roll(parts, 64, 1))


def to_plain(packed, out):
    for n in range(4):
        first, second = packed[2 * n].astype(F32), packed[2 * n + 1].astype(F32)
        first, second = first + pltpu.roll(first, 64, 1), second + pltpu.roll(second, 64, 1)
        out[:, n * 128 : (n + 1) * 128] = jnp.where(left_lanes(first.shape), first, second)


def packed_matvec(packed, vector):
    doubled = []
    for row in vector:
        doubled.append(jnp.concatenate([row[:, :64], row[:, :64]], axis=1))
        doubled.append(jnp.concatenate([row[:, 64:], row[:, 64:]], axis=1))
    out = []
    for g in range(4):
        total = None
        for n in range(8):
            term = packed[n, pl.ds(g * 128, 128), :].astype(F32) * doubled[n]
            total = term if total is None else total + term
        out.append(column_to_row(jnp.sum(total, axis=1, keepdims=True)))
    return out


def sum_rows(a, b):
    return [m + o for m, o in zip(a, b)]


def kernel(
    columns_count,
    vals_ref, gain_ref, obs_op_ref, cols_ref, blocks_ref, counts_ref, obs_values_ref, sources_ref, prior_ref,
    out_ref,
    third, packed, a_buf, b_buf, gain_buf, src_buf, cols_buf, blocks_buf, counts_buf,
    cols_smem, blocks_smem, counts_smem, op_buf, ov_buf,
    f_buf, fn_buf, e_buf, off_buf,
    maps, maps_q, chip, chip_q, before, before_q, left, left_q, first, first_q, last, whole, whole_q,
    mate, mate_q, plain_a, plain_b, plain_c, plain_d, x_in, x_pair, x_mid, x_out, x_work, sweep_buf,
    send_in, recv_in, send_small, recv_small, send_obs, recv_obs, smem_sem,
    send_map, recv_map, send_before, recv_before, send_left, recv_left, send_first, recv_first,
    send_mate, recv_mate, send_vec, recv_vec, send_share, recv_share, send_on, recv_on,
    send_x, recv_x, recv_pair, send_out, recv_out, third_sem,
):
    tm, y = lax.axis_index("tm"), lax.axis_index("state")
    core = lax.rem(tm, 2)
    column = tm // 2
    first_tm = tm - core
    other = 1 - core
    sibling = (first_tm + other, y)
    pair, second = column // 2, lax.rem(column, 2)
    even_pair = lax.rem(pair, 2) == 0
    last_pair = columns_count // 2 - 1

    def master_column(p):
        return 2 * p + 1 - lax.rem(p, 2)

    def device(c, j):
        return 2 * c + core, j

    in_master = column == master_column(pair)
    is_master = jnp.logical_and(in_master, y == 3)
    is_mate = jnp.logical_and(jnp.logical_not(in_master), y == 3)
    partner = device(column + 1 - 2 * second, 3)

    barrier = pltpu.get_barrier_semaphore()

    def greet(where):
        pl.semaphore_signal(barrier, inc=1, device_id=where, device_id_type=MESH)

    for c in range(2):
        for j in range(4):
            @pl.when(jnp.logical_or(c != core, j != y))
            def _():
                greet((first_tm + c, j))

    third_copy = pltpu.make_async_copy(vals_ref.at[:, :, :, pl.ds(128, 64)], third, third_sem)
    third_copy.start()

    from_earlier = jnp.logical_and(second == 0, pair > 0)
    from_own = jnp.logical_and(second == 1, jnp.logical_not(even_pair))
    earlier_master = device(master_column(pair - 1), 3)

    @pl.when(from_earlier)
    def _():
        greet(earlier_master)

    @pl.when(from_own)
    def _():
        greet(device(column - 1, 3))

    takes_pair = jnp.logical_and(is_master, jnp.logical_and(even_pair, pair > 0))

    @pl.when(takes_pair)
    def _():
        greet(earlier_master)

    @pl.when(is_master)
    def _():
        greet(partner)

    sends_on = jnp.logical_and(is_master, pair < last_pair)
    odd_master = jnp.logical_and(is_master, jnp.logical_not(even_pair))
    peers = (
        7
        + jnp.where(is_mate, 1, 0)
        + jnp.where(odd_master, 4, 0)
        + jnp.where(sends_on, 4, 0)
        + jnp.where(jnp.logical_and(sends_on, odd_master), 1, 0)
    )
    pl.semaphore_wait(barrier, peers)

    def target_of(b):
        return first_tm + b % 2, 2 * core + b // 2

    def is_me(b):
        dest_tm, dest_y = target_of(b)
        return jnp.logical_and(dest_tm == tm, dest_y == y)

    def remote(src, dst, send, recv, device):
        return pltpu.make_async_remote_copy(
            src_ref=src, dst_ref=dst, send_sem=send, recv_sem=recv, device_id=device, device_id_type=MESH
        )

    def small_pairs(b):
        start = pl.ds(8 * b, STEPS)
        return (
            (sources_ref.at[start], src_buf.at[y], 0),
            (cols_ref, cols_buf.at[y], 1),
        )

    def big_pairs(b, q):
        start, there = pl.ds(8 * b + CHUNK * q, CHUNK), pl.ds(CHUNK * q, CHUNK)
        return (
            (vals_ref.at[start, :, :, pl.ds(0, 128)], a_buf.at[y, there], 0),
            (gain_ref.at[start], gain_buf.at[y, there], 2),
            (packed.at[start], b_buf.at[y, there], 1),
        )

    def send_pair(b, src, dst, send, recv):
        @pl.when(jnp.logical_not(is_me(b)))
        def _():
            remote(src, dst, send, recv, target_of(b)).start()

        @pl.when(is_me(b))
        def _():
            pltpu.make_async_copy(src, dst, recv).start()

    for b in range(4):
        for src, dst, kind in small_pairs(b):
            send_pair(b, src, dst, send_small.at[b, kind], recv_small.at[y, kind])

    holds = core == y // 2
    first_step = 16 * lax.rem(y, 2) + 8 * core
    mine_at = pl.ds(first_step, STEPS)
    other_at = pl.ds(16 * lax.rem(y, 2) + 8 * other, STEPS)
    obs_arrays = (
        (obs_op_ref.at[mine_at], obs_op_ref.at[other_at], op_buf, 0),
        (obs_values_ref.at[mine_at], obs_values_ref.at[other_at], ov_buf, 1),
        (blocks_ref, blocks_ref, blocks_buf, 2),
        (counts_ref, counts_ref, counts_buf, 3),
    )

    @pl.when(holds)
    def _():
        for mine, others, dst, kind in obs_arrays:
            remote(others, dst, send_obs.at[kind], recv_obs.at[kind], sibling).start()
            pltpu.make_async_copy(mine, dst, recv_obs.at[kind]).start()

    def start_chunk(q, carry):
        for b in range(4):
            for src, dst, kind in big_pairs(b, q)[:2]:
                send_pair(b, src, dst, send_in.at[b, kind, q], recv_in.at[y, kind, q])

        @pl.when(q == 0)
        def _():
            third_copy.wait()

        for b in range(4):
            for t in range(CHUNK):
                at = 8 * b + CHUNK * q + t
                packed[at] = jnp.concatenate([third[at, 0], third[at, 1]], axis=1)
        for b in range(4):
            src, dst, kind = big_pairs(b, q)[2]
            send_pair(b, src, dst, send_in.at[b, kind, q], recv_in.at[y, kind, q])
        return carry

    lax.fori_loop(0, NCHUNK, start_chunk, 0)

    def arrived(dst, sem):
        pltpu.make_async_copy(dst, dst, sem).wait()

    for j in range(4):
        arrived(src_buf.at[j], recv_small.at[j, 0])
        arrived(cols_buf.at[j], recv_small.at[j, 1])
    for _, _, dst, kind in obs_arrays:
        arrived(dst, recv_obs.at[kind])
    to_smem = [
        pltpu.make_async_copy(src, dst, smem_sem.at[k])
        for k, (src, dst) in enumerate(((cols_buf, cols_smem), (blocks_buf, blocks_smem), (counts_buf, counts_smem)))
    ]
    for copy in to_smem:
        copy.start()
    for copy in to_smem:
        copy.wait()

    lane64 = lax.broadcasted_iota(jnp.int32, (64, 128), 1)
    row64 = lax.broadcasted_iota(jnp.int32, (64, 128), 0)
    left64 = lane64 < 64
    half64 = lane64 // 64
    lane1 = lax.broadcasted_iota(jnp.int32, (1, 128), 1)

    maps_q[core] = jnp.zeros((4, 128), F32)

    def step(s, carry):
        at = first_step + s

        @pl.when(lax.rem(s, CHUNK) == 0)
        def _():
            q = s // CHUNK
            there = pl.ds(CHUNK * q, CHUNK)
            for j in range(4):
                arrived(a_buf.at[j, there], recv_in.at[j, 0, q])
                arrived(b_buf.at[j, there], recv_in.at[j, 1, q])
                arrived(gain_buf.at[j, there], recv_in.at[j, 2, q])

        for j in range(4):
            thirds = b_buf[j, s].astype(F32)
            thirds_turned = pltpu.roll(thirds, 64, 1)
            for il in range(2):
                i = 2 * j + il
                pair = a_buf[j, s, il].astype(F32)
                turned = pltpu.roll(pair, 64, 1)
                block0 = jnp.where(left64, pair, turned)
                block1 = jnp.where(left64, turned, pair)
                block2 = jnp.where(left64 if il == 0 else jnp.logical_not(left64), thirds, thirds_turned)
                col1 = cols_smem[j, 1, il, at]
                col2 = cols_smem[j, 2, il, at]
                for p in range(4):
                    index = half64 + 2 * p
                    value = jnp.where(index == col1, block1, jnp.where(index == col2, block2, 0.0))
                    if p == j:
                        value = jnp.where(half64 == il, block0, value)
                    f_buf[i, :, p * 128 : (p + 1) * 128] = value
                    fn_buf[i, :, p * 128 : (p + 1) * 128] = value.astype(BF16)

        operator = op_buf[s].astype(F32)
        turned_operator = operator.T.astype(BF16)
        count = counts_smem[0, at]
        images, source_columns = [], []
        for o in range(2):
            block = blocks_smem[o, at]
            selected = fn_buf[block]
            images.append(jnp.dot(turned_operator[64 * o : 64 * o + 64], selected, preferred_element_type=F32))
            source_row = src_buf[block // 2, pl.ds(s, 1), :]
            offset = lax.rem(block, 2) * 64
            source_columns.append(
                jnp.sum(jnp.where(lane64 == row64 + offset, source_row, 0.0), axis=1, keepdims=True)
            )
        image = jnp.concatenate(images, axis=0)
        slot = lax.broadcasted_iota(jnp.int32, (128, NS), 0)
        masked = jnp.where(slot < count, image, 0.0).astype(BF16)
        gains = gain_buf[:, s].reshape(NS, 128)
        correction = jnp.dot(gains, masked, preferred_element_type=F32)
        e_buf[s] = (f_buf[...].reshape(NS, NS) - correction).astype(BF16)

        source_image = jnp.sum(
            operator * jnp.where(left64, source_columns[0], source_columns[1]), axis=0, keepdims=True
        )
        source_image = source_image.astype(BF16).astype(F32)
        innovation = jnp.where(lane1 < count, ov_buf[pl.ds(s, 1), :] - source_image, 0.0)
        offsets = []
        for g in range(4):
            moved = jnp.sum(gain_buf[g, s].astype(F32) * innovation, axis=1, keepdims=True)
            offsets.append(column_to_row(moved) + src_buf[g, pl.ds(s, 1), :])
        put_rows(off_buf.at[s], offsets)

        moved = matvec(block_of_plain(e_buf.at[s]), rows_of(maps_q.at[core]))
        put_rows(maps_q.at[core], [m + o for m, o in zip(moved, offsets)])

        @pl.when(s == 0)
        def _():
            for h in range(2):
                maps[core, h, 0] = e_buf[s, :, h * HALF : (h + 1) * HALF]
                maps[core, h, 1] = jnp.zeros((NS, HALF), BF16)

        @pl.when(s > 0)
        def _():
            for h in range(2):
                matrix = e_buf[s]
                value = jnp.dot(matrix, maps[core, h, 0], preferred_element_type=F32)
                value = value + jnp.dot(matrix, maps[core, h, 1], preferred_element_type=F32)
                maps[core, h, 0], maps[core, h, 1] = split(value)

        return carry

    lax.fori_loop(0, STEPS, step, 0)

    map_copy = remote(maps.at[core], maps.at[core], send_map.at[0], recv_map.at[0], sibling)
    q_copy = remote(maps_q.at[core], maps_q.at[core], send_map.at[1], recv_map.at[1], sibling)
    map_copy.start()
    q_copy.start()
    arrived(maps_q.at[other], recv_map.at[1])
    arrived(maps.at[other], recv_map.at[0])
    for h in range(2):
        total = product(maps.at[1], maps.at[0, core, :, :, pl.ds(128 * h, 128)])
        chip[4 * core + 2 * h], chip[4 * core + 2 * h + 1] = pack_pair(total)

    mine = pl.ds(4 * core, 4)
    theirs = pl.ds(4 * other, 4)

    def to_chip(j):
        return tm, j

    def share(ref, k):
        return remote(ref.at[mine], ref.at[mine], send_share.at[k], recv_share.at[k], sibling)

    def shared(ref, k):
        arrived(ref.at[theirs], recv_share.at[k])

    def chip_before_copy(k):
        n = 4 * core + k
        return remote(chip.at[n], before.at[n], send_before.at[k], recv_before.at[k], to_chip(1))

    def chip_left_copy(k):
        n = 4 * core + k
        return remote(chip.at[n], left.at[n], send_left.at[k], recv_left.at[k], to_chip(3))

    def first_copy(k):
        return remote(first.at[k], first.at[k], send_first.at[k], recv_first.at[k], to_chip(3))

    first_before_copy = remote(first, before.at[mine], send_before.at[4], recv_before.at[4], to_chip(2))

    def mate_copy(k):
        n = 4 * core + k
        return remote(whole.at[n], mate.at[n], send_mate.at[k], recv_mate.at[k], partner)

    def mate_on(k):
        n = 4 * core + k
        return remote(mate.at[n], mate.at[n], send_on.at[k], recv_on.at[k], sibling)

    vec_copies = (
        remote(chip_q, before_q, send_vec.at[0], recv_vec.at[0], to_chip(1)),
        remote(chip_q, left_q, send_vec.at[1], recv_vec.at[1], to_chip(3)),
        remote(first_q, first_q, send_vec.at[2], recv_vec.at[2], to_chip(3)),
        remote(first_q, before_q, send_vec.at[3], recv_vec.at[0], to_chip(2)),
        remote(whole_q, mate_q, send_vec.at[4], recv_vec.at[3], partner),
    )

    def chunks(step):
        def one(k, carry):
            step(k)
            return carry

        lax.fori_loop(0, 4, one, 0)

    @pl.when(y == 0)
    def _():
        chunks(lambda k: chip_before_copy(k).start())

    @pl.when(y == 2)
    def _():
        chunks(lambda k: chip_left_copy(k).start())

    @pl.when(lax.rem(y, 2) == 1)
    def _():
        share(chip, 0).start()

    half_map(maps.at[0], plain_c)
    half_map(maps.at[1], plain_b)
    moved = matvec(block_of_plain(plain_b), rows_of(maps_q.at[0]))
    put_rows(chip_q, sum_rows(moved, rows_of(maps_q.at[1])))

    @pl.when(y == 0)
    def _():
        vec_copies[0].start()

    @pl.when(y == 2)
    def _():
        vec_copies[1].start()

    @pl.when(lax.rem(y, 2) == 1)
    def _():
        shared(chip, 0)

    @pl.when(y == 1)
    def _():
        def one(k):
            n = 4 * core + k
            arrived(before.at[n], recv_before.at[k])
            first[k] = chunk_product(chip, before[n])
            first_copy(k).start()

        chunks(one)
        first_before_copy.start()
        share(before, 1).start()
        arrived(before_q, recv_vec.at[0])
        put_rows(first_q, sum_rows(packed_matvec(chip, rows_of(before_q)), rows_of(chip_q)))
        vec_copies[2].start()
        vec_copies[3].start()

    @pl.when(y == 2)
    def _():
        arrived(before.at[mine], recv_before.at[4])
        share(before, 1).start()
        arrived(before_q, recv_vec.at[0])

    @pl.when(y == 3)
    def _():
        def one_last(k):
            n = 4 * core + k
            arrived(left.at[n], recv_left.at[k])
            last[n] = chunk_product(chip, left[n])

        chunks(one_last)
        share(last, 2).start()
        share(left, 3).start()
        arrived(left_q, recv_vec.at[1])
        put_rows(whole_q, sum_rows(packed_matvec(chip, rows_of(left_q)), rows_of(chip_q)))
        shared(last, 2)

        def one_whole(k):
            n = 4 * core + k
            arrived(first.at[k], recv_first.at[k])
            whole[n] = chunk_product(last, first[k])

            @pl.when(is_mate)
            def _():
                mate_copy(k).start()

        chunks(one_whole)

        @pl.when(is_master)
        def _():
            share(whole, 4).start()

        arrived(first_q, recv_vec.at[2])
        put_rows(whole_q, sum_rows(packed_matvec(last, rows_of(first_q)), rows_of(whole_q)))

        @pl.when(is_mate)
        def _():
            vec_copies[4].start()

        shared(left, 3)

        def one_before(k):
            before[4 * core + k] = chunk_product(left, first[k])

        chunks(one_before)
        share(before, 1).start()
        put_rows(before_q, sum_rows(packed_matvec(left, rows_of(first_q)), rows_of(left_q)))

    @pl.when(is_master)
    def _():
        shared(whole, 4)
        to_plain(whole, plain_a)

        def one_mate(k):
            arrived(mate.at[4 * core + k], recv_mate.at[k])
            mate_on(k).start()

        chunks(one_mate)

    @pl.when(y > 0)
    def _():
        shared(before, 1)
        to_plain(before, plain_b)

    @pl.when(is_master)
    def _():
        arrived(mate_q, recv_vec.at[3])
        for k in range(4):
            arrived(mate.at[4 * other + k], recv_on.at[k])
        to_plain(mate, plain_d)

    def next_pair_copy():
        return remote(x_out, x_pair, send_x.at[8], recv_pair, device(master_column(pair + 1), 3))

    def next_copy(j):
        return remote(x_out, x_in, send_x.at[j], recv_x, device(2 * pair + 2, j))

    def second_copy(j):
        return remote(x_mid, x_in, send_x.at[4 + j], recv_x, device(2 * pair + 1, j))

    def apply(plain, vector, shift, out):
        moved = matvec(block_of_plain(plain), rows_of(vector))
        put_rows(out, [m + o for m, o in zip(moved, rows_of(shift))])

    @pl.when(jnp.logical_and(pair == 0, second == 0))
    def _():
        x_in[...] = prior_ref[...]

    @pl.when(jnp.logical_or(from_earlier, from_own))
    def _():
        arrived(x_in, recv_x)

    @pl.when(is_master)
    def _():
        @pl.when(even_pair)
        def _():
            @pl.when(pair == 0)
            def _():
                x_pair[...] = prior_ref[...]

            @pl.when(pair > 0)
            def _():
                arrived(x_pair, recv_pair)

            apply(plain_d, x_pair, mate_q, x_mid)
            apply(plain_a, x_mid, whole_q, x_out)

            @pl.when(sends_on)
            def _():
                for j in (3, 2, 1, 0):
                    next_copy(j).start()

            for j in range(3):
                second_copy(j).start()
            x_in[...] = x_mid[...]

        @pl.when(jnp.logical_not(even_pair))
        def _():
            apply(plain_a, x_in, whole_q, x_mid)
            apply(plain_d, x_mid, mate_q, x_out)

            @pl.when(sends_on)
            def _():
                next_pair_copy().start()
                for j in range(4):
                    next_copy(j).start()

            for j in range(4):
                second_copy(j).start()

    @pl.when(jnp.logical_and(jnp.logical_and(even_pair, second == 1), y < 3))
    def _():
        arrived(x_in, recv_x)

    @pl.when(y == 0)
    def _():
        x_work[...] = x_in[...]

    @pl.when(y > 0)
    def _():
        moved = matvec(block_of_plain(plain_b), rows_of(x_in))
        put_rows(x_work, [m + o for m, o in zip(moved, rows_of(before_q))])

    @pl.when(core == 1)
    def _():
        moved = matvec(block_of_plain(plain_c), rows_of(x_work))
        put_rows(x_work, [m + o for m, o in zip(moved, rows_of(maps_q.at[0]))])

    def sweep(s, carry):
        moved = matvec(block_of_plain(e_buf.at[s]), list(carry))
        rows = [m + o for m, o in zip(moved, rows_of(off_buf.at[s]))]
        for g in range(4):
            sweep_buf[g, pl.ds(s, 1), :] = rows[g]
        return tuple(rows)

    lax.fori_loop(0, STEPS, sweep, tuple(rows_of(x_work)))

    owner = first_tm + y // 2
    out_block = 2 * lax.rem(y, 2) + core
    here = pl.ds(8 * out_block, STEPS)

    def own_rows(g):
        return jnp.logical_and(owner == tm, g == y)

    for g in range(4):
        src, dst = sweep_buf.at[g], out_ref.at[here]

        @pl.when(jnp.logical_not(own_rows(g)))
        def _():
            remote(src, dst, send_out.at[g], recv_out.at[out_block], (owner, g)).start()

        @pl.when(own_rows(g))
        def _():
            pltpu.make_async_copy(src, dst, recv_out.at[out_block]).start()

    for b in range(4):
        arrived(out_ref.at[pl.ds(8 * b, STEPS)], recv_out.at[b])

    for g in range(4):
        @pl.when(jnp.logical_not(own_rows(g)))
        def _():
            remote(sweep_buf.at[g], out_ref.at[here], send_out.at[g], recv_out.at[out_block], (owner, g)).wait_send()

    for b in range(4):
        @pl.when(jnp.logical_not(is_me(b)))
        def _():
            for src, dst, kind in small_pairs(b):
                remote(src, dst, send_small.at[b, kind], recv_small.at[y, kind], target_of(b)).wait_send()

    def finish_chunk(q, carry):
        for b in range(4):
            @pl.when(jnp.logical_not(is_me(b)))
            def _():
                for src, dst, kind in big_pairs(b, q):
                    remote(src, dst, send_in.at[b, kind, q], recv_in.at[y, kind, q], target_of(b)).wait_send()
        return carry

    lax.fori_loop(0, NCHUNK, finish_chunk, 0)

    @pl.when(holds)
    def _():
        for mine, others, dst, kind in obs_arrays:
            remote(others, dst, send_obs.at[kind], recv_obs.at[kind], sibling).wait_send()

    map_copy.wait_send()
    q_copy.wait_send()

    @pl.when(y == 0)
    def _():
        chunks(lambda k: chip_before_copy(k).wait_send())
        vec_copies[0].wait_send()

    @pl.when(y == 1)
    def _():
        chunks(lambda k: first_copy(k).wait_send())
        first_before_copy.wait_send()
        vec_copies[2].wait_send()
        vec_copies[3].wait_send()

    @pl.when(y == 2)
    def _():
        chunks(lambda k: chip_left_copy(k).wait_send())
        vec_copies[1].wait_send()

    @pl.when(lax.rem(y, 2) == 1)
    def _():
        share(chip, 0).wait_send()

    @pl.when(y > 0)
    def _():
        share(before, 1).wait_send()

    @pl.when(y == 3)
    def _():
        share(last, 2).wait_send()
        share(left, 3).wait_send()

    @pl.when(is_mate)
    def _():
        chunks(lambda k: mate_copy(k).wait_send())
        vec_copies[4].wait_send()

    @pl.when(is_master)
    def _():
        share(whole, 4).wait_send()
        chunks(lambda k: mate_on(k).wait_send())
        for j in range(3):
            second_copy(j).wait_send()

    @pl.when(odd_master)
    def _():
        second_copy(3).wait_send()

    @pl.when(sends_on)
    def _():
        for j in range(4):
            next_copy(j).wait_send()

    @pl.when(jnp.logical_and(sends_on, odd_master))
    def _():
        next_pair_copy().wait_send()


def body(dyn_cols, dyn_vals, obs_blocks, obs_op, obs_counts, obs_values, gain, sources, prior):
    count = dyn_vals.shape[0]
    columns_count = lax.axis_size("tm") // 2
    cols = jnp.transpose(dyn_cols, (2, 1, 0))
    blocks = jnp.transpose(obs_blocks, (1, 0))
    counts = obs_counts.reshape(1, count)
    prior_rows = prior.reshape(4, 128)
    vmem = pl.BlockSpec(memory_space=pltpu.VMEM)
    hbm = pl.BlockSpec(memory_space=pl.ANY)
    dma = pltpu.SemaphoreType.DMA
    a_map = (2, 2, NS, HALF)
    packed_map = (8, NS, 128)

    def call(*refs):
        kernel(columns_count, *refs)

    return pl.pallas_call(
        call,
        out_shape=jax.ShapeDtypeStruct((count, 128), F32),
        in_specs=[hbm, hbm, hbm, vmem, vmem, vmem, vmem, vmem, vmem],
        out_specs=vmem,
        scratch_shapes=[
            pltpu.VMEM((count, 2, 64, 64), BF16),
            pltpu.VMEM((count, 64, 128), BF16),
            pltpu.VMEM((4, STEPS, 2, 64, 128), BF16),
            pltpu.VMEM((4, STEPS, 64, 128), BF16),
            pltpu.VMEM((4, STEPS, 128, 128), BF16),
            pltpu.VMEM((4, STEPS, 128), F32),
            pltpu.VMEM((4, *cols.shape), jnp.int32),
            pltpu.VMEM(blocks.shape, jnp.int32),
            pltpu.VMEM(counts.shape, jnp.int32),
            pltpu.SMEM((4, *cols.shape), jnp.int32),
            pltpu.SMEM(blocks.shape, jnp.int32),
            pltpu.SMEM(counts.shape, jnp.int32),
            pltpu.VMEM((STEPS, 64, 128), BF16),
            pltpu.VMEM((STEPS, 128), F32),
            pltpu.VMEM((8, 64, NS), F32),
            pltpu.VMEM((8, 64, NS), BF16),
            pltpu.VMEM((STEPS, NS, NS), BF16),
            pltpu.VMEM((STEPS, 4, 128), F32),
            pltpu.VMEM((2, *a_map), BF16),
            pltpu.VMEM((2, 4, 128), F32),
            pltpu.VMEM(packed_map, BF16),
            pltpu.VMEM((4, 128), F32),
            pltpu.VMEM(packed_map, BF16),
            pltpu.VMEM((4, 128), F32),
            pltpu.VMEM(packed_map, BF16),
            pltpu.VMEM((4, 128), F32),
            pltpu.VMEM((4, NS, 128), BF16),
            pltpu.VMEM((4, 128), F32),
            pltpu.VMEM(packed_map, BF16),
            pltpu.VMEM(packed_map, BF16),
            pltpu.VMEM((4, 128), F32),
            pltpu.VMEM(packed_map, BF16),
            pltpu.VMEM((4, 128), F32),
            pltpu.VMEM((NS, NS), F32),
            pltpu.VMEM((NS, NS), F32),
            pltpu.VMEM((NS, NS), F32),
            pltpu.VMEM((NS, NS), F32),
            pltpu.VMEM((4, 128), F32),
            pltpu.VMEM((4, 128), F32),
            pltpu.VMEM((4, 128), F32),
            pltpu.VMEM((4, 128), F32),
            pltpu.VMEM((4, 128), F32),
            pltpu.VMEM((4, STEPS, 128), F32),
            dma((4, 3, NCHUNK)), dma((4, 3, NCHUNK)),
            dma((4, 2)), dma((4, 2)),
            dma((4,)), dma((4,)), dma((3,)),
            dma((2,)), dma((2,)), dma((5,)), dma((5,)), dma((4,)), dma((4,)), dma((4,)), dma((4,)),
            dma((4,)), dma((4,)), dma((5,)), dma((4,)), dma((5,)), dma((5,)), dma((4,)), dma((4,)),
            dma((9,)), dma, dma, dma((4,)), dma((4,)), dma,
        ],
        compiler_params=pltpu.CompilerParams(
            collective_id=0, has_side_effects=True, vmem_limit_bytes=58 * 1024 * 1024
        ),
        cost_estimate=pl.CostEstimate(flops=10_000_000_000, bytes_accessed=4_000_000, transcendentals=0),
    )(dyn_vals, gain, obs_op, cols, blocks, counts, obs_values, sources, prior_rows)


def solution(mesh):
    return jax.shard_map(
        body,
        mesh=mesh,
        in_specs=(
            P("tm", "state", None),
            P("tm", "state", None, None),
            P("tm", None),
            P("tm", None, None),
            P("tm"),
            P("tm", None),
            P("tm", "state", None),
            P("tm", "state"),
            P(),
        ),
        out_specs=P("tm", "state"),
        check_vma=False,
    )
```

```python
import jax
import jax.numpy as jnp
from jax import lax
from jax.experimental import pallas as pl
from jax.experimental.pallas import tpu as pltpu
from jax.sharding import PartitionSpec as P

MESH = pl.DeviceIdType.MESH
F32 = jnp.float32
BF16 = jnp.bfloat16
NS = 512
HALF = 256
STEPS = 8
CHUNK = 2
NCHUNK = STEPS // CHUNK


def split(value):
    high = value.astype(BF16)
    low = (value - high.astype(F32)).astype(BF16)
    return high, low


def column_to_row(column):
    rows = lax.broadcasted_iota(jnp.int32, (128, 128), 0)
    lanes = lax.broadcasted_iota(jnp.int32, (128, 128), 1)
    return jnp.sum(jnp.where(rows == lanes, column, 0.0), axis=0, keepdims=True)


def matvec(load, vector):
    out = []
    for g in range(4):
        total = load(g, 0) * vector[0]
        for j in range(1, 4):
            total = total + load(g, j) * vector[j]
        out.append(column_to_row(jnp.sum(total, axis=1, keepdims=True)))
    return out


def rows_of(ref):
    return [ref[g : g + 1, :] for g in range(4)]


def put_rows(ref, rows):
    for g in range(4):
        ref[g : g + 1, :] = rows[g]


def block_of_plain(ref):
    def load(g, j):
        return ref[pl.ds(g * 128, 128), pl.ds(j * 128, 128)].astype(F32)

    return load


def product(left, right):
    total = None
    for h in range(2):
        rows = pl.ds(h * HALF, HALF)
        for a, b in ((0, 0), (0, 1), (1, 0)):
            term = jnp.dot(left[h, a], right[b, rows, :], preferred_element_type=F32)
            total = term if total is None else total + term
    return total


def half_map(maps_ref, out):
    for h in range(2):
        out[:, h * HALF : (h + 1) * HALF] = maps_ref[h, 0].astype(F32) + maps_ref[h, 1].astype(F32)


def left_lanes(shape):
    return lax.broadcasted_iota(jnp.int32, shape, 1) < 64


def pack_chunk(doubled):
    low = doubled - doubled.astype(BF16).astype(F32)
    return jnp.where(left_lanes(doubled.shape), doubled, low).astype(BF16)


def pack_pair(pair):
    turned = pltpu.roll(pair, 64, 1)
    left = left_lanes(pair.shape)
    return pack_chunk(jnp.where(left, pair, turned)), pack_chunk(jnp.where(left, turned, pair))


def chunk_product(left, right):
    rows = right.reshape(8, 64, 128)
    rows = jnp.concatenate([rows, rows], axis=1).reshape(2 * NS, 128)
    lanes = jnp.concatenate([left[n] for n in range(8)], axis=1)
    parts = jnp.dot(lanes, rows, preferred_element_type=F32)
    return pack_chunk(parts + pltpu.roll(parts, 64, 1))


def to_plain(packed, out):
    for n in range(4):
        first, second = packed[2 * n].astype(F32), packed[2 * n + 1].astype(F32)
        first, second = first + pltpu.roll(first, 64, 1), second + pltpu.roll(second, 64, 1)
        out[:, n * 128 : (n + 1) * 128] = jnp.where(left_lanes(first.shape), first, second)


def packed_matvec(packed, vector):
    doubled = []
    for row in vector:
        doubled.append(jnp.concatenate([row[:, :64], row[:, :64]], axis=1))
        doubled.append(jnp.concatenate([row[:, 64:], row[:, 64:]], axis=1))
    out = []
    for g in range(4):
        total = None
        for n in range(8):
            term = packed[n, pl.ds(g * 128, 128), :].astype(F32) * doubled[n]
            total = term if total is None else total + term
        out.append(column_to_row(jnp.sum(total, axis=1, keepdims=True)))
    return out


def sum_rows(a, b):
    return [m + o for m, o in zip(a, b)]


def kernel(
    columns_count,
    vals_ref, gain_ref, obs_op_ref, cols_ref, blocks_ref, counts_ref, obs_values_ref, sources_ref, prior_ref,
    out_ref,
    third, packed, a_buf, b_buf, gain_buf, src_buf, cols_buf, blocks_buf, counts_buf,
    cols_smem, blocks_smem, counts_smem, op_buf, ov_buf,
    f_buf, fn_buf, e_buf, off_buf,
    maps, maps_q, chip, chip_q, before, before_q, left, left_q, first, first_q, last, whole, whole_q,
    mate, mate_q, plain_a, plain_b, plain_c, plain_d, plain_e, x_in, x_pair, x_mid, x_out, x_end, x_work, sweep_buf,
    send_in, recv_in, send_small, recv_small, send_obs, recv_obs, smem_sem,
    send_map, recv_map, send_before, recv_before, send_left, recv_left, send_first, recv_first,
    send_mate, recv_mate, send_vec, recv_vec, send_share, recv_share, send_on, recv_on,
    send_x, recv_x, recv_pair, send_out, recv_out, third_sem, send_end,
):
    tm, y = lax.axis_index("tm"), lax.axis_index("state")
    core = lax.rem(tm, 2)
    column = tm // 2
    first_tm = tm - core
    other = 1 - core
    sibling = (first_tm + other, y)
    pair, second = column // 2, lax.rem(column, 2)
    even_pair = lax.rem(pair, 2) == 0
    last_pair = columns_count // 2 - 1

    def master_column(p):
        return 2 * p + 1 - lax.rem(p, 2)

    def device(c, j):
        return 2 * c + core, j

    single = column < 4
    last_row = column >= columns_count - 4
    end_column = columns_count - 1
    in_master = jnp.where(last_row, column == columns_count - 3, column == master_column(pair))
    at_last_chip = jnp.logical_and(y == 3, jnp.logical_not(single))
    single_master = jnp.logical_and(y == 3, single)
    is_master = jnp.logical_and(at_last_chip, in_master)
    is_mate = jnp.logical_and(
        at_last_chip, jnp.logical_and(jnp.logical_not(in_master), column != end_column)
    )
    end_master = jnp.logical_and(is_master, last_row)
    end_mate = jnp.logical_and(is_mate, column == columns_count - 2)
    partner = device(jnp.where(last_row, columns_count - 3, column + 1 - 2 * second), 3)
    mate_column = column + 1 - 2 * second
    mate_slot = jnp.where(column == columns_count - 2, 1, 0)

    barrier = pltpu.get_barrier_semaphore()

    def greet(where):
        pl.semaphore_signal(barrier, inc=1, device_id=where, device_id_type=MESH)

    for c in range(2):
        for j in range(4):
            @pl.when(jnp.logical_or(c != core, j != y))
            def _():
                greet((first_tm + c, j))

    third_copy = pltpu.make_async_copy(vals_ref.at[:, :, :, pl.ds(128, 64)], third, third_sem)
    third_copy.start()

    from_single = jnp.logical_and(column > 0, column <= 4)
    from_earlier = jnp.logical_and(second == 0, pair > 2)
    from_own = jnp.logical_and(second == 1, jnp.logical_not(jnp.logical_or(even_pair, single)))
    earlier_master = device(jnp.where(pair == 2, 3, master_column(pair - 1)), 3)

    @pl.when(from_single)
    def _():
        greet(device(column - 1, 3))

    @pl.when(from_earlier)
    def _():
        greet(earlier_master)

    @pl.when(from_own)
    def _():
        greet(device(jnp.where(last_row, columns_count - 3, column - 1), 3))

    even_master = jnp.logical_and(is_master, even_pair)
    odd_master = jnp.logical_and(is_master, jnp.logical_not(even_pair))

    @pl.when(even_master)
    def _():
        greet(earlier_master)

    @pl.when(is_master)
    def _():
        greet(device(mate_column, 3))

    @pl.when(end_master)
    def _():
        greet(device(column + 1, 3))

    sends_pair = jnp.logical_or(jnp.logical_and(single_master, column == 3), odd_master)
    peers = (
        7
        + jnp.where(jnp.logical_or(single_master, is_master), 4, 0)
        + jnp.where(is_mate, 1, 0)
        + jnp.where(odd_master, 4, 0)
        + jnp.where(end_master, 4, 0)
        + jnp.where(sends_pair, 1, 0)
    )
    pl.semaphore_wait(barrier, peers)

    def target_of(b):
        return first_tm + b % 2, 2 * core + b // 2

    def is_me(b):
        dest_tm, dest_y = target_of(b)
        return jnp.logical_and(dest_tm == tm, dest_y == y)

    def remote(src, dst, send, recv, device):
        return pltpu.make_async_remote_copy(
            src_ref=src, dst_ref=dst, send_sem=send, recv_sem=recv, device_id=device, device_id_type=MESH
        )

    def small_pairs(b):
        start = pl.ds(8 * b, STEPS)
        return (
            (sources_ref.at[start], src_buf.at[y], 0),
            (cols_ref, cols_buf.at[y], 1),
        )

    def big_pairs(b, q):
        start, there = pl.ds(8 * b + CHUNK * q, CHUNK), pl.ds(CHUNK * q, CHUNK)
        return (
            (vals_ref.at[start, :, :, pl.ds(0, 128)], a_buf.at[y, there], 0),
            (gain_ref.at[start], gain_buf.at[y, there], 2),
            (packed.at[start], b_buf.at[y, there], 1),
        )

    def send_pair(b, src, dst, send, recv):
        @pl.when(jnp.logical_not(is_me(b)))
        def _():
            remote(src, dst, send, recv, target_of(b)).start()

        @pl.when(is_me(b))
        def _():
            pltpu.make_async_copy(src, dst, recv).start()

    for b in range(4):
        for src, dst, kind in small_pairs(b):
            send_pair(b, src, dst, send_small.at[b, kind], recv_small.at[y, kind])

    holds = core == y // 2
    first_step = 16 * lax.rem(y, 2) + 8 * core
    mine_at = pl.ds(first_step, STEPS)
    other_at = pl.ds(16 * lax.rem(y, 2) + 8 * other, STEPS)
    obs_arrays = (
        (obs_op_ref.at[mine_at], obs_op_ref.at[other_at], op_buf, 0),
        (obs_values_ref.at[mine_at], obs_values_ref.at[other_at], ov_buf, 1),
        (blocks_ref, blocks_ref, blocks_buf, 2),
        (counts_ref, counts_ref, counts_buf, 3),
    )

    @pl.when(holds)
    def _():
        for mine, others, dst, kind in obs_arrays:
            remote(others, dst, send_obs.at[kind], recv_obs.at[kind], sibling).start()
            pltpu.make_async_copy(mine, dst, recv_obs.at[kind]).start()

    def start_chunk(q, carry):
        for b in range(4):
            for src, dst, kind in big_pairs(b, q)[:2]:
                send_pair(b, src, dst, send_in.at[b, kind, q], recv_in.at[y, kind, q])

        @pl.when(q == 0)
        def _():
            third_copy.wait()

        for b in range(4):
            for t in range(CHUNK):
                at = 8 * b + CHUNK * q + t
                packed[at] = jnp.concatenate([third[at, 0], third[at, 1]], axis=1)
        for b in range(4):
            src, dst, kind = big_pairs(b, q)[2]
            send_pair(b, src, dst, send_in.at[b, kind, q], recv_in.at[y, kind, q])
        return carry

    lax.fori_loop(0, NCHUNK, start_chunk, 0)

    def arrived(dst, sem):
        pltpu.make_async_copy(dst, dst, sem).wait()

    for j in range(4):
        arrived(src_buf.at[j], recv_small.at[j, 0])
        arrived(cols_buf.at[j], recv_small.at[j, 1])
    for _, _, dst, kind in obs_arrays:
        arrived(dst, recv_obs.at[kind])
    to_smem = [
        pltpu.make_async_copy(src, dst, smem_sem.at[k])
        for k, (src, dst) in enumerate(((cols_buf, cols_smem), (blocks_buf, blocks_smem), (counts_buf, counts_smem)))
    ]
    for copy in to_smem:
        copy.start()
    for copy in to_smem:
        copy.wait()

    lane64 = lax.broadcasted_iota(jnp.int32, (64, 128), 1)
    row64 = lax.broadcasted_iota(jnp.int32, (64, 128), 0)
    left64 = lane64 < 64
    half64 = lane64 // 64
    lane1 = lax.broadcasted_iota(jnp.int32, (1, 128), 1)

    maps_q[core] = jnp.zeros((4, 128), F32)

    def step(s, carry):
        at = first_step + s

        @pl.when(lax.rem(s, CHUNK) == 0)
        def _():
            q = s // CHUNK
            there = pl.ds(CHUNK * q, CHUNK)
            for j in range(4):
                arrived(a_buf.at[j, there], recv_in.at[j, 0, q])
                arrived(b_buf.at[j, there], recv_in.at[j, 1, q])
                arrived(gain_buf.at[j, there], recv_in.at[j, 2, q])

        for j in range(4):
            thirds = b_buf[j, s].astype(F32)
            thirds_turned = pltpu.roll(thirds, 64, 1)
            for il in range(2):
                i = 2 * j + il
                pair = a_buf[j, s, il].astype(F32)
                turned = pltpu.roll(pair, 64, 1)
                block0 = jnp.where(left64, pair, turned)
                block1 = jnp.where(left64, turned, pair)
                block2 = jnp.where(left64 if il == 0 else jnp.logical_not(left64), thirds, thirds_turned)
                col1 = cols_smem[j, 1, il, at]
                col2 = cols_smem[j, 2, il, at]
                for p in range(4):
                    index = half64 + 2 * p
                    value = jnp.where(index == col1, block1, jnp.where(index == col2, block2, 0.0))
                    if p == j:
                        value = jnp.where(half64 == il, block0, value)
                    f_buf[i, :, p * 128 : (p + 1) * 128] = value
                    fn_buf[i, :, p * 128 : (p + 1) * 128] = value.astype(BF16)

        operator = op_buf[s].astype(F32)
        turned_operator = operator.T.astype(BF16)
        count = counts_smem[0, at]
        images, source_columns = [], []
        for o in range(2):
            block = blocks_smem[o, at]
            selected = fn_buf[block]
            images.append(jnp.dot(turned_operator[64 * o : 64 * o + 64], selected, preferred_element_type=F32))
            source_row = src_buf[block // 2, pl.ds(s, 1), :]
            offset = lax.rem(block, 2) * 64
            source_columns.append(
                jnp.sum(jnp.where(lane64 == row64 + offset, source_row, 0.0), axis=1, keepdims=True)
            )
        image = jnp.concatenate(images, axis=0)
        slot = lax.broadcasted_iota(jnp.int32, (128, NS), 0)
        masked = jnp.where(slot < count, image, 0.0).astype(BF16)
        gains = gain_buf[:, s].reshape(NS, 128)
        correction = jnp.dot(gains, masked, preferred_element_type=F32)
        e_buf[s] = (f_buf[...].reshape(NS, NS) - correction).astype(BF16)

        source_image = jnp.sum(
            operator * jnp.where(left64, source_columns[0], source_columns[1]), axis=0, keepdims=True
        )
        source_image = source_image.astype(BF16).astype(F32)
        innovation = jnp.where(lane1 < count, ov_buf[pl.ds(s, 1), :] - source_image, 0.0)
        offsets = []
        for g in range(4):
            moved = jnp.sum(gain_buf[g, s].astype(F32) * innovation, axis=1, keepdims=True)
            offsets.append(column_to_row(moved) + src_buf[g, pl.ds(s, 1), :])
        put_rows(off_buf.at[s], offsets)

        moved = matvec(block_of_plain(e_buf.at[s]), rows_of(maps_q.at[core]))
        put_rows(maps_q.at[core], [m + o for m, o in zip(moved, offsets)])

        @pl.when(s == 0)
        def _():
            for h in range(2):
                maps[core, h, 0] = e_buf[s, :, h * HALF : (h + 1) * HALF]
                maps[core, h, 1] = jnp.zeros((NS, HALF), BF16)

        @pl.when(s > 0)
        def _():
            for h in range(2):
                matrix = e_buf[s]
                value = jnp.dot(matrix, maps[core, h, 0], preferred_element_type=F32)
                value = value + jnp.dot(matrix, maps[core, h, 1], preferred_element_type=F32)
                maps[core, h, 0], maps[core, h, 1] = split(value)

        return carry

    lax.fori_loop(0, STEPS, step, 0)

    map_copy = remote(maps.at[core], maps.at[core], send_map.at[0], recv_map.at[0], sibling)
    q_copy = remote(maps_q.at[core], maps_q.at[core], send_map.at[1], recv_map.at[1], sibling)
    map_copy.start()
    q_copy.start()
    arrived(maps_q.at[other], recv_map.at[1])
    arrived(maps.at[other], recv_map.at[0])
    for h in range(2):
        total = product(maps.at[1], maps.at[0, core, :, :, pl.ds(128 * h, 128)])
        chip[4 * core + 2 * h], chip[4 * core + 2 * h + 1] = pack_pair(total)

    mine = pl.ds(4 * core, 4)
    theirs = pl.ds(4 * other, 4)

    def to_chip(j):
        return tm, j

    def share(ref, k):
        return remote(ref.at[mine], ref.at[mine], send_share.at[k], recv_share.at[k], sibling)

    def shared(ref, k):
        arrived(ref.at[theirs], recv_share.at[k])

    def chip_before_copy(k):
        n = 4 * core + k
        return remote(chip.at[n], before.at[n], send_before.at[k], recv_before.at[k], to_chip(1))

    def chip_left_copy(k):
        n = 4 * core + k
        return remote(chip.at[n], left.at[n], send_left.at[k], recv_left.at[k], to_chip(3))

    def first_copy(k):
        return remote(first.at[k], first.at[k], send_first.at[k], recv_first.at[k], to_chip(3))

    first_before_copy = remote(first, before.at[mine], send_before.at[4], recv_before.at[4], to_chip(2))

    def mate_copy(k):
        n = 4 * core + k
        return remote(whole.at[n], mate.at[mate_slot, n], send_mate.at[k], recv_mate.at[mate_slot, k], partner)

    def mate_on(k, slot):
        n = 4 * core + k
        return remote(mate.at[slot, n], mate.at[slot, n], send_on.at[slot, k], recv_on.at[slot, k], sibling)

    vec_copies = (
        remote(chip_q, before_q, send_vec.at[0], recv_vec.at[0], to_chip(1)),
        remote(chip_q, left_q, send_vec.at[1], recv_vec.at[1], to_chip(3)),
        remote(first_q, first_q, send_vec.at[2], recv_vec.at[2], to_chip(3)),
        remote(first_q, before_q, send_vec.at[3], recv_vec.at[0], to_chip(2)),
        remote(whole_q, mate_q.at[mate_slot], send_vec.at[4], recv_vec.at[3 + mate_slot], partner),
    )

    def chunks(step):
        def one(k, carry):
            step(k)
            return carry

        lax.fori_loop(0, 4, one, 0)

    @pl.when(y == 0)
    def _():
        chunks(lambda k: chip_before_copy(k).start())

    @pl.when(y == 2)
    def _():
        chunks(lambda k: chip_left_copy(k).start())

    @pl.when(lax.rem(y, 2) == 1)
    def _():
        share(chip, 0).start()

    half_map(maps.at[0], plain_c)
    half_map(maps.at[1], plain_b)
    moved = matvec(block_of_plain(plain_b), rows_of(maps_q.at[0]))
    put_rows(chip_q, sum_rows(moved, rows_of(maps_q.at[1])))

    @pl.when(y == 0)
    def _():
        vec_copies[0].start()

    @pl.when(y == 2)
    def _():
        vec_copies[1].start()

    @pl.when(lax.rem(y, 2) == 1)
    def _():
        shared(chip, 0)

    @pl.when(y == 1)
    def _():
        def one(k):
            n = 4 * core + k
            arrived(before.at[n], recv_before.at[k])
            first[k] = chunk_product(chip, before[n])
            first_copy(k).start()

        chunks(one)
        first_before_copy.start()
        share(before, 1).start()
        arrived(before_q, recv_vec.at[0])
        put_rows(first_q, sum_rows(packed_matvec(chip, rows_of(before_q)), rows_of(chip_q)))
        vec_copies[2].start()
        vec_copies[3].start()

    @pl.when(y == 2)
    def _():
        arrived(before.at[mine], recv_before.at[4])
        share(before, 1).start()
        arrived(before_q, recv_vec.at[0])

    @pl.when(y == 3)
    def _():
        def one_last(k):
            n = 4 * core + k
            arrived(left.at[n], recv_left.at[k])
            last[n] = chunk_product(chip, left[n])

        chunks(one_last)
        share(last, 2).start()
        share(left, 3).start()
        arrived(left_q, recv_vec.at[1])
        put_rows(whole_q, sum_rows(packed_matvec(chip, rows_of(left_q)), rows_of(chip_q)))
        shared(last, 2)

        def one_whole(k):
            n = 4 * core + k
            arrived(first.at[k], recv_first.at[k])
            whole[n] = chunk_product(last, first[k])

            @pl.when(is_mate)
            def _():
                mate_copy(k).start()

        chunks(one_whole)

        @pl.when(jnp.logical_or(is_master, single_master))
        def _():
            share(whole, 4).start()

        arrived(first_q, recv_vec.at[2])
        put_rows(whole_q, sum_rows(packed_matvec(last, rows_of(first_q)), rows_of(whole_q)))

        @pl.when(is_mate)
        def _():
            vec_copies[4].start()

    def entry():
        @pl.when(column == 0)
        def _():
            x_in[...] = prior_ref[...]

        @pl.when(jnp.logical_or(from_single, jnp.logical_or(from_earlier, from_own)))
        def _():
            arrived(x_in, recv_x)

    def apply(plain, vector, shift, out):
        moved = matvec(block_of_plain(plain), rows_of(vector))
        put_rows(out, [m + o for m, o in zip(moved, rows_of(shift))])

    def next_pair_copy():
        there = jnp.where(single, 5, master_column(pair + 1))
        return remote(x_out, x_pair, send_x.at[8], recv_pair, device(there, 3))

    def next_copy(j):
        return remote(x_out, x_in, send_x.at[j], recv_x, device(jnp.where(single, column + 1, 2 * pair + 2), j))

    def second_copy(j):
        return remote(x_mid, x_in, send_x.at[4 + j], recv_x, device(2 * pair + 1, j))

    def end_copy(j):
        return remote(x_end, x_in, send_end.at[j], recv_x, device(end_column, j))

    @pl.when(single_master)
    def _():
        shared(whole, 4)
        to_plain(whole, plain_a)
        entry()
        apply(plain_a, x_in, whole_q, x_out)

        @pl.when(sends_pair)
        def _():
            next_pair_copy().start()

        for j in (3, 2, 1, 0):
            next_copy(j).start()

    @pl.when(y == 3)
    def _():
        shared(left, 3)

        def one_before(k):
            before[4 * core + k] = chunk_product(left, first[k])

        chunks(one_before)
        share(before, 1).start()
        put_rows(before_q, sum_rows(packed_matvec(left, rows_of(first_q)), rows_of(left_q)))

    @pl.when(is_master)
    def _():
        shared(whole, 4)
        to_plain(whole, plain_a)

        def one_mate(slot):
            def one(k):
                arrived(mate.at[slot, 4 * core + k], recv_mate.at[slot, k])
                mate_on(k, slot).start()

            chunks(one)

        one_mate(0)

        @pl.when(last_row)
        def _():
            one_mate(1)

    @pl.when(y > 0)
    def _():
        shared(before, 1)
        to_plain(before, plain_b)

    def take_mate(slot, plain):
        arrived(mate_q.at[slot], recv_vec.at[3 + slot])
        for k in range(4):
            arrived(mate.at[slot, 4 * other + k], recv_on.at[slot, k])
        to_plain(mate.at[slot], plain)

    @pl.when(jnp.logical_not(single_master))
    def _():
        @pl.when(is_master)
        def _():
            take_mate(0, plain_d)

            @pl.when(last_row)
            def _():
                take_mate(1, plain_e)

        entry()

    @pl.when(even_master)
    def _():
        arrived(x_pair, recv_pair)
        apply(plain_d, x_pair, mate_q.at[0], x_mid)
        apply(plain_a, x_mid, whole_q, x_out)

        @pl.when(last_row)
        def _():
            apply(plain_e, x_out, mate_q.at[1], x_end)
            for j in range(4):
                end_copy(j).start()

        for j in (3, 2, 1, 0):
            next_copy(j).start()
        for j in range(3):
            second_copy(j).start()
        x_in[...] = x_mid[...]

    @pl.when(odd_master)
    def _():
        apply(plain_a, x_in, whole_q, x_mid)
        apply(plain_d, x_mid, mate_q.at[0], x_out)
        next_pair_copy().start()
        for j in range(4):
            next_copy(j).start()
        for j in range(4):
            second_copy(j).start()

    waits_own = jnp.logical_and(jnp.logical_and(even_pair, second == 1), y < 3)

    @pl.when(jnp.logical_and(waits_own, jnp.logical_not(single)))
    def _():
        arrived(x_in, recv_x)

    @pl.when(y == 0)
    def _():
        x_work[...] = x_in[...]

    @pl.when(y > 0)
    def _():
        moved = matvec(block_of_plain(plain_b), rows_of(x_in))
        put_rows(x_work, [m + o for m, o in zip(moved, rows_of(before_q))])

    @pl.when(core == 1)
    def _():
        moved = matvec(block_of_plain(plain_c), rows_of(x_work))
        put_rows(x_work, [m + o for m, o in zip(moved, rows_of(maps_q.at[0]))])

    def sweep(s, carry):
        moved = matvec(block_of_plain(e_buf.at[s]), list(carry))
        rows = [m + o for m, o in zip(moved, rows_of(off_buf.at[s]))]
        for g in range(4):
            sweep_buf[g, pl.ds(s, 1), :] = rows[g]
        return tuple(rows)

    lax.fori_loop(0, STEPS, sweep, tuple(rows_of(x_work)))

    owner = first_tm + y // 2
    out_block = 2 * lax.rem(y, 2) + core
    here = pl.ds(8 * out_block, STEPS)

    def own_rows(g):
        return jnp.logical_and(owner == tm, g == y)

    for g in range(4):
        src, dst = sweep_buf.at[g], out_ref.at[here]

        @pl.when(jnp.logical_not(own_rows(g)))
        def _():
            remote(src, dst, send_out.at[g], recv_out.at[out_block], (owner, g)).start()

        @pl.when(own_rows(g))
        def _():
            pltpu.make_async_copy(src, dst, recv_out.at[out_block]).start()

    for b in range(4):
        arrived(out_ref.at[pl.ds(8 * b, STEPS)], recv_out.at[b])

    for g in range(4):
        @pl.when(jnp.logical_not(own_rows(g)))
        def _():
            remote(sweep_buf.at[g], out_ref.at[here], send_out.at[g], recv_out.at[out_block], (owner, g)).wait_send()

    for b in range(4):
        @pl.when(jnp.logical_not(is_me(b)))
        def _():
            for src, dst, kind in small_pairs(b):
                remote(src, dst, send_small.at[b, kind], recv_small.at[y, kind], target_of(b)).wait_send()

    def finish_chunk(q, carry):
        for b in range(4):
            @pl.when(jnp.logical_not(is_me(b)))
            def _():
                for src, dst, kind in big_pairs(b, q):
                    remote(src, dst, send_in.at[b, kind, q], recv_in.at[y, kind, q], target_of(b)).wait_send()
        return carry

    lax.fori_loop(0, NCHUNK, finish_chunk, 0)

    @pl.when(holds)
    def _():
        for mine, others, dst, kind in obs_arrays:
            remote(others, dst, send_obs.at[kind], recv_obs.at[kind], sibling).wait_send()

    map_copy.wait_send()
    q_copy.wait_send()

    @pl.when(y == 0)
    def _():
        chunks(lambda k: chip_before_copy(k).wait_send())
        vec_copies[0].wait_send()

    @pl.when(y == 1)
    def _():
        chunks(lambda k: first_copy(k).wait_send())
        first_before_copy.wait_send()
        vec_copies[2].wait_send()
        vec_copies[3].wait_send()

    @pl.when(y == 2)
    def _():
        chunks(lambda k: chip_left_copy(k).wait_send())
        vec_copies[1].wait_send()

    @pl.when(lax.rem(y, 2) == 1)
    def _():
        share(chip, 0).wait_send()

    @pl.when(y > 0)
    def _():
        share(before, 1).wait_send()

    @pl.when(y == 3)
    def _():
        share(last, 2).wait_send()
        share(left, 3).wait_send()

    @pl.when(is_mate)
    def _():
        chunks(lambda k: mate_copy(k).wait_send())
        vec_copies[4].wait_send()

    @pl.when(jnp.logical_or(is_master, single_master))
    def _():
        share(whole, 4).wait_send()
        for j in range(4):
            next_copy(j).wait_send()

    @pl.when(is_master)
    def _():
        chunks(lambda k: mate_on(k, 0).wait_send())
        for j in range(3):
            second_copy(j).wait_send()

    @pl.when(end_master)
    def _():
        chunks(lambda k: mate_on(k, 1).wait_send())
        for j in range(4):
            end_copy(j).wait_send()

    @pl.when(odd_master)
    def _():
        second_copy(3).wait_send()

    @pl.when(sends_pair)
    def _():
        next_pair_copy().wait_send()


def body(dyn_cols, dyn_vals, obs_blocks, obs_op, obs_counts, obs_values, gain, sources, prior):
    count = dyn_vals.shape[0]
    columns_count = lax.axis_size("tm") // 2
    cols = jnp.transpose(dyn_cols, (2, 1, 0))
    blocks = jnp.transpose(obs_blocks, (1, 0))
    counts = obs_counts.reshape(1, count)
    prior_rows = prior.reshape(4, 128)
    vmem = pl.BlockSpec(memory_space=pltpu.VMEM)
    hbm = pl.BlockSpec(memory_space=pl.ANY)
    dma = pltpu.SemaphoreType.DMA
    a_map = (2, 2, NS, HALF)
    packed_map = (8, NS, 128)

    def call(*refs):
        kernel(columns_count, *refs)

    return pl.pallas_call(
        call,
        out_shape=jax.ShapeDtypeStruct((count, 128), F32),
        in_specs=[hbm, hbm, hbm, vmem, vmem, vmem, vmem, vmem, vmem],
        out_specs=vmem,
        scratch_shapes=[
            pltpu.VMEM((count, 2, 64, 64), BF16),
            pltpu.VMEM((count, 64, 128), BF16),
            pltpu.VMEM((4, STEPS, 2, 64, 128), BF16),
            pltpu.VMEM((4, STEPS, 64, 128), BF16),
            pltpu.VMEM((4, STEPS, 128, 128), BF16),
            pltpu.VMEM((4, STEPS, 128), F32),
            pltpu.VMEM((4, *cols.shape), jnp.int32),
            pltpu.VMEM(blocks.shape, jnp.int32),
            pltpu.VMEM(counts.shape, jnp.int32),
            pltpu.SMEM((4, *cols.shape), jnp.int32),
            pltpu.SMEM(blocks.shape, jnp.int32),
            pltpu.SMEM(counts.shape, jnp.int32),
            pltpu.VMEM((STEPS, 64, 128), BF16),
            pltpu.VMEM((STEPS, 128), F32),
            pltpu.VMEM((8, 64, NS), F32),
            pltpu.VMEM((8, 64, NS), BF16),
            pltpu.VMEM((STEPS, NS, NS), BF16),
            pltpu.VMEM((STEPS, 4, 128), F32),
            pltpu.VMEM((2, *a_map), BF16),
            pltpu.VMEM((2, 4, 128), F32),
            pltpu.VMEM(packed_map, BF16),
            pltpu.VMEM((4, 128), F32),
            pltpu.VMEM(packed_map, BF16),
            pltpu.VMEM((4, 128), F32),
            pltpu.VMEM(packed_map, BF16),
            pltpu.VMEM((4, 128), F32),
            pltpu.VMEM((4, NS, 128), BF16),
            pltpu.VMEM((4, 128), F32),
            pltpu.VMEM(packed_map, BF16),
            pltpu.VMEM(packed_map, BF16),
            pltpu.VMEM((4, 128), F32),
            pltpu.VMEM((2, *packed_map), BF16),
            pltpu.VMEM((2, 4, 128), F32),
            pltpu.VMEM((NS, NS), F32),
            pltpu.VMEM((NS, NS), F32),
            pltpu.VMEM((NS, NS), F32),
            pltpu.VMEM((NS, NS), F32),
            pltpu.VMEM((NS, NS), F32),
            pltpu.VMEM((4, 128), F32),
            pltpu.VMEM((4, 128), F32),
            pltpu.VMEM((4, 128), F32),
            pltpu.VMEM((4, 128), F32),
            pltpu.VMEM((4, 128), F32),
            pltpu.VMEM((4, 128), F32),
            pltpu.VMEM((4, STEPS, 128), F32),
            dma((4, 3, NCHUNK)), dma((4, 3, NCHUNK)),
            dma((4, 2)), dma((4, 2)),
            dma((4,)), dma((4,)), dma((3,)),
            dma((2,)), dma((2,)), dma((5,)), dma((5,)), dma((4,)), dma((4,)), dma((4,)), dma((4,)),
            dma((4,)), dma((2, 4)), dma((5,)), dma((5,)), dma((5,)), dma((5,)), dma((2, 4)), dma((2, 4)),
            dma((9,)), dma, dma, dma((4,)), dma((4,)), dma, dma((4,)),
        ],
        compiler_params=pltpu.CompilerParams(
            collective_id=0, has_side_effects=True, vmem_limit_bytes=58 * 1024 * 1024
        ),
        cost_estimate=pl.CostEstimate(flops=10_000_000_000, bytes_accessed=4_000_000, transcendentals=0),
    )(dyn_vals, gain, obs_op, cols, blocks, counts, obs_values, sources, prior_rows)


def solution(mesh):
    return jax.shard_map(
        body,
        mesh=mesh,
        in_specs=(
            P("tm", "state", None),
            P("tm", "state", None, None),
            P("tm", None),
            P("tm", None, None),
            P("tm"),
            P("tm", None),
            P("tm", "state", None),
            P("tm", "state"),
            P(),
        ),
        out_specs=P("tm", "state"),
        check_vma=False,
    )
```

```python
import jax
import jax.numpy as jnp
from jax import lax
from jax.experimental import pallas as pl
from jax.experimental.pallas import tpu as pltpu
from jax.sharding import PartitionSpec as P

MESH = pl.DeviceIdType.MESH
F32 = jnp.float32
BF16 = jnp.bfloat16
NS = 512
HALF = 256
STEPS = 8
CHUNK = 2
NCHUNK = STEPS // CHUNK


def split(value):
    high = value.astype(BF16)
    low = (value - high.astype(F32)).astype(BF16)
    return high, low


def column_to_row(column):
    rows = lax.broadcasted_iota(jnp.int32, (128, 128), 0)
    lanes = lax.broadcasted_iota(jnp.int32, (128, 128), 1)
    return jnp.sum(jnp.where(rows == lanes, column, 0.0), axis=0, keepdims=True)


def matvec(load, vector):
    out = []
    for g in range(4):
        total = load(g, 0) * vector[0]
        for j in range(1, 4):
            total = total + load(g, j) * vector[j]
        out.append(column_to_row(jnp.sum(total, axis=1, keepdims=True)))
    return out


def rows_of(ref):
    return [ref[g : g + 1, :] for g in range(4)]


def put_rows(ref, rows):
    for g in range(4):
        ref[g : g + 1, :] = rows[g]


def block_of_plain(ref):
    def load(g, j):
        return ref[pl.ds(g * 128, 128), pl.ds(j * 128, 128)].astype(F32)

    return load


def product(left, right):
    total = None
    for h in range(2):
        rows = pl.ds(h * HALF, HALF)
        for a, b in ((0, 0), (0, 1), (1, 0)):
            term = jnp.dot(left[h, a], right[b, rows, :], preferred_element_type=F32)
            total = term if total is None else total + term
    return total


def half_map(maps_ref, out):
    for h in range(2):
        out[:, h * HALF : (h + 1) * HALF] = maps_ref[h, 0].astype(F32) + maps_ref[h, 1].astype(F32)


def left_lanes(shape):
    return lax.broadcasted_iota(jnp.int32, shape, 1) < 64


def pack_chunk(doubled):
    low = doubled - doubled.astype(BF16).astype(F32)
    return jnp.where(left_lanes(doubled.shape), doubled, low).astype(BF16)


def pack_pair(pair):
    turned = pltpu.roll(pair, 64, 1)
    left = left_lanes(pair.shape)
    return pack_chunk(jnp.where(left, pair, turned)), pack_chunk(jnp.where(left, turned, pair))


def chunk_product(left, right):
    rows = right.reshape(8, 64, 128)
    rows = jnp.concatenate([rows, rows], axis=1).reshape(2 * NS, 128)
    lanes = jnp.concatenate([left[n] for n in range(8)], axis=1)
    parts = jnp.dot(lanes, rows, preferred_element_type=F32)
    return pack_chunk(parts + pltpu.roll(parts, 64, 1))


def to_plain(packed, out):
    for n in range(4):
        first, second = packed[2 * n].astype(F32), packed[2 * n + 1].astype(F32)
        first, second = first + pltpu.roll(first, 64, 1), second + pltpu.roll(second, 64, 1)
        out[:, n * 128 : (n + 1) * 128] = jnp.where(left_lanes(first.shape), first, second)


def packed_matvec(packed, vector):
    doubled = []
    for row in vector:
        doubled.append(jnp.concatenate([row[:, :64], row[:, :64]], axis=1))
        doubled.append(jnp.concatenate([row[:, 64:], row[:, 64:]], axis=1))
    out = []
    for g in range(4):
        total = None
        for n in range(8):
            term = packed[n, pl.ds(g * 128, 128), :].astype(F32) * doubled[n]
            total = term if total is None else total + term
        out.append(column_to_row(jnp.sum(total, axis=1, keepdims=True)))
    return out


def sum_rows(a, b):
    return [m + o for m, o in zip(a, b)]


def kernel(
    columns_count,
    vals_ref, gain_ref, obs_op_ref, cols_ref, blocks_ref, counts_ref, obs_values_ref, sources_ref, prior_ref,
    out_ref,
    third, packed, a_buf, b_buf, gain_buf, src_buf, cols_buf, blocks_buf, counts_buf,
    cols_smem, blocks_smem, counts_smem, op_buf, ov_buf,
    f_buf, fn_buf, e_buf, off_buf,
    maps, maps_q, chip, chip_q, before, before_q, left, left_q, first, first_q, last, whole, whole_q,
    mate, mate_q, plain_a, plain_b, plain_c, plain_d, plain_e, x_in, x_pair, x_mid, x_out, x_end, x_work, sweep_buf,
    send_in, recv_in, send_small, recv_small, send_obs, recv_obs, smem_sem,
    send_map, recv_map, send_before, recv_before, send_left, recv_left, send_first, recv_first,
    send_mate, recv_mate, send_vec, recv_vec, send_share, recv_share, send_on, recv_on,
    send_x, recv_x, recv_pair, send_out, recv_out, third_sem, send_end, prior_sem,
):
    tm, y = lax.axis_index("tm"), lax.axis_index("state")
    core = lax.rem(tm, 2)
    column = tm // 2
    first_tm = tm - core
    other = 1 - core
    sibling = (first_tm + other, y)
    pair, second = column // 2, lax.rem(column, 2)
    even_pair = lax.rem(pair, 2) == 0
    last_pair = columns_count // 2 - 1

    def master_column(p):
        return 2 * p + 1 - lax.rem(p, 2)

    def device(c, j):
        return 2 * c + core, j

    single = column < 4
    last_row = column >= columns_count - 4
    end_column = columns_count - 1
    in_master = jnp.where(last_row, column == columns_count - 3, column == master_column(pair))
    at_last_chip = jnp.logical_and(y == 3, jnp.logical_not(single))
    first_column = column == 0
    merges = column > 0
    single_master = jnp.logical_and(y == 3, jnp.logical_and(single, merges))
    exits_first = jnp.logical_and(first_column, y == 3)
    is_master = jnp.logical_and(at_last_chip, in_master)
    is_mate = jnp.logical_and(
        at_last_chip, jnp.logical_and(jnp.logical_not(in_master), column != end_column)
    )
    end_master = jnp.logical_and(is_master, last_row)
    end_mate = jnp.logical_and(is_mate, column == columns_count - 2)
    partner = device(jnp.where(last_row, columns_count - 3, column + 1 - 2 * second), 3)
    mate_column = column + 1 - 2 * second
    mate_slot = jnp.where(column == columns_count - 2, 1, 0)

    barrier = pltpu.get_barrier_semaphore()

    def greet(where):
        pl.semaphore_signal(barrier, inc=1, device_id=where, device_id_type=MESH)

    for c in range(2):
        for j in range(4):
            @pl.when(jnp.logical_or(c != core, j != y))
            def _():
                greet((first_tm + c, j))

    third_copy = pltpu.make_async_copy(vals_ref.at[:, :, :, pl.ds(128, 64)], third, third_sem)
    third_copy.start()
    prior_copy = pltpu.make_async_copy(prior_ref, x_in, prior_sem)
    starts = jnp.logical_and(column == 0, y == 0)

    @pl.when(starts)
    def _():
        prior_copy.start()


    from_single = jnp.logical_and(column > 0, column <= 4)
    from_earlier = jnp.logical_and(second == 0, pair > 2)
    from_own = jnp.logical_and(second == 1, jnp.logical_not(jnp.logical_or(even_pair, single)))
    earlier_master = device(jnp.where(pair == 2, 3, master_column(pair - 1)), 3)

    @pl.when(from_single)
    def _():
        greet(device(column - 1, 3))

    @pl.when(from_earlier)
    def _():
        greet(earlier_master)

    @pl.when(from_own)
    def _():
        greet(device(jnp.where(last_row, columns_count - 3, column - 1), 3))

    even_master = jnp.logical_and(is_master, even_pair)
    odd_master = jnp.logical_and(is_master, jnp.logical_not(even_pair))

    @pl.when(even_master)
    def _():
        greet(earlier_master)

    @pl.when(is_master)
    def _():
        greet(device(mate_column, 3))

    @pl.when(end_master)
    def _():
        greet(device(column + 1, 3))

    sends_pair = jnp.logical_or(jnp.logical_and(single_master, column == 3), odd_master)
    peers = (
        7
        + jnp.where(jnp.logical_or(exits_first, jnp.logical_or(single_master, is_master)), 4, 0)
        + jnp.where(is_mate, 1, 0)
        + jnp.where(odd_master, 4, 0)
        + jnp.where(end_master, 4, 0)
        + jnp.where(sends_pair, 1, 0)
    )
    pl.semaphore_wait(barrier, peers)

    def target_of(b):
        return first_tm + b % 2, 2 * core + b // 2

    def is_me(b):
        dest_tm, dest_y = target_of(b)
        return jnp.logical_and(dest_tm == tm, dest_y == y)

    def remote(src, dst, send, recv, device):
        return pltpu.make_async_remote_copy(
            src_ref=src, dst_ref=dst, send_sem=send, recv_sem=recv, device_id=device, device_id_type=MESH
        )

    def small_pairs(b):
        start = pl.ds(8 * b, STEPS)
        return (
            (sources_ref.at[start], src_buf.at[y], 0),
            (cols_ref, cols_buf.at[y], 1),
        )

    def big_pairs(b, q):
        start, there = pl.ds(8 * b + CHUNK * q, CHUNK), pl.ds(CHUNK * q, CHUNK)
        return (
            (vals_ref.at[start, :, :, pl.ds(0, 128)], a_buf.at[y, there], 0),
            (packed.at[start], b_buf.at[y, there], 1),
            (gain_ref.at[start], gain_buf.at[y, there], 2),
        )

    def send_pair(b, src, dst, send, recv):
        @pl.when(jnp.logical_not(is_me(b)))
        def _():
            remote(src, dst, send, recv, target_of(b)).start()

        @pl.when(is_me(b))
        def _():
            pltpu.make_async_copy(src, dst, recv).start()

    for b in range(4):
        for src, dst, kind in small_pairs(b):
            send_pair(b, src, dst, send_small.at[b, kind], recv_small.at[y, kind])

    holds = core == y // 2
    first_step = 16 * lax.rem(y, 2) + 8 * core
    mine_at = pl.ds(first_step, STEPS)
    other_at = pl.ds(16 * lax.rem(y, 2) + 8 * other, STEPS)
    obs_arrays = (
        (obs_op_ref.at[mine_at], obs_op_ref.at[other_at], op_buf, 0),
        (obs_values_ref.at[mine_at], obs_values_ref.at[other_at], ov_buf, 1),
        (blocks_ref, blocks_ref, blocks_buf, 2),
        (counts_ref, counts_ref, counts_buf, 3),
    )

    @pl.when(holds)
    def _():
        for mine, others, dst, kind in obs_arrays:
            remote(others, dst, send_obs.at[kind], recv_obs.at[kind], sibling).start()
            pltpu.make_async_copy(mine, dst, recv_obs.at[kind]).start()

    def start_chunk(q, carry):
        for b in range(4):
            for src, dst, kind in big_pairs(b, q)[:1]:
                send_pair(b, src, dst, send_in.at[b, kind, q], recv_in.at[y, kind, q])

        @pl.when(q == 0)
        def _():
            third_copy.wait()

        for b in range(4):
            for t in range(CHUNK):
                at = 8 * b + CHUNK * q + t
                packed[at] = jnp.concatenate([third[at, 0], third[at, 1]], axis=1)
        for k in (1, 2):
            for b in range(4):
                src, dst, kind = big_pairs(b, q)[k]
                send_pair(b, src, dst, send_in.at[b, kind, q], recv_in.at[y, kind, q])
        return carry

    lax.fori_loop(0, NCHUNK, start_chunk, 0)

    def arrived(dst, sem):
        pltpu.make_async_copy(dst, dst, sem).wait()

    for j in range(4):
        arrived(src_buf.at[j], recv_small.at[j, 0])
        arrived(cols_buf.at[j], recv_small.at[j, 1])
    for _, _, dst, kind in obs_arrays:
        arrived(dst, recv_obs.at[kind])
    to_smem = [
        pltpu.make_async_copy(src, dst, smem_sem.at[k])
        for k, (src, dst) in enumerate(((cols_buf, cols_smem), (blocks_buf, blocks_smem), (counts_buf, counts_smem)))
    ]
    for copy in to_smem:
        copy.start()
    for copy in to_smem:
        copy.wait()

    lane64 = lax.broadcasted_iota(jnp.int32, (64, 128), 1)
    row64 = lax.broadcasted_iota(jnp.int32, (64, 128), 0)
    left64 = lane64 < 64
    half64 = lane64 // 64
    lane1 = lax.broadcasted_iota(jnp.int32, (1, 128), 1)

    maps_q[core] = jnp.zeros((4, 128), F32)

    def step(s, carry):
        at = first_step + s

        @pl.when(lax.rem(s, CHUNK) == 0)
        def _():
            q = s // CHUNK
            there = pl.ds(CHUNK * q, CHUNK)
            for j in range(4):
                arrived(a_buf.at[j, there], recv_in.at[j, 0, q])
                arrived(b_buf.at[j, there], recv_in.at[j, 1, q])

        for j in range(4):
            thirds = b_buf[j, s].astype(F32)
            thirds_turned = pltpu.roll(thirds, 64, 1)
            for il in range(2):
                i = 2 * j + il
                pair = a_buf[j, s, il].astype(F32)
                turned = pltpu.roll(pair, 64, 1)
                block0 = jnp.where(left64, pair, turned)
                block1 = jnp.where(left64, turned, pair)
                block2 = jnp.where(left64 if il == 0 else jnp.logical_not(left64), thirds, thirds_turned)
                col1 = cols_smem[j, 1, il, at]
                col2 = cols_smem[j, 2, il, at]
                for p in range(4):
                    index = half64 + 2 * p
                    value = jnp.where(index == col1, block1, jnp.where(index == col2, block2, 0.0))
                    if p == j:
                        value = jnp.where(half64 == il, block0, value)
                    f_buf[i, :, p * 128 : (p + 1) * 128] = value
                    fn_buf[i, :, p * 128 : (p + 1) * 128] = value.astype(BF16)

        operator = op_buf[s].astype(F32)
        turned_operator = operator.T.astype(BF16)
        count = counts_smem[0, at]
        images, source_columns = [], []
        for o in range(2):
            block = blocks_smem[o, at]
            selected = fn_buf[block]
            images.append(jnp.dot(turned_operator[64 * o : 64 * o + 64], selected, preferred_element_type=F32))
            source_row = src_buf[block // 2, pl.ds(s, 1), :]
            offset = lax.rem(block, 2) * 64
            source_columns.append(
                jnp.sum(jnp.where(lane64 == row64 + offset, source_row, 0.0), axis=1, keepdims=True)
            )
        image = jnp.concatenate(images, axis=0)
        slot = lax.broadcasted_iota(jnp.int32, (128, NS), 0)
        masked = jnp.where(slot < count, image, 0.0).astype(BF16)

        @pl.when(lax.rem(s, CHUNK) == 0)
        def _():
            q = s // CHUNK
            for j in range(4):
                arrived(gain_buf.at[j, pl.ds(CHUNK * q, CHUNK)], recv_in.at[j, 2, q])

        gains = gain_buf[:, s].reshape(NS, 128)
        correction = jnp.dot(gains, masked, preferred_element_type=F32)
        e_buf[s] = (f_buf[...].reshape(NS, NS) - correction).astype(BF16)

        source_image = jnp.sum(
            operator * jnp.where(left64, source_columns[0], source_columns[1]), axis=0, keepdims=True
        )
        source_image = source_image.astype(BF16).astype(F32)
        innovation = jnp.where(lane1 < count, ov_buf[pl.ds(s, 1), :] - source_image, 0.0)
        offsets = []
        for g in range(4):
            moved = jnp.sum(gain_buf[g, s].astype(F32) * innovation, axis=1, keepdims=True)
            offsets.append(column_to_row(moved) + src_buf[g, pl.ds(s, 1), :])
        put_rows(off_buf.at[s], offsets)

        moved = matvec(block_of_plain(e_buf.at[s]), rows_of(maps_q.at[core]))
        put_rows(maps_q.at[core], [m + o for m, o in zip(moved, offsets)])

        @pl.when(s == 0)
        def _():
            for h in range(2):
                maps[core, h, 0] = e_buf[s, :, h * HALF : (h + 1) * HALF]
                maps[core, h, 1] = jnp.zeros((NS, HALF), BF16)

        @pl.when(s > 0)
        def _():
            for h in range(2):
                matrix = e_buf[s]
                value = jnp.dot(matrix, maps[core, h, 0], preferred_element_type=F32)
                value = value + jnp.dot(matrix, maps[core, h, 1], preferred_element_type=F32)
                maps[core, h, 0], maps[core, h, 1] = split(value)

        return carry

    lax.fori_loop(0, STEPS, step, 0)

    map_copy = remote(maps.at[core], maps.at[core], send_map.at[0], recv_map.at[0], sibling)
    q_copy = remote(maps_q.at[core], maps_q.at[core], send_map.at[1], recv_map.at[1], sibling)
    map_copy.start()
    q_copy.start()
    arrived(maps_q.at[other], recv_map.at[1])
    arrived(maps.at[other], recv_map.at[0])
    mine = pl.ds(4 * core, 4)
    theirs = pl.ds(4 * other, 4)

    def to_chip(j):
        return tm, j

    def share(ref, k):
        return remote(ref.at[mine], ref.at[mine], send_share.at[k], recv_share.at[k], sibling)

    def shared(ref, k):
        arrived(ref.at[theirs], recv_share.at[k])

    def chip_before_copy(k):
        n = 4 * core + k
        return remote(chip.at[n], before.at[n], send_before.at[k], recv_before.at[k], to_chip(1))

    def chip_left_copy(k):
        n = 4 * core + k
        return remote(chip.at[n], left.at[n], send_left.at[k], recv_left.at[k], to_chip(3))

    def first_copy(k):
        return remote(first.at[k], first.at[k], send_first.at[k], recv_first.at[k], to_chip(3))

    first_before_copy = remote(first, before.at[mine], send_before.at[4], recv_before.at[4], to_chip(2))

    def mate_copy(k):
        n = 4 * core + k
        return remote(whole.at[n], mate.at[mate_slot, n], send_mate.at[k], recv_mate.at[mate_slot, k], partner)

    def mate_on(k, slot):
        n = 4 * core + k
        return remote(mate.at[slot, n], mate.at[slot, n], send_on.at[slot, k], recv_on.at[slot, k], sibling)

    vec_copies = (
        remote(chip_q, before_q, send_vec.at[0], recv_vec.at[0], to_chip(1)),
        remote(chip_q, left_q, send_vec.at[1], recv_vec.at[1], to_chip(3)),
        remote(first_q, first_q, send_vec.at[2], recv_vec.at[2], to_chip(3)),
        remote(first_q, before_q, send_vec.at[3], recv_vec.at[0], to_chip(2)),
        remote(whole_q, mate_q.at[mate_slot], send_vec.at[4], recv_vec.at[3 + mate_slot], partner),
    )

    def chunks(step):
        def one(k, carry):
            step(k)
            return carry

        lax.fori_loop(0, 4, one, 0)

    for h in range(2):
        total = product(maps.at[1], maps.at[0, core, :, :, pl.ds(128 * h, 128)])
        chip[4 * core + 2 * h], chip[4 * core + 2 * h + 1] = pack_pair(total)
        for k in (2 * h, 2 * h + 1):
            @pl.when(jnp.logical_and(merges, y == 0))
            def _():
                chip_before_copy(k).start()

            @pl.when(jnp.logical_and(merges, y == 2))
            def _():
                chip_left_copy(k).start()

    shares_chip = jnp.logical_or(first_column, lax.rem(y, 2) == 1)

    @pl.when(shares_chip)
    def _():
        share(chip, 0).start()

    half_map(maps.at[0], plain_c)
    half_map(maps.at[1], plain_b)
    moved = matvec(block_of_plain(plain_b), rows_of(maps_q.at[0]))
    put_rows(chip_q, sum_rows(moved, rows_of(maps_q.at[1])))

    @pl.when(merges & (y == 0))
    def _():
        vec_copies[0].start()

    @pl.when(merges & (y == 2))
    def _():
        vec_copies[1].start()

    @pl.when(shares_chip)
    def _():
        shared(chip, 0)

    def entry():
        @pl.when(jnp.logical_or(from_single, jnp.logical_or(from_earlier, from_own)))
        def _():
            arrived(x_in, recv_x)

    def apply(plain, vector, shift, out):
        moved = matvec(block_of_plain(plain), rows_of(vector))
        put_rows(out, [m + o for m, o in zip(moved, rows_of(shift))])

    def next_pair_copy():
        there = jnp.where(single, 5, master_column(pair + 1))
        return remote(x_out, x_pair, send_x.at[8], recv_pair, device(there, 3))

    def next_copy(j):
        return remote(x_out, x_in, send_x.at[j], recv_x, device(jnp.where(single, column + 1, 2 * pair + 2), j))

    def second_copy(j):
        return remote(x_mid, x_in, send_x.at[4 + j], recv_x, device(2 * pair + 1, j))

    def end_copy(j):
        return remote(x_end, x_in, send_end.at[j], recv_x, device(end_column, j))

    along_copy = remote(x_out, x_in, send_end.at[0], recv_x, to_chip(lax.rem(y + 1, 4)))

    @pl.when(first_column)
    def _():
        @pl.when(y == 0)
        def _():
            prior_copy.wait()

        @pl.when(y > 0)
        def _():
            arrived(x_in, recv_x)

        put_rows(x_out, sum_rows(packed_matvec(chip, rows_of(x_in)), rows_of(chip_q)))

        @pl.when(y < 3)
        def _():
            along_copy.start()

        @pl.when(y == 3)
        def _():
            for j in (3, 2, 1, 0):
                next_copy(j).start()

    @pl.when(merges & (y == 1))
    def _():
        def one(k):
            n = 4 * core + k
            arrived(before.at[n], recv_before.at[k])
            first[k] = chunk_product(chip, before[n])
            first_copy(k).start()

        chunks(one)
        first_before_copy.start()
        share(before, 1).start()
        arrived(before_q, recv_vec.at[0])
        put_rows(first_q, sum_rows(packed_matvec(chip, rows_of(before_q)), rows_of(chip_q)))
        vec_copies[2].start()
        vec_copies[3].start()

    @pl.when(merges & (y == 2))
    def _():
        arrived(before.at[mine], recv_before.at[4])
        share(before, 1).start()
        arrived(before_q, recv_vec.at[0])

    @pl.when(merges & (y == 3))
    def _():
        def one_last(k):
            n = 4 * core + k
            arrived(left.at[n], recv_left.at[k])
            last[n] = chunk_product(chip, left[n])

        chunks(one_last)
        share(last, 2).start()
        share(left, 3).start()
        arrived(left_q, recv_vec.at[1])
        put_rows(whole_q, sum_rows(packed_matvec(chip, rows_of(left_q)), rows_of(chip_q)))
        shared(last, 2)

        def one_whole(k):
            n = 4 * core + k
            arrived(first.at[k], recv_first.at[k])
            whole[n] = chunk_product(last, first[k])

            @pl.when(is_mate)
            def _():
                mate_copy(k).start()

        chunks(one_whole)

        @pl.when(jnp.logical_or(is_master, single_master))
        def _():
            share(whole, 4).start()

        arrived(first_q, recv_vec.at[2])
        put_rows(whole_q, sum_rows(packed_matvec(last, rows_of(first_q)), rows_of(whole_q)))

        @pl.when(is_mate)
        def _():
            vec_copies[4].start()

    @pl.when(single_master)
    def _():
        shared(whole, 4)
        to_plain(whole, plain_a)
        entry()
        apply(plain_a, x_in, whole_q, x_out)

        @pl.when(sends_pair)
        def _():
            next_pair_copy().start()

        for j in (3, 2, 1, 0):
            next_copy(j).start()

    @pl.when(merges & (y == 3))
    def _():
        shared(left, 3)

        def one_before(k):
            before[4 * core + k] = chunk_product(left, first[k])

        chunks(one_before)
        share(before, 1).start()
        put_rows(before_q, sum_rows(packed_matvec(left, rows_of(first_q)), rows_of(left_q)))

    @pl.when(is_master)
    def _():
        shared(whole, 4)
        to_plain(whole, plain_a)

        def one_mate(slot):
            def one(k):
                arrived(mate.at[slot, 4 * core + k], recv_mate.at[slot, k])
                mate_on(k, slot).start()

            chunks(one)

        one_mate(0)

        @pl.when(last_row)
        def _():
            one_mate(1)

    @pl.when(merges & (y > 0))
    def _():
        shared(before, 1)
        to_plain(before, plain_b)

    def take_mate(slot, plain):
        arrived(mate_q.at[slot], recv_vec.at[3 + slot])
        for k in range(4):
            arrived(mate.at[slot, 4 * other + k], recv_on.at[slot, k])
        to_plain(mate.at[slot], plain)

    @pl.when(jnp.logical_not(single_master))
    def _():
        @pl.when(is_master)
        def _():
            take_mate(0, plain_d)

            @pl.when(last_row)
            def _():
                take_mate(1, plain_e)

        entry()

    @pl.when(even_master)
    def _():
        arrived(x_pair, recv_pair)
        apply(plain_d, x_pair, mate_q.at[0], x_mid)
        apply(plain_a, x_mid, whole_q, x_out)

        @pl.when(last_row)
        def _():
            apply(plain_e, x_out, mate_q.at[1], x_end)
            for j in range(4):
                end_copy(j).start()

        for j in (3, 2, 1, 0):
            next_copy(j).start()
        for j in range(3):
            second_copy(j).start()
        x_in[...] = x_mid[...]

    @pl.when(odd_master)
    def _():
        apply(plain_a, x_in, whole_q, x_mid)
        apply(plain_d, x_mid, mate_q.at[0], x_out)
        next_pair_copy().start()
        for j in range(4):
            next_copy(j).start()
        for j in range(4):
            second_copy(j).start()

    waits_own = jnp.logical_and(jnp.logical_and(even_pair, second == 1), y < 3)

    @pl.when(jnp.logical_and(waits_own, jnp.logical_not(single)))
    def _():
        arrived(x_in, recv_x)

    enters = jnp.logical_or(first_column, y == 0)

    @pl.when(enters)
    def _():
        x_work[...] = x_in[...]

    @pl.when(jnp.logical_not(enters))
    def _():
        moved = matvec(block_of_plain(plain_b), rows_of(x_in))
        put_rows(x_work, [m + o for m, o in zip(moved, rows_of(before_q))])

    @pl.when(core == 1)
    def _():
        moved = matvec(block_of_plain(plain_c), rows_of(x_work))
        put_rows(x_work, [m + o for m, o in zip(moved, rows_of(maps_q.at[0]))])

    def sweep(s, carry):
        moved = matvec(block_of_plain(e_buf.at[s]), list(carry))
        rows = [m + o for m, o in zip(moved, rows_of(off_buf.at[s]))]
        for g in range(4):
            sweep_buf[g, pl.ds(s, 1), :] = rows[g]
        return tuple(rows)

    lax.fori_loop(0, STEPS, sweep, tuple(rows_of(x_work)))

    owner = first_tm + y // 2
    out_block = 2 * lax.rem(y, 2) + core
    here = pl.ds(8 * out_block, STEPS)

    def own_rows(g):
        return jnp.logical_and(owner == tm, g == y)

    for g in range(4):
        src, dst = sweep_buf.at[g], out_ref.at[here]

        @pl.when(jnp.logical_not(own_rows(g)))
        def _():
            remote(src, dst, send_out.at[g], recv_out.at[out_block], (owner, g)).start()

        @pl.when(own_rows(g))
        def _():
            pltpu.make_async_copy(src, dst, recv_out.at[out_block]).start()

    for b in range(4):
        arrived(out_ref.at[pl.ds(8 * b, STEPS)], recv_out.at[b])

    for g in range(4):
        @pl.when(jnp.logical_not(own_rows(g)))
        def _():
            remote(sweep_buf.at[g], out_ref.at[here], send_out.at[g], recv_out.at[out_block], (owner, g)).wait_send()

    for b in range(4):
        @pl.when(jnp.logical_not(is_me(b)))
        def _():
            for src, dst, kind in small_pairs(b):
                remote(src, dst, send_small.at[b, kind], recv_small.at[y, kind], target_of(b)).wait_send()

    def finish_chunk(q, carry):
        for b in range(4):
            @pl.when(jnp.logical_not(is_me(b)))
            def _():
                for src, dst, kind in big_pairs(b, q):
                    remote(src, dst, send_in.at[b, kind, q], recv_in.at[y, kind, q], target_of(b)).wait_send()
        return carry

    lax.fori_loop(0, NCHUNK, finish_chunk, 0)

    @pl.when(holds)
    def _():
        for mine, others, dst, kind in obs_arrays:
            remote(others, dst, send_obs.at[kind], recv_obs.at[kind], sibling).wait_send()

    map_copy.wait_send()
    q_copy.wait_send()

    @pl.when(merges & (y == 0))
    def _():
        chunks(lambda k: chip_before_copy(k).wait_send())
        vec_copies[0].wait_send()

    @pl.when(merges & (y == 1))
    def _():
        chunks(lambda k: first_copy(k).wait_send())
        first_before_copy.wait_send()
        vec_copies[2].wait_send()
        vec_copies[3].wait_send()

    @pl.when(merges & (y == 2))
    def _():
        chunks(lambda k: chip_left_copy(k).wait_send())
        vec_copies[1].wait_send()

    @pl.when(shares_chip)
    def _():
        share(chip, 0).wait_send()

    @pl.when(first_column)
    def _():
        @pl.when(y < 3)
        def _():
            along_copy.wait_send()

        @pl.when(y == 3)
        def _():
            for j in range(4):
                next_copy(j).wait_send()

    @pl.when(merges & (y > 0))
    def _():
        share(before, 1).wait_send()

    @pl.when(merges & (y == 3))
    def _():
        share(last, 2).wait_send()
        share(left, 3).wait_send()

    @pl.when(is_mate)
    def _():
        chunks(lambda k: mate_copy(k).wait_send())
        vec_copies[4].wait_send()

    @pl.when(jnp.logical_or(is_master, single_master))
    def _():
        share(whole, 4).wait_send()
        for j in range(4):
            next_copy(j).wait_send()

    @pl.when(is_master)
    def _():
        chunks(lambda k: mate_on(k, 0).wait_send())
        for j in range(3):
            second_copy(j).wait_send()

    @pl.when(end_master)
    def _():
        chunks(lambda k: mate_on(k, 1).wait_send())
        for j in range(4):
            end_copy(j).wait_send()

    @pl.when(odd_master)
    def _():
        second_copy(3).wait_send()

    @pl.when(sends_pair)
    def _():
        next_pair_copy().wait_send()


def body(dyn_cols, dyn_vals, obs_blocks, obs_op, obs_counts, obs_values, gain, sources, prior):
    count = dyn_vals.shape[0]
    columns_count = lax.axis_size("tm") // 2
    cols = jnp.transpose(dyn_cols, (2, 1, 0))
    blocks = jnp.transpose(obs_blocks, (1, 0))
    counts = obs_counts.reshape(1, count)
    prior_rows = prior.reshape(4, 128)
    vmem = pl.BlockSpec(memory_space=pltpu.VMEM)
    hbm = pl.BlockSpec(memory_space=pl.ANY)
    dma = pltpu.SemaphoreType.DMA
    a_map = (2, 2, NS, HALF)
    packed_map = (8, NS, 128)

    def call(*refs):
        kernel(columns_count, *refs)

    return pl.pallas_call(
        call,
        out_shape=jax.ShapeDtypeStruct((count, 128), F32),
        in_specs=[hbm] * 9,
        out_specs=vmem,
        scratch_shapes=[
            pltpu.VMEM((count, 2, 64, 64), BF16),
            pltpu.VMEM((count, 64, 128), BF16),
            pltpu.VMEM((4, STEPS, 2, 64, 128), BF16),
            pltpu.VMEM((4, STEPS, 64, 128), BF16),
            pltpu.VMEM((4, STEPS, 128, 128), BF16),
            pltpu.VMEM((4, STEPS, 128), F32),
            pltpu.VMEM((4, *cols.shape), jnp.int32),
            pltpu.VMEM(blocks.shape, jnp.int32),
            pltpu.VMEM(counts.shape, jnp.int32),
            pltpu.SMEM((4, *cols.shape), jnp.int32),
            pltpu.SMEM(blocks.shape, jnp.int32),
            pltpu.SMEM(counts.shape, jnp.int32),
            pltpu.VMEM((STEPS, 64, 128), BF16),
            pltpu.VMEM((STEPS, 128), F32),
            pltpu.VMEM((8, 64, NS), F32),
            pltpu.VMEM((8, 64, NS), BF16),
            pltpu.VMEM((STEPS, NS, NS), BF16),
            pltpu.VMEM((STEPS, 4, 128), F32),
            pltpu.VMEM((2, *a_map), BF16),
            pltpu.VMEM((2, 4, 128), F32),
            pltpu.VMEM(packed_map, BF16),
            pltpu.VMEM((4, 128), F32),
            pltpu.VMEM(packed_map, BF16),
            pltpu.VMEM((4, 128), F32),
            pltpu.VMEM(packed_map, BF16),
            pltpu.VMEM((4, 128), F32),
            pltpu.VMEM((4, NS, 128), BF16),
            pltpu.VMEM((4, 128), F32),
            pltpu.VMEM(packed_map, BF16),
            pltpu.VMEM(packed_map, BF16),
            pltpu.VMEM((4, 128), F32),
            pltpu.VMEM((2, *packed_map), BF16),
            pltpu.VMEM((2, 4, 128), F32),
            pltpu.VMEM((NS, NS), F32),
            pltpu.VMEM((NS, NS), F32),
            pltpu.VMEM((NS, NS), F32),
            pltpu.VMEM((NS, NS), F32),
            pltpu.VMEM((NS, NS), F32),
            pltpu.VMEM((4, 128), F32),
            pltpu.VMEM((4, 128), F32),
            pltpu.VMEM((4, 128), F32),
            pltpu.VMEM((4, 128), F32),
            pltpu.VMEM((4, 128), F32),
            pltpu.VMEM((4, 128), F32),
            pltpu.VMEM((4, STEPS, 128), F32),
            dma((4, 3, NCHUNK)), dma((4, 3, NCHUNK)),
            dma((4, 2)), dma((4, 2)),
            dma((4,)), dma((4,)), dma((3,)),
            dma((2,)), dma((2,)), dma((5,)), dma((5,)), dma((4,)), dma((4,)), dma((4,)), dma((4,)),
            dma((4,)), dma((2, 4)), dma((5,)), dma((5,)), dma((5,)), dma((5,)), dma((2, 4)), dma((2, 4)),
            dma((9,)), dma, dma, dma((4,)), dma((4,)), dma, dma((4,)), dma,
        ],
        compiler_params=pltpu.CompilerParams(
            collective_id=0, has_side_effects=True, vmem_limit_bytes=58 * 1024 * 1024
        ),
        cost_estimate=pl.CostEstimate(flops=10_000_000_000, bytes_accessed=4_000_000, transcendentals=0),
    )(dyn_vals, gain, obs_op, cols, blocks, counts, obs_values, sources, prior_rows)


def solution(mesh):
    return jax.shard_map(
        body,
        mesh=mesh,
        in_specs=(
            P("tm", "state", None),
            P("tm", "state", None, None),
            P("tm", None),
            P("tm", None, None),
            P("tm"),
            P("tm", None),
            P("tm", "state", None),
            P("tm", "state"),
            P(),
        ),
        out_specs=P("tm", "state"),
        check_vma=False,
    )
```

```python
import jax
import jax.numpy as jnp
from jax import lax
from jax.experimental import pallas as pl
from jax.experimental.pallas import tpu as pltpu
from jax.sharding import PartitionSpec as P

MESH = pl.DeviceIdType.MESH
F32 = jnp.float32
BF16 = jnp.bfloat16
NS = 512
HALF = 256
STEPS = 8
CHUNK = 2
NCHUNK = STEPS // CHUNK


def split(value):
    high = value.astype(BF16)
    low = (value - high.astype(F32)).astype(BF16)
    return high, low


def column_to_row(column):
    rows = lax.broadcasted_iota(jnp.int32, (128, 128), 0)
    lanes = lax.broadcasted_iota(jnp.int32, (128, 128), 1)
    return jnp.sum(jnp.where(rows == lanes, column, 0.0), axis=0, keepdims=True)


def matvec(load, vector):
    out = []
    for g in range(4):
        total = load(g, 0) * vector[0]
        for j in range(1, 4):
            total = total + load(g, j) * vector[j]
        out.append(column_to_row(jnp.sum(total, axis=1, keepdims=True)))
    return out


def rows_of(ref):
    return [ref[g : g + 1, :] for g in range(4)]


def put_rows(ref, rows):
    for g in range(4):
        ref[g : g + 1, :] = rows[g]


def block_of_plain(ref):
    def load(g, j):
        return ref[pl.ds(g * 128, 128), pl.ds(j * 128, 128)].astype(F32)

    return load


def product(left, right):
    total = None
    for h in range(2):
        rows = pl.ds(h * HALF, HALF)
        for a, b in ((0, 0), (0, 1), (1, 0)):
            term = jnp.dot(left[h, a], right[b, rows, :], preferred_element_type=F32)
            total = term if total is None else total + term
    return total


def half_map(maps_ref, out):
    for h in range(2):
        out[:, h * HALF : (h + 1) * HALF] = maps_ref[h, 0].astype(F32) + maps_ref[h, 1].astype(F32)


def left_lanes(shape):
    return lax.broadcasted_iota(jnp.int32, shape, 1) < 64


def pack_chunk(doubled):
    low = doubled - doubled.astype(BF16).astype(F32)
    return jnp.where(left_lanes(doubled.shape), doubled, low).astype(BF16)


def pack_pair(pair):
    turned = pltpu.roll(pair, 64, 1)
    left = left_lanes(pair.shape)
    return pack_chunk(jnp.where(left, pair, turned)), pack_chunk(jnp.where(left, turned, pair))


def chunk_product(left, right):
    rows = right.reshape(8, 64, 128)
    rows = jnp.concatenate([rows, rows], axis=1).reshape(2 * NS, 128)
    lanes = jnp.concatenate([left[n] for n in range(8)], axis=1)
    parts = jnp.dot(lanes, rows, preferred_element_type=F32)
    return pack_chunk(parts + pltpu.roll(parts, 64, 1))


def to_plain(packed, out):
    for n in range(4):
        first, second = packed[2 * n].astype(F32), packed[2 * n + 1].astype(F32)
        first, second = first + pltpu.roll(first, 64, 1), second + pltpu.roll(second, 64, 1)
        out[:, n * 128 : (n + 1) * 128] = jnp.where(left_lanes(first.shape), first, second)


def packed_matvec(packed, vector):
    doubled = []
    for row in vector:
        doubled.append(jnp.concatenate([row[:, :64], row[:, :64]], axis=1))
        doubled.append(jnp.concatenate([row[:, 64:], row[:, 64:]], axis=1))
    out = []
    for g in range(4):
        total = None
        for n in range(8):
            term = packed[n, pl.ds(g * 128, 128), :].astype(F32) * doubled[n]
            total = term if total is None else total + term
        out.append(column_to_row(jnp.sum(total, axis=1, keepdims=True)))
    return out


def sum_rows(a, b):
    return [m + o for m, o in zip(a, b)]


def kernel(
    columns_count,
    vals_ref, gain_ref, obs_op_ref, cols_ref, blocks_ref, counts_ref, obs_values_ref, sources_ref, prior_ref,
    out_ref,
    third, packed, a_buf, b_buf, gain_buf, src_buf, cols_buf, blocks_buf, counts_buf,
    cols_smem, blocks_smem, counts_smem, op_buf, ov_buf,
    f_buf, fn_buf, e_buf, off_buf,
    maps, maps_q, chip, chip_q, before, before_q, left, left_q, first, first_q, last, whole, whole_q,
    mate, mate_q, plain_a, plain_b, plain_c, plain_d, plain_e, x_in, x_pair, x_mid, x_out, x_end, x_work, sweep_buf,
    send_in, recv_in, send_small, recv_small, send_obs, recv_obs, smem_sem,
    send_map, recv_map, send_before, recv_before, send_left, recv_left, send_first, recv_first,
    send_mate, recv_mate, send_vec, recv_vec, send_share, recv_share, send_on, recv_on,
    send_x, recv_x, recv_pair, send_out, recv_out, third_sem, send_end, prior_sem,
):
    tm, y = lax.axis_index("tm"), lax.axis_index("state")
    core = lax.rem(tm, 2)
    column = tm // 2
    first_tm = tm - core
    other = 1 - core
    sibling = (first_tm + other, y)
    groups = (columns_count - 4) // 3
    single = column < 4
    grouped = jnp.logical_not(single)
    group = (column - 4) // 3
    place = column - 4 - 3 * group
    last_group = group == groups - 1

    def device(c, j):
        return 2 * c + core, j

    first_column = column == 0
    merges = column > 0
    at_last_chip = jnp.logical_and(y == 3, grouped)
    single_master = jnp.logical_and(y == 3, jnp.logical_and(single, merges))
    exits_first = jnp.logical_and(first_column, y == 3)
    is_master = jnp.logical_and(at_last_chip, place == 1)
    long_master = jnp.logical_and(is_master, jnp.logical_not(last_group))
    is_mate = jnp.logical_and(
        at_last_chip, jnp.logical_or(place == 0, jnp.logical_and(place == 2, jnp.logical_not(last_group)))
    )
    mate_slot = jnp.where(place == 2, 1, 0)
    partner = device(5 + 3 * group, 3)

    barrier = pltpu.get_barrier_semaphore()

    def greet(where):
        pl.semaphore_signal(barrier, inc=1, device_id=where, device_id_type=MESH)

    for c in range(2):
        for j in range(4):
            @pl.when(jnp.logical_or(c != core, j != y))
            def _():
                greet((first_tm + c, j))

    third_copy = pltpu.make_async_copy(vals_ref.at[:, :, :, pl.ds(128, 64)], third, third_sem)
    third_copy.start()
    prior_copy = pltpu.make_async_copy(prior_ref, x_in, prior_sem)
    starts = jnp.logical_and(column == 0, y == 0)

    @pl.when(starts)
    def _():
        prior_copy.start()


    from_before = jnp.logical_or(
        jnp.logical_and(column > 0, column <= 4), jnp.logical_and(grouped, place == 2)
    )
    from_earlier = jnp.logical_and(grouped, jnp.logical_and(place == 0, group > 0))
    earlier = device(jnp.where(group == 0, 3, 2 + 3 * group), 3)

    @pl.when(from_before)
    def _():
        greet(device(column - 1, 3))

    @pl.when(jnp.logical_or(from_earlier, is_master))
    def _():
        greet(earlier)

    @pl.when(is_master)
    def _():
        greet(device(column - 1, 3))

    @pl.when(long_master)
    def _():
        greet(device(column + 1, 3))

    last_single = jnp.logical_and(single_master, column == 3)
    peers = (
        7
        + jnp.where(jnp.logical_or(exits_first, jnp.logical_or(single_master, is_master)), 4, 0)
        + jnp.where(is_mate, 1, 0)
        + jnp.where(last_single, 1, 0)
        + jnp.where(long_master, 5, 0)
    )
    pl.semaphore_wait(barrier, peers)

    def target_of(b):
        return first_tm + b % 2, 2 * core + b // 2

    def is_me(b):
        dest_tm, dest_y = target_of(b)
        return jnp.logical_and(dest_tm == tm, dest_y == y)

    def remote(src, dst, send, recv, device):
        return pltpu.make_async_remote_copy(
            src_ref=src, dst_ref=dst, send_sem=send, recv_sem=recv, device_id=device, device_id_type=MESH
        )

    def small_pairs(b):
        start = pl.ds(8 * b, STEPS)
        return (
            (sources_ref.at[start], src_buf.at[y], 0),
            (cols_ref, cols_buf.at[y], 1),
        )

    def big_pairs(b, q):
        start, there = pl.ds(8 * b + CHUNK * q, CHUNK), pl.ds(CHUNK * q, CHUNK)
        return (
            (vals_ref.at[start, :, :, pl.ds(0, 128)], a_buf.at[y, there], 0),
            (packed.at[start], b_buf.at[y, there], 1),
            (gain_ref.at[start], gain_buf.at[y, there], 2),
        )

    def send_pair(b, src, dst, send, recv):
        @pl.when(jnp.logical_not(is_me(b)))
        def _():
            remote(src, dst, send, recv, target_of(b)).start()

        @pl.when(is_me(b))
        def _():
            pltpu.make_async_copy(src, dst, recv).start()

    for b in range(4):
        for src, dst, kind in small_pairs(b):
            send_pair(b, src, dst, send_small.at[b, kind], recv_small.at[y, kind])

    holds = core == y // 2
    first_step = 16 * lax.rem(y, 2) + 8 * core
    mine_at = pl.ds(first_step, STEPS)
    other_at = pl.ds(16 * lax.rem(y, 2) + 8 * other, STEPS)
    obs_arrays = (
        (obs_op_ref.at[mine_at], obs_op_ref.at[other_at], op_buf, 0),
        (obs_values_ref.at[mine_at], obs_values_ref.at[other_at], ov_buf, 1),
        (blocks_ref, blocks_ref, blocks_buf, 2),
        (counts_ref, counts_ref, counts_buf, 3),
    )

    @pl.when(holds)
    def _():
        for mine, others, dst, kind in obs_arrays:
            remote(others, dst, send_obs.at[kind], recv_obs.at[kind], sibling).start()
            pltpu.make_async_copy(mine, dst, recv_obs.at[kind]).start()

    def start_chunk(q, carry):
        for b in range(4):
            for src, dst, kind in big_pairs(b, q)[:1]:
                send_pair(b, src, dst, send_in.at[b, kind, q], recv_in.at[y, kind, q])

        @pl.when(q == 0)
        def _():
            third_copy.wait()

        for b in range(4):
            for t in range(CHUNK):
                at = 8 * b + CHUNK * q + t
                packed[at] = jnp.concatenate([third[at, 0], third[at, 1]], axis=1)
        for k in (1, 2):
            for b in range(4):
                src, dst, kind = big_pairs(b, q)[k]
                send_pair(b, src, dst, send_in.at[b, kind, q], recv_in.at[y, kind, q])
        return carry

    lax.fori_loop(0, NCHUNK, start_chunk, 0)

    def arrived(dst, sem):
        pltpu.make_async_copy(dst, dst, sem).wait()

    for j in range(4):
        arrived(src_buf.at[j], recv_small.at[j, 0])
        arrived(cols_buf.at[j], recv_small.at[j, 1])
    for _, _, dst, kind in obs_arrays:
        arrived(dst, recv_obs.at[kind])
    to_smem = [
        pltpu.make_async_copy(src, dst, smem_sem.at[k])
        for k, (src, dst) in enumerate(((cols_buf, cols_smem), (blocks_buf, blocks_smem), (counts_buf, counts_smem)))
    ]
    for copy in to_smem:
        copy.start()
    for copy in to_smem:
        copy.wait()

    lane64 = lax.broadcasted_iota(jnp.int32, (64, 128), 1)
    row64 = lax.broadcasted_iota(jnp.int32, (64, 128), 0)
    left64 = lane64 < 64
    half64 = lane64 // 64
    lane1 = lax.broadcasted_iota(jnp.int32, (1, 128), 1)

    maps_q[core] = jnp.zeros((4, 128), F32)

    def step(s, carry):
        at = first_step + s

        @pl.when(lax.rem(s, CHUNK) == 0)
        def _():
            q = s // CHUNK
            there = pl.ds(CHUNK * q, CHUNK)
            for j in range(4):
                arrived(a_buf.at[j, there], recv_in.at[j, 0, q])
                arrived(b_buf.at[j, there], recv_in.at[j, 1, q])

        for j in range(4):
            thirds = b_buf[j, s].astype(F32)
            thirds_turned = pltpu.roll(thirds, 64, 1)
            for il in range(2):
                i = 2 * j + il
                pair = a_buf[j, s, il].astype(F32)
                turned = pltpu.roll(pair, 64, 1)
                block0 = jnp.where(left64, pair, turned)
                block1 = jnp.where(left64, turned, pair)
                block2 = jnp.where(left64 if il == 0 else jnp.logical_not(left64), thirds, thirds_turned)
                col1 = cols_smem[j, 1, il, at]
                col2 = cols_smem[j, 2, il, at]
                for p in range(4):
                    index = half64 + 2 * p
                    value = jnp.where(index == col1, block1, jnp.where(index == col2, block2, 0.0))
                    if p == j:
                        value = jnp.where(half64 == il, block0, value)
                    f_buf[i, :, p * 128 : (p + 1) * 128] = value
                    fn_buf[i, :, p * 128 : (p + 1) * 128] = value.astype(BF16)

        operator = op_buf[s].astype(F32)
        turned_operator = operator.T.astype(BF16)
        count = counts_smem[0, at]
        images, source_columns = [], []
        for o in range(2):
            block = blocks_smem[o, at]
            selected = fn_buf[block]
            images.append(jnp.dot(turned_operator[64 * o : 64 * o + 64], selected, preferred_element_type=F32))
            source_row = src_buf[block // 2, pl.ds(s, 1), :]
            offset = lax.rem(block, 2) * 64
            source_columns.append(
                jnp.sum(jnp.where(lane64 == row64 + offset, source_row, 0.0), axis=1, keepdims=True)
            )
        image = jnp.concatenate(images, axis=0)
        slot = lax.broadcasted_iota(jnp.int32, (128, NS), 0)
        masked = jnp.where(slot < count, image, 0.0).astype(BF16)

        @pl.when(lax.rem(s, CHUNK) == 0)
        def _():
            q = s // CHUNK
            for j in range(4):
                arrived(gain_buf.at[j, pl.ds(CHUNK * q, CHUNK)], recv_in.at[j, 2, q])

        gains = gain_buf[:, s].reshape(NS, 128)
        correction = jnp.dot(gains, masked, preferred_element_type=F32)
        e_buf[s] = (f_buf[...].reshape(NS, NS) - correction).astype(BF16)

        source_image = jnp.sum(
            operator * jnp.where(left64, source_columns[0], source_columns[1]), axis=0, keepdims=True
        )
        source_image = source_image.astype(BF16).astype(F32)
        innovation = jnp.where(lane1 < count, ov_buf[pl.ds(s, 1), :] - source_image, 0.0)
        offsets = []
        for g in range(4):
            moved = jnp.sum(gain_buf[g, s].astype(F32) * innovation, axis=1, keepdims=True)
            offsets.append(column_to_row(moved) + src_buf[g, pl.ds(s, 1), :])
        put_rows(off_buf.at[s], offsets)

        moved = matvec(block_of_plain(e_buf.at[s]), rows_of(maps_q.at[core]))
        put_rows(maps_q.at[core], [m + o for m, o in zip(moved, offsets)])

        @pl.when(s == 0)
        def _():
            for h in range(2):
                maps[core, h, 0] = e_buf[s, :, h * HALF : (h + 1) * HALF]
                maps[core, h, 1] = jnp.zeros((NS, HALF), BF16)

        @pl.when(s > 0)
        def _():
            for h in range(2):
                matrix = e_buf[s]
                value = jnp.dot(matrix, maps[core, h, 0], preferred_element_type=F32)
                value = value + jnp.dot(matrix, maps[core, h, 1], preferred_element_type=F32)
                maps[core, h, 0], maps[core, h, 1] = split(value)

        return carry

    lax.fori_loop(0, STEPS, step, 0)

    map_copy = remote(maps.at[core], maps.at[core], send_map.at[0], recv_map.at[0], sibling)
    q_copy = remote(maps_q.at[core], maps_q.at[core], send_map.at[1], recv_map.at[1], sibling)
    map_copy.start()
    q_copy.start()
    arrived(maps_q.at[other], recv_map.at[1])
    arrived(maps.at[other], recv_map.at[0])
    mine = pl.ds(4 * core, 4)
    theirs = pl.ds(4 * other, 4)

    def to_chip(j):
        return tm, j

    def share(ref, k):
        return remote(ref.at[mine], ref.at[mine], send_share.at[k], recv_share.at[k], sibling)

    def shared(ref, k):
        arrived(ref.at[theirs], recv_share.at[k])

    def chip_before_copy(k):
        n = 4 * core + k
        return remote(chip.at[n], before.at[n], send_before.at[k], recv_before.at[k], to_chip(1))

    def chip_left_copy(k):
        n = 4 * core + k
        return remote(chip.at[n], left.at[n], send_left.at[k], recv_left.at[k], to_chip(3))

    def first_copy(k):
        return remote(first.at[k], first.at[k], send_first.at[k], recv_first.at[k], to_chip(3))

    first_before_copy = remote(first, before.at[mine], send_before.at[4], recv_before.at[4], to_chip(2))

    def mate_copy(k):
        n = 4 * core + k
        return remote(whole.at[n], mate.at[mate_slot, n], send_mate.at[k], recv_mate.at[mate_slot, k], partner)

    def mate_on(k, slot):
        n = 4 * core + k
        return remote(mate.at[slot, n], mate.at[slot, n], send_on.at[slot, k], recv_on.at[slot, k], sibling)

    vec_copies = (
        remote(chip_q, before_q, send_vec.at[0], recv_vec.at[0], to_chip(1)),
        remote(chip_q, left_q, send_vec.at[1], recv_vec.at[1], to_chip(3)),
        remote(first_q, first_q, send_vec.at[2], recv_vec.at[2], to_chip(3)),
        remote(first_q, before_q, send_vec.at[3], recv_vec.at[0], to_chip(2)),
        remote(whole_q, mate_q.at[mate_slot], send_vec.at[4], recv_vec.at[3 + mate_slot], partner),
    )

    def chunks(step):
        def one(k, carry):
            step(k)
            return carry

        lax.fori_loop(0, 4, one, 0)

    for h in range(2):
        total = product(maps.at[1], maps.at[0, core, :, :, pl.ds(128 * h, 128)])
        chip[4 * core + 2 * h], chip[4 * core + 2 * h + 1] = pack_pair(total)
        for k in (2 * h, 2 * h + 1):
            @pl.when(jnp.logical_and(merges, y == 0))
            def _():
                chip_before_copy(k).start()

            @pl.when(jnp.logical_and(merges, y == 2))
            def _():
                chip_left_copy(k).start()

    shares_chip = jnp.logical_or(first_column, lax.rem(y, 2) == 1)

    @pl.when(shares_chip)
    def _():
        share(chip, 0).start()

    half_map(maps.at[0], plain_c)
    half_map(maps.at[1], plain_b)
    moved = matvec(block_of_plain(plain_b), rows_of(maps_q.at[0]))
    put_rows(chip_q, sum_rows(moved, rows_of(maps_q.at[1])))

    @pl.when(merges & (y == 0))
    def _():
        vec_copies[0].start()

    @pl.when(merges & (y == 2))
    def _():
        vec_copies[1].start()

    @pl.when(shares_chip)
    def _():
        shared(chip, 0)

    def entry():
        @pl.when(jnp.logical_or(from_before, from_earlier))
        def _():
            arrived(x_in, recv_x)

    def apply(plain, vector, shift, out):
        moved = matvec(block_of_plain(plain), rows_of(vector))
        put_rows(out, [m + o for m, o in zip(moved, rows_of(shift))])

    def pair_copy(source, there):
        return remote(source, x_pair, send_x.at[8], recv_pair, device(there, 3))

    def next_copy(j):
        return remote(x_out, x_in, send_x.at[j], recv_x, device(column + 1, j))

    def middle_copy(j):
        return remote(x_mid, x_in, send_x.at[4 + j], recv_x, device(column, j))

    def end_copy(j):
        return remote(x_end, x_in, send_end.at[j], recv_x, device(column + 2, j))

    along_copy = remote(x_out, x_in, send_end.at[0], recv_x, to_chip(lax.rem(y + 1, 4)))

    @pl.when(first_column)
    def _():
        @pl.when(y == 0)
        def _():
            prior_copy.wait()

        @pl.when(y > 0)
        def _():
            arrived(x_in, recv_x)

        put_rows(x_out, sum_rows(packed_matvec(chip, rows_of(x_in)), rows_of(chip_q)))

        @pl.when(y < 3)
        def _():
            along_copy.start()

        @pl.when(y == 3)
        def _():
            for j in (3, 2, 1, 0):
                next_copy(j).start()

    @pl.when(merges & (y == 1))
    def _():
        def one(k):
            n = 4 * core + k
            arrived(before.at[n], recv_before.at[k])
            first[k] = chunk_product(chip, before[n])
            first_copy(k).start()

        chunks(one)
        first_before_copy.start()
        share(before, 1).start()
        arrived(before_q, recv_vec.at[0])
        put_rows(first_q, sum_rows(packed_matvec(chip, rows_of(before_q)), rows_of(chip_q)))
        vec_copies[2].start()
        vec_copies[3].start()

    @pl.when(merges & (y == 2))
    def _():
        arrived(before.at[mine], recv_before.at[4])
        share(before, 1).start()
        arrived(before_q, recv_vec.at[0])

    @pl.when(merges & (y == 3))
    def _():
        def one_last(k):
            n = 4 * core + k
            arrived(left.at[n], recv_left.at[k])
            last[n] = chunk_product(chip, left[n])

        chunks(one_last)
        share(last, 2).start()
        share(left, 3).start()
        arrived(left_q, recv_vec.at[1])
        put_rows(whole_q, sum_rows(packed_matvec(chip, rows_of(left_q)), rows_of(chip_q)))
        shared(last, 2)

        def one_whole(k):
            n = 4 * core + k
            arrived(first.at[k], recv_first.at[k])
            whole[n] = chunk_product(last, first[k])

            @pl.when(is_mate)
            def _():
                mate_copy(k).start()

        chunks(one_whole)

        @pl.when(jnp.logical_or(is_master, single_master))
        def _():
            share(whole, 4).start()

        arrived(first_q, recv_vec.at[2])
        put_rows(whole_q, sum_rows(packed_matvec(last, rows_of(first_q)), rows_of(whole_q)))

        @pl.when(is_mate)
        def _():
            vec_copies[4].start()

    @pl.when(single_master)
    def _():
        shared(whole, 4)
        to_plain(whole, plain_a)
        entry()
        apply(plain_a, x_in, whole_q, x_out)

        @pl.when(last_single)
        def _():
            pair_copy(x_out, 5).start()

        for j in (3, 2, 1, 0):
            next_copy(j).start()

    @pl.when(merges & (y == 3))
    def _():
        shared(left, 3)

        def one_before(k):
            before[4 * core + k] = chunk_product(left, first[k])

        chunks(one_before)
        share(before, 1).start()
        put_rows(before_q, sum_rows(packed_matvec(left, rows_of(first_q)), rows_of(left_q)))

    @pl.when(is_master)
    def _():
        shared(whole, 4)
        to_plain(whole, plain_a)

        def one_mate(slot):
            def one(k):
                arrived(mate.at[slot, 4 * core + k], recv_mate.at[slot, k])
                mate_on(k, slot).start()

            chunks(one)

        one_mate(0)

        @pl.when(long_master)
        def _():
            one_mate(1)

    @pl.when(merges & (y > 0))
    def _():
        shared(before, 1)
        to_plain(before, plain_b)

    def take_mate(slot, plain):
        arrived(mate_q.at[slot], recv_vec.at[3 + slot])
        for k in range(4):
            arrived(mate.at[slot, 4 * other + k], recv_on.at[slot, k])
        to_plain(mate.at[slot], plain)

    @pl.when(jnp.logical_not(single_master))
    def _():
        @pl.when(is_master)
        def _():
            take_mate(0, plain_d)

            @pl.when(long_master)
            def _():
                take_mate(1, plain_e)

        entry()

    @pl.when(is_master)
    def _():
        arrived(x_pair, recv_pair)
        apply(plain_d, x_pair, mate_q.at[0], x_mid)
        apply(plain_a, x_mid, whole_q, x_out)

        @pl.when(long_master)
        def _():
            apply(plain_e, x_out, mate_q.at[1], x_end)
            pair_copy(x_end, column + 3).start()
            for j in range(4):
                end_copy(j).start()

        for j in range(4):
            next_copy(j).start()
        for j in range(3):
            middle_copy(j).start()
        x_in[...] = x_mid[...]

    @pl.when(jnp.logical_and(grouped, jnp.logical_and(place == 1, y < 3)))
    def _():
        arrived(x_in, recv_x)

    enters = jnp.logical_or(first_column, y == 0)

    @pl.when(enters)
    def _():
        x_work[...] = x_in[...]

    @pl.when(jnp.logical_not(enters))
    def _():
        moved = matvec(block_of_plain(plain_b), rows_of(x_in))
        put_rows(x_work, [m + o for m, o in zip(moved, rows_of(before_q))])

    @pl.when(core == 1)
    def _():
        moved = matvec(block_of_plain(plain_c), rows_of(x_work))
        put_rows(x_work, [m + o for m, o in zip(moved, rows_of(maps_q.at[0]))])

    def sweep(s, carry):
        moved = matvec(block_of_plain(e_buf.at[s]), list(carry))
        rows = [m + o for m, o in zip(moved, rows_of(off_buf.at[s]))]
        for g in range(4):
            sweep_buf[g, pl.ds(s, 1), :] = rows[g]
        return tuple(rows)

    lax.fori_loop(0, STEPS, sweep, tuple(rows_of(x_work)))

    owner = first_tm + y // 2
    out_block = 2 * lax.rem(y, 2) + core
    here = pl.ds(8 * out_block, STEPS)

    def own_rows(g):
        return jnp.logical_and(owner == tm, g == y)

    for g in range(4):
        src, dst = sweep_buf.at[g], out_ref.at[here]

        @pl.when(jnp.logical_not(own_rows(g)))
        def _():
            remote(src, dst, send_out.at[g], recv_out.at[out_block], (owner, g)).start()

        @pl.when(own_rows(g))
        def _():
            pltpu.make_async_copy(src, dst, recv_out.at[out_block]).start()

    for b in range(4):
        arrived(out_ref.at[pl.ds(8 * b, STEPS)], recv_out.at[b])

    for g in range(4):
        @pl.when(jnp.logical_not(own_rows(g)))
        def _():
            remote(sweep_buf.at[g], out_ref.at[here], send_out.at[g], recv_out.at[out_block], (owner, g)).wait_send()

    for b in range(4):
        @pl.when(jnp.logical_not(is_me(b)))
        def _():
            for src, dst, kind in small_pairs(b):
                remote(src, dst, send_small.at[b, kind], recv_small.at[y, kind], target_of(b)).wait_send()

    def finish_chunk(q, carry):
        for b in range(4):
            @pl.when(jnp.logical_not(is_me(b)))
            def _():
                for src, dst, kind in big_pairs(b, q):
                    remote(src, dst, send_in.at[b, kind, q], recv_in.at[y, kind, q], target_of(b)).wait_send()
        return carry

    lax.fori_loop(0, NCHUNK, finish_chunk, 0)

    @pl.when(holds)
    def _():
        for mine, others, dst, kind in obs_arrays:
            remote(others, dst, send_obs.at[kind], recv_obs.at[kind], sibling).wait_send()

    map_copy.wait_send()
    q_copy.wait_send()

    @pl.when(merges & (y == 0))
    def _():
        chunks(lambda k: chip_before_copy(k).wait_send())
        vec_copies[0].wait_send()

    @pl.when(merges & (y == 1))
    def _():
        chunks(lambda k: first_copy(k).wait_send())
        first_before_copy.wait_send()
        vec_copies[2].wait_send()
        vec_copies[3].wait_send()

    @pl.when(merges & (y == 2))
    def _():
        chunks(lambda k: chip_left_copy(k).wait_send())
        vec_copies[1].wait_send()

    @pl.when(shares_chip)
    def _():
        share(chip, 0).wait_send()

    @pl.when(first_column)
    def _():
        @pl.when(y < 3)
        def _():
            along_copy.wait_send()

        @pl.when(y == 3)
        def _():
            for j in range(4):
                next_copy(j).wait_send()

    @pl.when(merges & (y > 0))
    def _():
        share(before, 1).wait_send()

    @pl.when(merges & (y == 3))
    def _():
        share(last, 2).wait_send()
        share(left, 3).wait_send()

    @pl.when(is_mate)
    def _():
        chunks(lambda k: mate_copy(k).wait_send())
        vec_copies[4].wait_send()

    @pl.when(jnp.logical_or(is_master, single_master))
    def _():
        share(whole, 4).wait_send()
        for j in range(4):
            next_copy(j).wait_send()

    @pl.when(is_master)
    def _():
        chunks(lambda k: mate_on(k, 0).wait_send())
        for j in range(3):
            middle_copy(j).wait_send()

    @pl.when(long_master)
    def _():
        chunks(lambda k: mate_on(k, 1).wait_send())
        for j in range(4):
            end_copy(j).wait_send()
        pair_copy(x_end, column + 3).wait_send()

    @pl.when(last_single)
    def _():
        pair_copy(x_out, 5).wait_send()


def body(dyn_cols, dyn_vals, obs_blocks, obs_op, obs_counts, obs_values, gain, sources, prior):
    count = dyn_vals.shape[0]
    columns_count = lax.axis_size("tm") // 2
    cols = jnp.transpose(dyn_cols, (2, 1, 0))
    blocks = jnp.transpose(obs_blocks, (1, 0))
    counts = obs_counts.reshape(1, count)
    prior_rows = prior.reshape(4, 128)
    vmem = pl.BlockSpec(memory_space=pltpu.VMEM)
    hbm = pl.BlockSpec(memory_space=pl.ANY)
    dma = pltpu.SemaphoreType.DMA
    a_map = (2, 2, NS, HALF)
    packed_map = (8, NS, 128)

    def call(*refs):
        kernel(columns_count, *refs)

    return pl.pallas_call(
        call,
        out_shape=jax.ShapeDtypeStruct((count, 128), F32),
        in_specs=[hbm] * 9,
        out_specs=vmem,
        scratch_shapes=[
            pltpu.VMEM((count, 2, 64, 64), BF16),
            pltpu.VMEM((count, 64, 128), BF16),
            pltpu.VMEM((4, STEPS, 2, 64, 128), BF16),
            pltpu.VMEM((4, STEPS, 64, 128), BF16),
            pltpu.VMEM((4, STEPS, 128, 128), BF16),
            pltpu.VMEM((4, STEPS, 128), F32),
            pltpu.VMEM((4, *cols.shape), jnp.int32),
            pltpu.VMEM(blocks.shape, jnp.int32),
            pltpu.VMEM(counts.shape, jnp.int32),
            pltpu.SMEM((4, *cols.shape), jnp.int32),
            pltpu.SMEM(blocks.shape, jnp.int32),
            pltpu.SMEM(counts.shape, jnp.int32),
            pltpu.VMEM((STEPS, 64, 128), BF16),
            pltpu.VMEM((STEPS, 128), F32),
            pltpu.VMEM((8, 64, NS), F32),
            pltpu.VMEM((8, 64, NS), BF16),
            pltpu.VMEM((STEPS, NS, NS), BF16),
            pltpu.VMEM((STEPS, 4, 128), F32),
            pltpu.VMEM((2, *a_map), BF16),
            pltpu.VMEM((2, 4, 128), F32),
            pltpu.VMEM(packed_map, BF16),
            pltpu.VMEM((4, 128), F32),
            pltpu.VMEM(packed_map, BF16),
            pltpu.VMEM((4, 128), F32),
            pltpu.VMEM(packed_map, BF16),
            pltpu.VMEM((4, 128), F32),
            pltpu.VMEM((4, NS, 128), BF16),
            pltpu.VMEM((4, 128), F32),
            pltpu.VMEM(packed_map, BF16),
            pltpu.VMEM(packed_map, BF16),
            pltpu.VMEM((4, 128), F32),
            pltpu.VMEM((2, *packed_map), BF16),
            pltpu.VMEM((2, 4, 128), F32),
            pltpu.VMEM((NS, NS), F32),
            pltpu.VMEM((NS, NS), F32),
            pltpu.VMEM((NS, NS), F32),
            pltpu.VMEM((NS, NS), F32),
            pltpu.VMEM((NS, NS), F32),
            pltpu.VMEM((4, 128), F32),
            pltpu.VMEM((4, 128), F32),
            pltpu.VMEM((4, 128), F32),
            pltpu.VMEM((4, 128), F32),
            pltpu.VMEM((4, 128), F32),
            pltpu.VMEM((4, 128), F32),
            pltpu.VMEM((4, STEPS, 128), F32),
            dma((4, 3, NCHUNK)), dma((4, 3, NCHUNK)),
            dma((4, 2)), dma((4, 2)),
            dma((4,)), dma((4,)), dma((3,)),
            dma((2,)), dma((2,)), dma((5,)), dma((5,)), dma((4,)), dma((4,)), dma((4,)), dma((4,)),
            dma((4,)), dma((2, 4)), dma((5,)), dma((5,)), dma((5,)), dma((5,)), dma((2, 4)), dma((2, 4)),
            dma((9,)), dma, dma, dma((4,)), dma((4,)), dma, dma((4,)), dma,
        ],
        compiler_params=pltpu.CompilerParams(
            collective_id=0, has_side_effects=True, vmem_limit_bytes=58 * 1024 * 1024
        ),
        cost_estimate=pl.CostEstimate(flops=10_000_000_000, bytes_accessed=4_000_000, transcendentals=0),
    )(dyn_vals, gain, obs_op, cols, blocks, counts, obs_values, sources, prior_rows)


def solution(mesh):
    return jax.shard_map(
        body,
        mesh=mesh,
        in_specs=(
            P("tm", "state", None),
            P("tm", "state", None, None),
            P("tm", None),
            P("tm", None, None),
            P("tm"),
            P("tm", None),
            P("tm", "state", None),
            P("tm", "state"),
            P(),
        ),
        out_specs=P("tm", "state"),
        check_vma=False,
    )
```

```python
import jax
import jax.numpy as jnp
from jax import lax
from jax.experimental import pallas as pl
from jax.experimental.pallas import tpu as pltpu
from jax.sharding import PartitionSpec as P

MESH = pl.DeviceIdType.MESH
F32 = jnp.float32
BF16 = jnp.bfloat16
NS = 512
HALF = 256
STEPS = 8
CHUNK = 1
NCHUNK = STEPS // CHUNK


def split(value):
    high = value.astype(BF16)
    low = (value - high.astype(F32)).astype(BF16)
    return high, low


def column_to_row(column):
    rows = lax.broadcasted_iota(jnp.int32, (128, 128), 0)
    lanes = lax.broadcasted_iota(jnp.int32, (128, 128), 1)
    return jnp.sum(jnp.where(rows == lanes, column, 0.0), axis=0, keepdims=True)


def matvec(load, vector):
    out = []
    for g in range(4):
        total = load(g, 0) * vector[0]
        for j in range(1, 4):
            total = total + load(g, j) * vector[j]
        out.append(column_to_row(jnp.sum(total, axis=1, keepdims=True)))
    return out


def rows_of(ref):
    return [ref[g : g + 1, :] for g in range(4)]


def put_rows(ref, rows):
    for g in range(4):
        ref[g : g + 1, :] = rows[g]


def block_of_plain(ref):
    def load(g, j):
        return ref[pl.ds(g * 128, 128), pl.ds(j * 128, 128)].astype(F32)

    return load


def product(left, right):
    total = None
    for h in range(2):
        rows = pl.ds(h * HALF, HALF)
        for a, b in ((0, 0), (0, 1), (1, 0)):
            term = jnp.dot(left[h, a], right[b, rows, :], preferred_element_type=F32)
            total = term if total is None else total + term
    return total


def half_map(maps_ref, out):
    for h in range(2):
        out[:, h * HALF : (h + 1) * HALF] = maps_ref[h, 0].astype(F32) + maps_ref[h, 1].astype(F32)


def left_lanes(shape):
    return lax.broadcasted_iota(jnp.int32, shape, 1) < 64


def pack_chunk(doubled):
    low = doubled - doubled.astype(BF16).astype(F32)
    return jnp.where(left_lanes(doubled.shape), doubled, low).astype(BF16)


def pack_pair(pair):
    turned = pltpu.roll(pair, 64, 1)
    left = left_lanes(pair.shape)
    return pack_chunk(jnp.where(left, pair, turned)), pack_chunk(jnp.where(left, turned, pair))


def chunk_product(left, right):
    rows = right.reshape(8, 64, 128)
    rows = jnp.concatenate([rows, rows], axis=1).reshape(2 * NS, 128)
    lanes = jnp.concatenate([left[n] for n in range(8)], axis=1)
    parts = jnp.dot(lanes, rows, preferred_element_type=F32)
    return pack_chunk(parts + pltpu.roll(parts, 64, 1))


def to_plain(packed, out):
    for n in range(4):
        first, second = packed[2 * n].astype(F32), packed[2 * n + 1].astype(F32)
        first, second = first + pltpu.roll(first, 64, 1), second + pltpu.roll(second, 64, 1)
        out[:, n * 128 : (n + 1) * 128] = jnp.where(left_lanes(first.shape), first, second)


def packed_matvec(packed, vector):
    doubled = []
    for row in vector:
        doubled.append(jnp.concatenate([row[:, :64], row[:, :64]], axis=1))
        doubled.append(jnp.concatenate([row[:, 64:], row[:, 64:]], axis=1))
    out = []
    for g in range(4):
        total = None
        for n in range(8):
            term = packed[n, pl.ds(g * 128, 128), :].astype(F32) * doubled[n]
            total = term if total is None else total + term
        out.append(column_to_row(jnp.sum(total, axis=1, keepdims=True)))
    return out


def sum_rows(a, b):
    return [m + o for m, o in zip(a, b)]


def kernel(
    columns_count,
    vals_ref, gain_ref, obs_op_ref, cols_ref, blocks_ref, counts_ref, obs_values_ref, sources_ref, prior_ref,
    out_ref,
    third, packed, a_buf, b_buf, gain_buf, src_buf, cols_buf, blocks_buf, counts_buf,
    cols_smem, blocks_smem, counts_smem, op_buf, ov_buf,
    f_buf, fn_buf, e_buf, off_buf,
    maps, maps_q, chip, chip_q, before, before_q, left, left_q, first, first_q, last, whole, whole_q,
    mate, mate_q, plain_a, plain_b, plain_c, plain_d, plain_e, x_in, x_pair, x_mid, x_out, x_end, x_work, sweep_buf,
    send_in, recv_in, send_small, recv_small, send_obs, recv_obs, smem_sem,
    send_map, recv_map, send_before, recv_before, send_left, recv_left, send_first, recv_first,
    send_mate, recv_mate, send_vec, recv_vec, send_share, recv_share, send_on, recv_on,
    send_x, recv_x, recv_pair, send_out, recv_out, third_sem, send_end, prior_sem,
):
    tm, y = lax.axis_index("tm"), lax.axis_index("state")
    core = lax.rem(tm, 2)
    column = tm // 2
    first_tm = tm - core
    other = 1 - core
    sibling = (first_tm + other, y)
    groups = (columns_count - 4) // 3
    single = column < 4
    grouped = jnp.logical_not(single)
    group = (column - 4) // 3
    place = column - 4 - 3 * group
    last_group = group == groups - 1

    def device(c, j):
        return 2 * c + core, j

    first_column = column == 0
    merges = column > 0
    at_last_chip = jnp.logical_and(y == 3, grouped)
    single_master = jnp.logical_and(y == 3, jnp.logical_and(single, merges))
    exits_first = jnp.logical_and(first_column, y == 3)
    is_master = jnp.logical_and(at_last_chip, place == 1)
    long_master = jnp.logical_and(is_master, jnp.logical_not(last_group))
    is_mate = jnp.logical_and(
        at_last_chip, jnp.logical_or(place == 0, jnp.logical_and(place == 2, jnp.logical_not(last_group)))
    )
    mate_slot = jnp.where(place == 2, 1, 0)
    partner = device(5 + 3 * group, 3)

    barrier = pltpu.get_barrier_semaphore()

    def greet(where):
        pl.semaphore_signal(barrier, inc=1, device_id=where, device_id_type=MESH)

    for c in range(2):
        for j in range(4):
            @pl.when(jnp.logical_or(c != core, j != y))
            def _():
                greet((first_tm + c, j))

    third_copy = pltpu.make_async_copy(vals_ref.at[:, :, :, pl.ds(128, 64)], third, third_sem)
    third_copy.start()
    prior_copy = pltpu.make_async_copy(prior_ref, x_in, prior_sem)
    starts = jnp.logical_and(column == 0, y == 0)

    @pl.when(starts)
    def _():
        prior_copy.start()


    from_before = jnp.logical_or(
        jnp.logical_and(column > 0, column <= 4), jnp.logical_and(grouped, place == 2)
    )
    from_earlier = jnp.logical_and(grouped, jnp.logical_and(place == 0, group > 0))
    earlier = device(jnp.where(group == 0, 3, 2 + 3 * group), 3)

    @pl.when(from_before)
    def _():
        greet(device(column - 1, 3))

    @pl.when(jnp.logical_or(from_earlier, is_master))
    def _():
        greet(earlier)

    @pl.when(is_master)
    def _():
        greet(device(column - 1, 3))

    @pl.when(long_master)
    def _():
        greet(device(column + 1, 3))

    last_single = jnp.logical_and(single_master, column == 3)
    peers = (
        7
        + jnp.where(jnp.logical_or(exits_first, jnp.logical_or(single_master, is_master)), 4, 0)
        + jnp.where(is_mate, 1, 0)
        + jnp.where(last_single, 1, 0)
        + jnp.where(long_master, 5, 0)
    )
    pl.semaphore_wait(barrier, peers)

    def target_of(b):
        return first_tm + b % 2, 2 * core + b // 2

    def is_me(b):
        dest_tm, dest_y = target_of(b)
        return jnp.logical_and(dest_tm == tm, dest_y == y)

    def remote(src, dst, send, recv, device):
        return pltpu.make_async_remote_copy(
            src_ref=src, dst_ref=dst, send_sem=send, recv_sem=recv, device_id=device, device_id_type=MESH
        )

    def small_pairs(b):
        start = pl.ds(8 * b, STEPS)
        return (
            (sources_ref.at[start], src_buf.at[y], 0),
            (cols_ref, cols_buf.at[y], 1),
        )

    def big_pairs(b, q):
        start, there = pl.ds(8 * b + CHUNK * q, CHUNK), pl.ds(CHUNK * q, CHUNK)
        return (
            (vals_ref.at[start, :, :, pl.ds(0, 128)], a_buf.at[y, there], 0),
            (packed.at[start], b_buf.at[y, there], 1),
            (gain_ref.at[start], gain_buf.at[y, there], 2),
        )

    def send_pair(b, src, dst, send, recv):
        @pl.when(jnp.logical_not(is_me(b)))
        def _():
            remote(src, dst, send, recv, target_of(b)).start()

        @pl.when(is_me(b))
        def _():
            pltpu.make_async_copy(src, dst, recv).start()

    for b in range(4):
        for src, dst, kind in small_pairs(b):
            send_pair(b, src, dst, send_small.at[b, kind], recv_small.at[y, kind])

    holds = core == y // 2
    first_step = 16 * lax.rem(y, 2) + 8 * core
    mine_at = pl.ds(first_step, STEPS)
    other_at = pl.ds(16 * lax.rem(y, 2) + 8 * other, STEPS)
    obs_arrays = (
        (obs_op_ref.at[mine_at], obs_op_ref.at[other_at], op_buf, 0),
        (obs_values_ref.at[mine_at], obs_values_ref.at[other_at], ov_buf, 1),
        (blocks_ref, blocks_ref, blocks_buf, 2),
        (counts_ref, counts_ref, counts_buf, 3),
    )

    @pl.when(holds)
    def _():
        for mine, others, dst, kind in obs_arrays:
            remote(others, dst, send_obs.at[kind], recv_obs.at[kind], sibling).start()
            pltpu.make_async_copy(mine, dst, recv_obs.at[kind]).start()

    def start_chunk(q, carry):
        for b in range(4):
            for src, dst, kind in big_pairs(b, q)[:1]:
                send_pair(b, src, dst, send_in.at[b, kind, q], recv_in.at[y, kind, q])

        @pl.when(q == 0)
        def _():
            third_copy.wait()

        for b in range(4):
            for t in range(CHUNK):
                at = 8 * b + CHUNK * q + t
                packed[at] = jnp.concatenate([third[at, 0], third[at, 1]], axis=1)
        for k in (1, 2):
            for b in range(4):
                src, dst, kind = big_pairs(b, q)[k]
                send_pair(b, src, dst, send_in.at[b, kind, q], recv_in.at[y, kind, q])
        return carry

    lax.fori_loop(0, NCHUNK, start_chunk, 0)

    def arrived(dst, sem):
        pltpu.make_async_copy(dst, dst, sem).wait()

    for j in range(4):
        arrived(src_buf.at[j], recv_small.at[j, 0])
        arrived(cols_buf.at[j], recv_small.at[j, 1])
    for _, _, dst, kind in obs_arrays:
        arrived(dst, recv_obs.at[kind])
    to_smem = [
        pltpu.make_async_copy(src, dst, smem_sem.at[k])
        for k, (src, dst) in enumerate(((cols_buf, cols_smem), (blocks_buf, blocks_smem), (counts_buf, counts_smem)))
    ]
    for copy in to_smem:
        copy.start()
    for copy in to_smem:
        copy.wait()

    lane64 = lax.broadcasted_iota(jnp.int32, (64, 128), 1)
    row64 = lax.broadcasted_iota(jnp.int32, (64, 128), 0)
    left64 = lane64 < 64
    half64 = lane64 // 64
    lane1 = lax.broadcasted_iota(jnp.int32, (1, 128), 1)

    maps_q[core] = jnp.zeros((4, 128), F32)

    def step(s, carry):
        at = first_step + s

        @pl.when(lax.rem(s, CHUNK) == 0)
        def _():
            q = s // CHUNK
            there = pl.ds(CHUNK * q, CHUNK)
            for j in range(4):
                arrived(a_buf.at[j, there], recv_in.at[j, 0, q])
                arrived(b_buf.at[j, there], recv_in.at[j, 1, q])

        for j in range(4):
            thirds = b_buf[j, s].astype(F32)
            thirds_turned = pltpu.roll(thirds, 64, 1)
            for il in range(2):
                i = 2 * j + il
                pair = a_buf[j, s, il].astype(F32)
                turned = pltpu.roll(pair, 64, 1)
                block0 = jnp.where(left64, pair, turned)
                block1 = jnp.where(left64, turned, pair)
                block2 = jnp.where(left64 if il == 0 else jnp.logical_not(left64), thirds, thirds_turned)
                col1 = cols_smem[j, 1, il, at]
                col2 = cols_smem[j, 2, il, at]
                for p in range(4):
                    index = half64 + 2 * p
                    value = jnp.where(index == col1, block1, jnp.where(index == col2, block2, 0.0))
                    if p == j:
                        value = jnp.where(half64 == il, block0, value)
                    f_buf[i, :, p * 128 : (p + 1) * 128] = value
                    fn_buf[i, :, p * 128 : (p + 1) * 128] = value.astype(BF16)

        operator = op_buf[s].astype(F32)
        turned_operator = operator.T.astype(BF16)
        count = counts_smem[0, at]
        images, source_columns = [], []
        for o in range(2):
            block = blocks_smem[o, at]
            selected = fn_buf[block]
            images.append(jnp.dot(turned_operator[64 * o : 64 * o + 64], selected, preferred_element_type=F32))
            source_row = src_buf[block // 2, pl.ds(s, 1), :]
            offset = lax.rem(block, 2) * 64
            source_columns.append(
                jnp.sum(jnp.where(lane64 == row64 + offset, source_row, 0.0), axis=1, keepdims=True)
            )
        image = jnp.concatenate(images, axis=0)
        slot = lax.broadcasted_iota(jnp.int32, (128, NS), 0)
        masked = jnp.where(slot < count, image, 0.0).astype(BF16)

        @pl.when(lax.rem(s, CHUNK) == 0)
        def _():
            q = s // CHUNK
            for j in range(4):
                arrived(gain_buf.at[j, pl.ds(CHUNK * q, CHUNK)], recv_in.at[j, 2, q])

        gains = gain_buf[:, s].reshape(NS, 128)
        correction = jnp.dot(gains, masked, preferred_element_type=F32)
        e_buf[s] = (f_buf[...].reshape(NS, NS) - correction).astype(BF16)

        source_image = jnp.sum(
            operator * jnp.where(left64, source_columns[0], source_columns[1]), axis=0, keepdims=True
        )
        source_image = source_image.astype(BF16).astype(F32)
        innovation = jnp.where(lane1 < count, ov_buf[pl.ds(s, 1), :] - source_image, 0.0)
        offsets = []
        for g in range(4):
            moved = jnp.sum(gain_buf[g, s].astype(F32) * innovation, axis=1, keepdims=True)
            offsets.append(column_to_row(moved) + src_buf[g, pl.ds(s, 1), :])
        put_rows(off_buf.at[s], offsets)

        moved = matvec(block_of_plain(e_buf.at[s]), rows_of(maps_q.at[core]))
        put_rows(maps_q.at[core], [m + o for m, o in zip(moved, offsets)])

        @pl.when(s == 0)
        def _():
            for h in range(2):
                maps[core, h, 0] = e_buf[s, :, h * HALF : (h + 1) * HALF]
                maps[core, h, 1] = jnp.zeros((NS, HALF), BF16)

        @pl.when(s > 0)
        def _():
            for h in range(2):
                matrix = e_buf[s]
                value = jnp.dot(matrix, maps[core, h, 0], preferred_element_type=F32)
                value = value + jnp.dot(matrix, maps[core, h, 1], preferred_element_type=F32)
                maps[core, h, 0], maps[core, h, 1] = split(value)

        return carry

    lax.fori_loop(0, STEPS, step, 0)

    map_copy = remote(maps.at[core], maps.at[core], send_map.at[0], recv_map.at[0], sibling)
    q_copy = remote(maps_q.at[core], maps_q.at[core], send_map.at[1], recv_map.at[1], sibling)
    map_copy.start()
    q_copy.start()
    arrived(maps_q.at[other], recv_map.at[1])
    arrived(maps.at[other], recv_map.at[0])
    mine = pl.ds(4 * core, 4)
    theirs = pl.ds(4 * other, 4)

    def to_chip(j):
        return tm, j

    def share(ref, k):
        return remote(ref.at[mine], ref.at[mine], send_share.at[k], recv_share.at[k], sibling)

    def shared(ref, k):
        arrived(ref.at[theirs], recv_share.at[k])

    def chip_before_copy(k):
        n = 4 * core + k
        return remote(chip.at[n], before.at[n], send_before.at[k], recv_before.at[k], to_chip(1))

    def chip_left_copy(k):
        n = 4 * core + k
        return remote(chip.at[n], left.at[n], send_left.at[k], recv_left.at[k], to_chip(3))

    def first_copy(k):
        return remote(first.at[k], first.at[k], send_first.at[k], recv_first.at[k], to_chip(3))

    first_before_copy = remote(first, before.at[mine], send_before.at[4], recv_before.at[4], to_chip(2))

    def mate_copy(k):
        n = 4 * core + k
        return remote(whole.at[n], mate.at[mate_slot, n], send_mate.at[k], recv_mate.at[mate_slot, k], partner)

    def mate_on(k, slot):
        n = 4 * core + k
        return remote(mate.at[slot, n], mate.at[slot, n], send_on.at[slot, k], recv_on.at[slot, k], sibling)

    vec_copies = (
        remote(chip_q, before_q, send_vec.at[0], recv_vec.at[0], to_chip(1)),
        remote(chip_q, left_q, send_vec.at[1], recv_vec.at[1], to_chip(3)),
        remote(first_q, first_q, send_vec.at[2], recv_vec.at[2], to_chip(3)),
        remote(first_q, before_q, send_vec.at[3], recv_vec.at[0], to_chip(2)),
        remote(whole_q, mate_q.at[mate_slot], send_vec.at[4], recv_vec.at[3 + mate_slot], partner),
    )

    def chunks(step):
        def one(k, carry):
            step(k)
            return carry

        lax.fori_loop(0, 4, one, 0)

    for h in range(2):
        total = product(maps.at[1], maps.at[0, core, :, :, pl.ds(128 * h, 128)])
        chip[4 * core + 2 * h], chip[4 * core + 2 * h + 1] = pack_pair(total)
        for k in (2 * h, 2 * h + 1):
            @pl.when(jnp.logical_and(merges, y == 0))
            def _():
                chip_before_copy(k).start()

            @pl.when(jnp.logical_and(merges, y == 2))
            def _():
                chip_left_copy(k).start()

    shares_chip = jnp.logical_or(first_column, lax.rem(y, 2) == 1)

    @pl.when(shares_chip)
    def _():
        share(chip, 0).start()

    half_map(maps.at[0], plain_c)
    half_map(maps.at[1], plain_b)
    moved = matvec(block_of_plain(plain_b), rows_of(maps_q.at[0]))
    put_rows(chip_q, sum_rows(moved, rows_of(maps_q.at[1])))

    @pl.when(merges & (y == 0))
    def _():
        vec_copies[0].start()

    @pl.when(merges & (y == 2))
    def _():
        vec_copies[1].start()

    @pl.when(shares_chip)
    def _():
        shared(chip, 0)

    def entry():
        @pl.when(jnp.logical_or(from_before, from_earlier))
        def _():
            arrived(x_in, recv_x)

    def apply(plain, vector, shift, out):
        moved = matvec(block_of_plain(plain), rows_of(vector))
        put_rows(out, [m + o for m, o in zip(moved, rows_of(shift))])

    def pair_copy(source, there):
        return remote(source, x_pair, send_x.at[8], recv_pair, device(there, 3))

    def next_copy(j):
        return remote(x_out, x_in, send_x.at[j], recv_x, device(column + 1, j))

    def middle_copy(j):
        return remote(x_mid, x_in, send_x.at[4 + j], recv_x, device(column, j))

    def end_copy(j):
        return remote(x_end, x_in, send_end.at[j], recv_x, device(column + 2, j))

    along_copy = remote(x_out, x_in, send_end.at[0], recv_x, to_chip(lax.rem(y + 1, 4)))

    @pl.when(first_column)
    def _():
        @pl.when(y == 0)
        def _():
            prior_copy.wait()

        @pl.when(y > 0)
        def _():
            arrived(x_in, recv_x)

        put_rows(x_out, sum_rows(packed_matvec(chip, rows_of(x_in)), rows_of(chip_q)))

        @pl.when(y < 3)
        def _():
            along_copy.start()

        @pl.when(y == 3)
        def _():
            for j in (3, 2, 1, 0):
                next_copy(j).start()

    @pl.when(merges & (y == 1))
    def _():
        def one(k):
            n = 4 * core + k
            arrived(before.at[n], recv_before.at[k])
            first[k] = chunk_product(chip, before[n])
            first_copy(k).start()

        chunks(one)
        first_before_copy.start()
        share(before, 1).start()
        arrived(before_q, recv_vec.at[0])
        put_rows(first_q, sum_rows(packed_matvec(chip, rows_of(before_q)), rows_of(chip_q)))
        vec_copies[2].start()
        vec_copies[3].start()

    @pl.when(merges & (y == 2))
    def _():
        arrived(before.at[mine], recv_before.at[4])
        share(before, 1).start()
        arrived(before_q, recv_vec.at[0])

    @pl.when(merges & (y == 3))
    def _():
        def one_last(k):
            n = 4 * core + k
            arrived(left.at[n], recv_left.at[k])
            last[n] = chunk_product(chip, left[n])

        chunks(one_last)
        share(last, 2).start()
        share(left, 3).start()
        arrived(left_q, recv_vec.at[1])
        put_rows(whole_q, sum_rows(packed_matvec(chip, rows_of(left_q)), rows_of(chip_q)))
        shared(last, 2)

        def one_whole(k):
            n = 4 * core + k
            arrived(first.at[k], recv_first.at[k])
            whole[n] = chunk_product(last, first[k])

            @pl.when(is_mate)
            def _():
                mate_copy(k).start()

        chunks(one_whole)

        @pl.when(jnp.logical_or(is_master, single_master))
        def _():
            share(whole, 4).start()

        arrived(first_q, recv_vec.at[2])
        put_rows(whole_q, sum_rows(packed_matvec(last, rows_of(first_q)), rows_of(whole_q)))

        @pl.when(is_mate)
        def _():
            vec_copies[4].start()

    @pl.when(single_master)
    def _():
        shared(whole, 4)
        to_plain(whole, plain_a)
        entry()
        apply(plain_a, x_in, whole_q, x_out)

        @pl.when(last_single)
        def _():
            pair_copy(x_out, 5).start()

        for j in (3, 2, 1, 0):
            next_copy(j).start()

    @pl.when(merges & (y == 3))
    def _():
        shared(left, 3)

        def one_before(k):
            before[4 * core + k] = chunk_product(left, first[k])

        chunks(one_before)
        share(before, 1).start()
        put_rows(before_q, sum_rows(packed_matvec(left, rows_of(first_q)), rows_of(left_q)))

    def inputs_sent():
        for b in range(4):
            @pl.when(jnp.logical_not(is_me(b)))
            def _():
                for src, dst, kind in small_pairs(b):
                    remote(src, dst, send_small.at[b, kind], recv_small.at[y, kind], target_of(b)).wait_send()

        def finish_chunk(q, carry):
            for b in range(4):
                @pl.when(jnp.logical_not(is_me(b)))
                def _():
                    for src, dst, kind in big_pairs(b, q):
                        remote(src, dst, send_in.at[b, kind, q], recv_in.at[y, kind, q], target_of(b)).wait_send()
            return carry

        lax.fori_loop(0, NCHUNK, finish_chunk, 0)

        @pl.when(holds)
        def _():
            for mine, others, dst, kind in obs_arrays:
                remote(others, dst, send_obs.at[kind], recv_obs.at[kind], sibling).wait_send()

    @pl.when(is_master)
    def _():
        shared(whole, 4)
        to_plain(whole, plain_a)
        inputs_sent()

        def one_mate(slot):
            def one(k):
                arrived(mate.at[slot, 4 * core + k], recv_mate.at[slot, k])
                mate_on(k, slot).start()

            chunks(one)

        one_mate(0)

        @pl.when(long_master)
        def _():
            one_mate(1)

    @pl.when(merges & (y > 0))
    def _():
        shared(before, 1)
        to_plain(before, plain_b)

    def take_mate(slot, plain):
        arrived(mate_q.at[slot], recv_vec.at[3 + slot])
        for k in range(4):
            arrived(mate.at[slot, 4 * other + k], recv_on.at[slot, k])
        to_plain(mate.at[slot], plain)

    @pl.when(jnp.logical_not(is_master))
    def _():
        inputs_sent()

    @pl.when(jnp.logical_not(single_master))
    def _():
        @pl.when(is_master)
        def _():
            take_mate(0, plain_d)

            @pl.when(long_master)
            def _():
                take_mate(1, plain_e)

        entry()

    @pl.when(is_master)
    def _():
        arrived(x_pair, recv_pair)
        apply(plain_d, x_pair, mate_q.at[0], x_mid)
        apply(plain_a, x_mid, whole_q, x_out)

        @pl.when(long_master)
        def _():
            apply(plain_e, x_out, mate_q.at[1], x_end)
            pair_copy(x_end, column + 3).start()
            for j in range(4):
                end_copy(j).start()

        for j in range(4):
            next_copy(j).start()
        for j in range(3):
            middle_copy(j).start()
        x_in[...] = x_mid[...]

    @pl.when(jnp.logical_and(grouped, jnp.logical_and(place == 1, y < 3)))
    def _():
        arrived(x_in, recv_x)

    enters = jnp.logical_or(first_column, y == 0)

    @pl.when(enters)
    def _():
        x_work[...] = x_in[...]

    @pl.when(jnp.logical_not(enters))
    def _():
        moved = matvec(block_of_plain(plain_b), rows_of(x_in))
        put_rows(x_work, [m + o for m, o in zip(moved, rows_of(before_q))])

    @pl.when(core == 1)
    def _():
        moved = matvec(block_of_plain(plain_c), rows_of(x_work))
        put_rows(x_work, [m + o for m, o in zip(moved, rows_of(maps_q.at[0]))])

    def sweep(s, carry):
        moved = matvec(block_of_plain(e_buf.at[s]), list(carry))
        rows = [m + o for m, o in zip(moved, rows_of(off_buf.at[s]))]
        for g in range(4):
            sweep_buf[g, pl.ds(s, 1), :] = rows[g]
        return tuple(rows)

    lax.fori_loop(0, STEPS, sweep, tuple(rows_of(x_work)))

    owner = first_tm + y // 2
    out_block = 2 * lax.rem(y, 2) + core
    here = pl.ds(8 * out_block, STEPS)

    def own_rows(g):
        return jnp.logical_and(owner == tm, g == y)

    for g in range(4):
        src, dst = sweep_buf.at[g], out_ref.at[here]

        @pl.when(jnp.logical_not(own_rows(g)))
        def _():
            remote(src, dst, send_out.at[g], recv_out.at[out_block], (owner, g)).start()

        @pl.when(own_rows(g))
        def _():
            pltpu.make_async_copy(src, dst, recv_out.at[out_block]).start()

    for b in range(4):
        arrived(out_ref.at[pl.ds(8 * b, STEPS)], recv_out.at[b])

    for g in range(4):
        @pl.when(jnp.logical_not(own_rows(g)))
        def _():
            remote(sweep_buf.at[g], out_ref.at[here], send_out.at[g], recv_out.at[out_block], (owner, g)).wait_send()

    map_copy.wait_send()
    q_copy.wait_send()

    @pl.when(merges & (y == 0))
    def _():
        chunks(lambda k: chip_before_copy(k).wait_send())
        vec_copies[0].wait_send()

    @pl.when(merges & (y == 1))
    def _():
        chunks(lambda k: first_copy(k).wait_send())
        first_before_copy.wait_send()
        vec_copies[2].wait_send()
        vec_copies[3].wait_send()

    @pl.when(merges & (y == 2))
    def _():
        chunks(lambda k: chip_left_copy(k).wait_send())
        vec_copies[1].wait_send()

    @pl.when(shares_chip)
    def _():
        share(chip, 0).wait_send()

    @pl.when(first_column)
    def _():
        @pl.when(y < 3)
        def _():
            along_copy.wait_send()

        @pl.when(y == 3)
        def _():
            for j in range(4):
                next_copy(j).wait_send()

    @pl.when(merges & (y > 0))
    def _():
        share(before, 1).wait_send()

    @pl.when(merges & (y == 3))
    def _():
        share(last, 2).wait_send()
        share(left, 3).wait_send()

    @pl.when(is_mate)
    def _():
        chunks(lambda k: mate_copy(k).wait_send())
        vec_copies[4].wait_send()

    @pl.when(jnp.logical_or(is_master, single_master))
    def _():
        share(whole, 4).wait_send()
        for j in range(4):
            next_copy(j).wait_send()

    @pl.when(is_master)
    def _():
        chunks(lambda k: mate_on(k, 0).wait_send())
        for j in range(3):
            middle_copy(j).wait_send()

    @pl.when(long_master)
    def _():
        chunks(lambda k: mate_on(k, 1).wait_send())
        for j in range(4):
            end_copy(j).wait_send()
        pair_copy(x_end, column + 3).wait_send()

    @pl.when(last_single)
    def _():
        pair_copy(x_out, 5).wait_send()


def body(dyn_cols, dyn_vals, obs_blocks, obs_op, obs_counts, obs_values, gain, sources, prior):
    count = dyn_vals.shape[0]
    columns_count = lax.axis_size("tm") // 2
    cols = jnp.transpose(dyn_cols, (2, 1, 0))
    blocks = jnp.transpose(obs_blocks, (1, 0))
    counts = obs_counts.reshape(1, count)
    prior_rows = prior.reshape(4, 128)
    vmem = pl.BlockSpec(memory_space=pltpu.VMEM)
    hbm = pl.BlockSpec(memory_space=pl.ANY)
    dma = pltpu.SemaphoreType.DMA
    a_map = (2, 2, NS, HALF)
    packed_map = (8, NS, 128)

    def call(*refs):
        kernel(columns_count, *refs)

    return pl.pallas_call(
        call,
        out_shape=pltpu.VMEM((count, 128), F32),
        in_specs=[hbm] * 9,
        out_specs=vmem,
        scratch_shapes=[
            pltpu.VMEM((count, 2, 64, 64), BF16),
            pltpu.VMEM((count, 64, 128), BF16),
            pltpu.VMEM((4, STEPS, 2, 64, 128), BF16),
            pltpu.VMEM((4, STEPS, 64, 128), BF16),
            pltpu.VMEM((4, STEPS, 128, 128), BF16),
            pltpu.VMEM((4, STEPS, 128), F32),
            pltpu.VMEM((4, *cols.shape), jnp.int32),
            pltpu.VMEM(blocks.shape, jnp.int32),
            pltpu.VMEM(counts.shape, jnp.int32),
            pltpu.SMEM((4, *cols.shape), jnp.int32),
            pltpu.SMEM(blocks.shape, jnp.int32),
            pltpu.SMEM(counts.shape, jnp.int32),
            pltpu.VMEM((STEPS, 64, 128), BF16),
            pltpu.VMEM((STEPS, 128), F32),
            pltpu.VMEM((8, 64, NS), F32),
            pltpu.VMEM((8, 64, NS), BF16),
            pltpu.VMEM((STEPS, NS, NS), BF16),
            pltpu.VMEM((STEPS, 4, 128), F32),
            pltpu.VMEM((2, *a_map), BF16),
            pltpu.VMEM((2, 4, 128), F32),
            pltpu.VMEM(packed_map, BF16),
            pltpu.VMEM((4, 128), F32),
            pltpu.VMEM(packed_map, BF16),
            pltpu.VMEM((4, 128), F32),
            pltpu.VMEM(packed_map, BF16),
            pltpu.VMEM((4, 128), F32),
            pltpu.VMEM((4, NS, 128), BF16),
            pltpu.VMEM((4, 128), F32),
            pltpu.VMEM(packed_map, BF16),
            pltpu.VMEM(packed_map, BF16),
            pltpu.VMEM((4, 128), F32),
            pltpu.VMEM((2, *packed_map), BF16),
            pltpu.VMEM((2, 4, 128), F32),
            pltpu.VMEM((NS, NS), F32),
            pltpu.VMEM((NS, NS), F32),
            pltpu.VMEM((NS, NS), F32),
            pltpu.VMEM((NS, NS), F32),
            pltpu.VMEM((NS, NS), F32),
            pltpu.VMEM((4, 128), F32),
            pltpu.VMEM((4, 128), F32),
            pltpu.VMEM((4, 128), F32),
            pltpu.VMEM((4, 128), F32),
            pltpu.VMEM((4, 128), F32),
            pltpu.VMEM((4, 128), F32),
            pltpu.VMEM((4, STEPS, 128), F32),
            dma((4, 3, NCHUNK)), dma((4, 3, NCHUNK)),
            dma((4, 2)), dma((4, 2)),
            dma((4,)), dma((4,)), dma((3,)),
            dma((2,)), dma((2,)), dma((5,)), dma((5,)), dma((4,)), dma((4,)), dma((4,)), dma((4,)),
            dma((4,)), dma((2, 4)), dma((5,)), dma((5,)), dma((5,)), dma((5,)), dma((2, 4)), dma((2, 4)),
            dma((9,)), dma, dma, dma((4,)), dma((4,)), dma, dma((4,)), dma,
        ],
        compiler_params=pltpu.CompilerParams(
            collective_id=0, has_side_effects=True, vmem_limit_bytes=58 * 1024 * 1024
        ),
        cost_estimate=pl.CostEstimate(flops=10_000_000_000, bytes_accessed=4_000_000, transcendentals=0),
    )(dyn_vals, gain, obs_op, cols, blocks, counts, obs_values, sources, prior_rows)


def solution(mesh):
    return jax.shard_map(
        body,
        mesh=mesh,
        in_specs=(
            P("tm", "state", None),
            P("tm", "state", None, None),
            P("tm", None),
            P("tm", None, None),
            P("tm"),
            P("tm", None),
            P("tm", "state", None),
            P("tm", "state"),
            P(),
        ),
        out_specs=P("tm", "state"),
        check_vma=False,
    )
```

```python
import jax
import jax.numpy as jnp
from jax import lax
from jax.experimental import pallas as pl
from jax.experimental.pallas import tpu as pltpu
from jax.sharding import PartitionSpec as P

MESH = pl.DeviceIdType.MESH
F32 = jnp.float32
BF16 = jnp.bfloat16
NS = 512
HALF = 256
STEPS = 8
CHUNK = 1
NCHUNK = STEPS // CHUNK


def split(value):
    high = value.astype(BF16)
    low = (value - high.astype(F32)).astype(BF16)
    return high, low


def column_to_row(column):
    rows = lax.broadcasted_iota(jnp.int32, (128, 128), 0)
    lanes = lax.broadcasted_iota(jnp.int32, (128, 128), 1)
    return jnp.sum(jnp.where(rows == lanes, column, 0.0), axis=0, keepdims=True)


def matvec(load, vector):
    out = []
    for g in range(4):
        total = load(g, 0) * vector[0]
        for j in range(1, 4):
            total = total + load(g, j) * vector[j]
        out.append(column_to_row(jnp.sum(total, axis=1, keepdims=True)))
    return out


def rows_of(ref):
    return [ref[g : g + 1, :] for g in range(4)]


def put_rows(ref, rows):
    for g in range(4):
        ref[g : g + 1, :] = rows[g]


def block_of_plain(ref):
    def load(g, j):
        return ref[pl.ds(g * 128, 128), pl.ds(j * 128, 128)].astype(F32)

    return load


def product(left, right):
    total = None
    for h in range(2):
        rows = pl.ds(h * HALF, HALF)
        for a, b in ((0, 0), (0, 1), (1, 0)):
            term = jnp.dot(left[h, a], right[b, rows, :], preferred_element_type=F32)
            total = term if total is None else total + term
    return total


def half_map(maps_ref, out):
    for h in range(2):
        out[:, h * HALF : (h + 1) * HALF] = maps_ref[h, 0].astype(F32) + maps_ref[h, 1].astype(F32)


def left_lanes(shape):
    return lax.broadcasted_iota(jnp.int32, shape, 1) < 64


def pack_chunk(doubled):
    low = doubled - doubled.astype(BF16).astype(F32)
    return jnp.where(left_lanes(doubled.shape), doubled, low).astype(BF16)


def pack_pair(pair):
    turned = pltpu.roll(pair, 64, 1)
    left = left_lanes(pair.shape)
    return pack_chunk(jnp.where(left, pair, turned)), pack_chunk(jnp.where(left, turned, pair))


def chunk_product(left, right):
    rows = right.reshape(8, 64, 128)
    rows = jnp.concatenate([rows, rows], axis=1).reshape(2 * NS, 128)
    lanes = jnp.concatenate([left[n] for n in range(8)], axis=1)
    parts = jnp.dot(lanes, rows, preferred_element_type=F32)
    return pack_chunk(parts + pltpu.roll(parts, 64, 1))


def plain_pair(packed, n, out):
    first, second = packed[2 * n].astype(F32), packed[2 * n + 1].astype(F32)
    first, second = first + pltpu.roll(first, 64, 1), second + pltpu.roll(second, 64, 1)
    out[:, pl.ds(pl.multiple_of(n * 128, 128), 128)] = jnp.where(left_lanes(first.shape), first, second)


def to_plain(packed, out):
    for n in range(4):
        plain_pair(packed, n, out)


def packed_matvec(packed, vector):
    doubled = []
    for row in vector:
        doubled.append(jnp.concatenate([row[:, :64], row[:, :64]], axis=1))
        doubled.append(jnp.concatenate([row[:, 64:], row[:, 64:]], axis=1))
    out = []
    for g in range(4):
        total = None
        for n in range(8):
            term = packed[n, pl.ds(g * 128, 128), :].astype(F32) * doubled[n]
            total = term if total is None else total + term
        out.append(column_to_row(jnp.sum(total, axis=1, keepdims=True)))
    return out


def sum_rows(a, b):
    return [m + o for m, o in zip(a, b)]


def kernel(
    columns_count,
    vals_ref, gain_ref, obs_op_ref, cols_ref, blocks_ref, counts_ref, obs_values_ref, sources_ref, prior_ref,
    out_ref,
    third, packed, a_buf, b_buf, gain_buf, src_buf, cols_buf, blocks_buf, counts_buf,
    cols_smem, blocks_smem, counts_smem, op_buf, ov_buf,
    f_buf, fn_buf, e_buf, off_buf,
    maps, maps_q, chip, chip_q, before, before_q, left, left_q, first, first_q, last, whole, whole_q,
    mate, mate_q, plain_a, plain_b, plain_c, plain_d, plain_e, x_in, x_pair, x_mid, x_out, x_end, x_work, sweep_buf,
    send_in, recv_in, send_small, recv_small, send_obs, recv_obs, smem_sem,
    send_map, recv_map, send_before, recv_before, send_left, recv_left, send_first, recv_first,
    send_mate, recv_mate, send_vec, recv_vec, send_share, recv_share, send_on, recv_on,
    send_x, recv_x, recv_pair, send_out, recv_out, third_sem, send_end, prior_sem, send_whole, recv_whole,
):
    tm, y = lax.axis_index("tm"), lax.axis_index("state")
    core = lax.rem(tm, 2)
    column = tm // 2
    first_tm = tm - core
    other = 1 - core
    sibling = (first_tm + other, y)
    groups = (columns_count - 4) // 3
    single = column < 4
    grouped = jnp.logical_not(single)
    group = (column - 4) // 3
    place = column - 4 - 3 * group
    last_group = group == groups - 1

    def device(c, j):
        return 2 * c + core, j

    first_column = column == 0
    merges = column > 0
    at_last_chip = jnp.logical_and(y == 3, grouped)
    single_master = jnp.logical_and(y == 3, jnp.logical_and(single, merges))
    exits_first = jnp.logical_and(first_column, y == 3)
    is_master = jnp.logical_and(at_last_chip, place == 1)
    long_master = jnp.logical_and(is_master, jnp.logical_not(last_group))
    is_mate = jnp.logical_and(
        at_last_chip, jnp.logical_or(place == 0, jnp.logical_and(place == 2, jnp.logical_not(last_group)))
    )
    mate_slot = jnp.where(place == 2, 1, 0)
    partner = device(5 + 3 * group, 3)

    barrier = pltpu.get_barrier_semaphore()

    def greet(where):
        pl.semaphore_signal(barrier, inc=1, device_id=where, device_id_type=MESH)

    for c in range(2):
        for j in range(4):
            @pl.when(jnp.logical_or(c != core, j != y))
            def _():
                greet((first_tm + c, j))

    third_copy = pltpu.make_async_copy(vals_ref.at[:, :, :, pl.ds(128, 64)], third, third_sem)
    third_copy.start()
    prior_copy = pltpu.make_async_copy(prior_ref, x_in, prior_sem)
    starts = jnp.logical_and(column == 0, y == 0)

    @pl.when(starts)
    def _():
        prior_copy.start()


    from_before = jnp.logical_or(
        jnp.logical_and(column > 0, column <= 4), jnp.logical_and(grouped, place == 2)
    )
    from_earlier = jnp.logical_and(grouped, jnp.logical_and(place == 0, group > 0))
    earlier = device(jnp.where(group == 0, 3, 2 + 3 * group), 3)

    @pl.when(from_before)
    def _():
        greet(device(column - 1, 3))

    @pl.when(jnp.logical_or(from_earlier, is_master))
    def _():
        greet(earlier)

    @pl.when(is_master)
    def _():
        greet(device(column - 1, 3))

    @pl.when(long_master)
    def _():
        greet(device(column + 1, 3))

    last_single = jnp.logical_and(single_master, column == 3)
    peers = (
        7
        + jnp.where(jnp.logical_or(exits_first, jnp.logical_or(single_master, is_master)), 4, 0)
        + jnp.where(is_mate, 1, 0)
        + jnp.where(last_single, 1, 0)
        + jnp.where(long_master, 5, 0)
    )
    pl.semaphore_wait(barrier, peers)

    def target_of(b):
        return first_tm + b % 2, 2 * core + b // 2

    def is_me(b):
        dest_tm, dest_y = target_of(b)
        return jnp.logical_and(dest_tm == tm, dest_y == y)

    def remote(src, dst, send, recv, device):
        return pltpu.make_async_remote_copy(
            src_ref=src, dst_ref=dst, send_sem=send, recv_sem=recv, device_id=device, device_id_type=MESH
        )

    def small_pairs(b):
        start = pl.ds(8 * b, STEPS)
        return (
            (sources_ref.at[start], src_buf.at[y], 0),
            (cols_ref, cols_buf.at[y], 1),
        )

    def big_pairs(b, q):
        start, there = pl.ds(8 * b + CHUNK * q, CHUNK), pl.ds(CHUNK * q, CHUNK)
        return (
            (vals_ref.at[start, :, :, pl.ds(0, 128)], a_buf.at[y, there], 0),
            (packed.at[start], b_buf.at[y, there], 1),
            (gain_ref.at[start], gain_buf.at[y, there], 2),
        )

    def send_pair(b, src, dst, send, recv):
        @pl.when(jnp.logical_not(is_me(b)))
        def _():
            remote(src, dst, send, recv, target_of(b)).start()

        @pl.when(is_me(b))
        def _():
            pltpu.make_async_copy(src, dst, recv).start()

    for b in range(4):
        for src, dst, kind in small_pairs(b):
            send_pair(b, src, dst, send_small.at[b, kind], recv_small.at[y, kind])

    holds = core == y // 2
    first_step = 16 * lax.rem(y, 2) + 8 * core
    mine_at = pl.ds(first_step, STEPS)
    other_at = pl.ds(16 * lax.rem(y, 2) + 8 * other, STEPS)
    obs_arrays = (
        (obs_op_ref.at[mine_at], obs_op_ref.at[other_at], op_buf, 0),
        (obs_values_ref.at[mine_at], obs_values_ref.at[other_at], ov_buf, 1),
        (blocks_ref, blocks_ref, blocks_buf, 2),
        (counts_ref, counts_ref, counts_buf, 3),
    )

    @pl.when(holds)
    def _():
        for mine, others, dst, kind in obs_arrays:
            remote(others, dst, send_obs.at[kind], recv_obs.at[kind], sibling).start()
            pltpu.make_async_copy(mine, dst, recv_obs.at[kind]).start()

    def start_chunk(q, carry):
        for b in range(4):
            for src, dst, kind in big_pairs(b, q)[:1]:
                send_pair(b, src, dst, send_in.at[b, kind, q], recv_in.at[y, kind, q])

        @pl.when(q == 0)
        def _():
            third_copy.wait()

        for b in range(4):
            for t in range(CHUNK):
                at = 8 * b + CHUNK * q + t
                packed[at] = jnp.concatenate([third[at, 0], third[at, 1]], axis=1)
        for k in (1, 2):
            for b in range(4):
                src, dst, kind = big_pairs(b, q)[k]
                send_pair(b, src, dst, send_in.at[b, kind, q], recv_in.at[y, kind, q])
        return carry

    lax.fori_loop(0, NCHUNK, start_chunk, 0)

    def arrived(dst, sem):
        pltpu.make_async_copy(dst, dst, sem).wait()

    for j in range(4):
        arrived(src_buf.at[j], recv_small.at[j, 0])
        arrived(cols_buf.at[j], recv_small.at[j, 1])
    for _, _, dst, kind in obs_arrays:
        arrived(dst, recv_obs.at[kind])
    to_smem = [
        pltpu.make_async_copy(src, dst, smem_sem.at[k])
        for k, (src, dst) in enumerate(((cols_buf, cols_smem), (blocks_buf, blocks_smem), (counts_buf, counts_smem)))
    ]
    for copy in to_smem:
        copy.start()
    for copy in to_smem:
        copy.wait()

    lane64 = lax.broadcasted_iota(jnp.int32, (64, 128), 1)
    row64 = lax.broadcasted_iota(jnp.int32, (64, 128), 0)
    left64 = lane64 < 64
    half64 = lane64 // 64
    lane1 = lax.broadcasted_iota(jnp.int32, (1, 128), 1)

    maps_q[core] = jnp.zeros((4, 128), F32)

    def step(s, carry):
        at = first_step + s

        @pl.when(lax.rem(s, CHUNK) == 0)
        def _():
            q = s // CHUNK
            there = pl.ds(CHUNK * q, CHUNK)
            for j in range(4):
                arrived(a_buf.at[j, there], recv_in.at[j, 0, q])
                arrived(b_buf.at[j, there], recv_in.at[j, 1, q])

        for j in range(4):
            thirds = b_buf[j, s].astype(F32)
            thirds_turned = pltpu.roll(thirds, 64, 1)
            for il in range(2):
                i = 2 * j + il
                pair = a_buf[j, s, il].astype(F32)
                turned = pltpu.roll(pair, 64, 1)
                block0 = jnp.where(left64, pair, turned)
                block1 = jnp.where(left64, turned, pair)
                block2 = jnp.where(left64 if il == 0 else jnp.logical_not(left64), thirds, thirds_turned)
                col1 = cols_smem[j, 1, il, at]
                col2 = cols_smem[j, 2, il, at]
                for p in range(4):
                    index = half64 + 2 * p
                    value = jnp.where(index == col1, block1, jnp.where(index == col2, block2, 0.0))
                    if p == j:
                        value = jnp.where(half64 == il, block0, value)
                    f_buf[i, :, p * 128 : (p + 1) * 128] = value
                    fn_buf[i, :, p * 128 : (p + 1) * 128] = value.astype(BF16)

        operator = op_buf[s].astype(F32)
        turned_operator = operator.T.astype(BF16)
        count = counts_smem[0, at]
        images, source_columns = [], []
        for o in range(2):
            block = blocks_smem[o, at]
            selected = fn_buf[block]
            images.append(jnp.dot(turned_operator[64 * o : 64 * o + 64], selected, preferred_element_type=F32))
            source_row = src_buf[block // 2, pl.ds(s, 1), :]
            offset = lax.rem(block, 2) * 64
            source_columns.append(
                jnp.sum(jnp.where(lane64 == row64 + offset, source_row, 0.0), axis=1, keepdims=True)
            )
        image = jnp.concatenate(images, axis=0)
        slot = lax.broadcasted_iota(jnp.int32, (128, NS), 0)
        masked = jnp.where(slot < count, image, 0.0).astype(BF16)

        @pl.when(lax.rem(s, CHUNK) == 0)
        def _():
            q = s // CHUNK
            for j in range(4):
                arrived(gain_buf.at[j, pl.ds(CHUNK * q, CHUNK)], recv_in.at[j, 2, q])

        gains = gain_buf[:, s].reshape(NS, 128)
        correction = jnp.dot(gains, masked, preferred_element_type=F32)
        e_buf[s] = (f_buf[...].reshape(NS, NS) - correction).astype(BF16)

        source_image = jnp.sum(
            operator * jnp.where(left64, source_columns[0], source_columns[1]), axis=0, keepdims=True
        )
        source_image = source_image.astype(BF16).astype(F32)
        innovation = jnp.where(lane1 < count, ov_buf[pl.ds(s, 1), :] - source_image, 0.0)
        offsets = []
        for g in range(4):
            moved = jnp.sum(gain_buf[g, s].astype(F32) * innovation, axis=1, keepdims=True)
            offsets.append(column_to_row(moved) + src_buf[g, pl.ds(s, 1), :])
        put_rows(off_buf.at[s], offsets)

        moved = matvec(block_of_plain(e_buf.at[s]), rows_of(maps_q.at[core]))
        put_rows(maps_q.at[core], [m + o for m, o in zip(moved, offsets)])

        @pl.when(s == 0)
        def _():
            for h in range(2):
                maps[core, h, 0] = e_buf[s, :, h * HALF : (h + 1) * HALF]
                maps[core, h, 1] = jnp.zeros((NS, HALF), BF16)

        @pl.when(s > 0)
        def _():
            for h in range(2):
                matrix = e_buf[s]
                value = jnp.dot(matrix, maps[core, h, 0], preferred_element_type=F32)
                value = value + jnp.dot(matrix, maps[core, h, 1], preferred_element_type=F32)
                maps[core, h, 0], maps[core, h, 1] = split(value)

        return carry

    lax.fori_loop(0, STEPS, step, 0)

    map_copy = remote(maps.at[core], maps.at[core], send_map.at[0], recv_map.at[0], sibling)
    q_copy = remote(maps_q.at[core], maps_q.at[core], send_map.at[1], recv_map.at[1], sibling)
    map_copy.start()
    q_copy.start()
    arrived(maps_q.at[other], recv_map.at[1])
    arrived(maps.at[other], recv_map.at[0])
    mine = pl.ds(4 * core, 4)
    theirs = pl.ds(4 * other, 4)

    def to_chip(j):
        return tm, j

    def share(ref, k):
        return remote(ref.at[mine], ref.at[mine], send_share.at[k], recv_share.at[k], sibling)

    def shared(ref, k):
        arrived(ref.at[theirs], recv_share.at[k])

    def chip_before_copy(k):
        n = 4 * core + k
        return remote(chip.at[n], before.at[n], send_before.at[k], recv_before.at[k], to_chip(1))

    def chip_left_copy(k):
        n = 4 * core + k
        return remote(chip.at[n], left.at[n], send_left.at[k], recv_left.at[k], to_chip(3))

    def first_copy(k):
        return remote(first.at[k], first.at[k], send_first.at[k], recv_first.at[k], to_chip(3))

    first_before_copy = remote(first, before.at[mine], send_before.at[4], recv_before.at[4], to_chip(2))

    def mate_copy(k):
        n = 4 * core + k
        return remote(whole.at[n], mate.at[mate_slot, n], send_mate.at[k], recv_mate.at[mate_slot, k], partner)

    holds_whole = jnp.logical_or(is_master, single_master)

    def whole_on(k):
        n = 4 * core + k
        return remote(whole.at[n], whole.at[n], send_whole.at[k], recv_whole.at[k], sibling)

    def take_whole():
        for h in range(2):
            plain_pair(whole, 2 * core + h, plain_a)
        for k in range(4):
            arrived(whole.at[4 * other + k], recv_whole.at[k])
        for h in range(2):
            plain_pair(whole, 2 * other + h, plain_a)

    def mate_on(k, slot):
        n = 4 * core + k
        return remote(mate.at[slot, n], mate.at[slot, n], send_on.at[slot, k], recv_on.at[slot, k], sibling)

    vec_copies = (
        remote(chip_q, before_q, send_vec.at[0], recv_vec.at[0], to_chip(1)),
        remote(chip_q, left_q, send_vec.at[1], recv_vec.at[1], to_chip(3)),
        remote(first_q, first_q, send_vec.at[2], recv_vec.at[2], to_chip(3)),
        remote(first_q, before_q, send_vec.at[3], recv_vec.at[0], to_chip(2)),
        remote(whole_q, mate_q.at[mate_slot], send_vec.at[4], recv_vec.at[3 + mate_slot], partner),
    )

    def chunks(step):
        def one(k, carry):
            step(k)
            return carry

        lax.fori_loop(0, 4, one, 0)

    for h in range(2):
        total = product(maps.at[1], maps.at[0, core, :, :, pl.ds(128 * h, 128)])
        chip[4 * core + 2 * h], chip[4 * core + 2 * h + 1] = pack_pair(total)
        for k in (2 * h, 2 * h + 1):
            @pl.when(jnp.logical_and(merges, y == 0))
            def _():
                chip_before_copy(k).start()

            @pl.when(jnp.logical_and(merges, y == 2))
            def _():
                chip_left_copy(k).start()

    shares_chip = jnp.logical_or(first_column, lax.rem(y, 2) == 1)

    @pl.when(shares_chip)
    def _():
        share(chip, 0).start()

    half_map(maps.at[0], plain_c)
    half_map(maps.at[1], plain_b)
    moved = matvec(block_of_plain(plain_b), rows_of(maps_q.at[0]))
    put_rows(chip_q, sum_rows(moved, rows_of(maps_q.at[1])))

    @pl.when(merges & (y == 0))
    def _():
        vec_copies[0].start()

    @pl.when(merges & (y == 2))
    def _():
        vec_copies[1].start()

    @pl.when(shares_chip)
    def _():
        shared(chip, 0)

    def entry():
        @pl.when(jnp.logical_or(from_before, from_earlier))
        def _():
            arrived(x_in, recv_x)

    def apply(plain, vector, shift, out):
        moved = matvec(block_of_plain(plain), rows_of(vector))
        put_rows(out, [m + o for m, o in zip(moved, rows_of(shift))])

    def pair_copy(source, there):
        return remote(source, x_pair, send_x.at[8], recv_pair, device(there, 3))

    def next_copy(j):
        return remote(x_out, x_in, send_x.at[j], recv_x, device(column + 1, j))

    def middle_copy(j):
        return remote(x_mid, x_in, send_x.at[4 + j], recv_x, device(column, j))

    def end_copy(j):
        return remote(x_end, x_in, send_end.at[j], recv_x, device(column + 2, j))

    along_copy = remote(x_out, x_in, send_end.at[0], recv_x, to_chip(lax.rem(y + 1, 4)))

    @pl.when(first_column)
    def _():
        @pl.when(y == 0)
        def _():
            prior_copy.wait()

        @pl.when(y > 0)
        def _():
            arrived(x_in, recv_x)

        put_rows(x_out, sum_rows(packed_matvec(chip, rows_of(x_in)), rows_of(chip_q)))

        @pl.when(y < 3)
        def _():
            along_copy.start()

        @pl.when(y == 3)
        def _():
            for j in (3, 2, 1, 0):
                next_copy(j).start()

    @pl.when(merges & (y == 1))
    def _():
        def one(k):
            n = 4 * core + k
            arrived(before.at[n], recv_before.at[k])
            first[k] = chunk_product(chip, before[n])
            first_copy(k).start()

        chunks(one)
        first_before_copy.start()
        share(before, 1).start()
        arrived(before_q, recv_vec.at[0])
        put_rows(first_q, sum_rows(packed_matvec(chip, rows_of(before_q)), rows_of(chip_q)))
        vec_copies[2].start()
        vec_copies[3].start()

    @pl.when(merges & (y == 2))
    def _():
        arrived(before.at[mine], recv_before.at[4])
        share(before, 1).start()
        arrived(before_q, recv_vec.at[0])

    @pl.when(merges & (y == 3))
    def _():
        def one_last(k):
            n = 4 * core + k
            arrived(left.at[n], recv_left.at[k])
            last[n] = chunk_product(chip, left[n])

        chunks(one_last)
        share(last, 2).start()
        share(left, 3).start()
        arrived(left_q, recv_vec.at[1])
        put_rows(whole_q, sum_rows(packed_matvec(chip, rows_of(left_q)), rows_of(chip_q)))
        shared(last, 2)

        def one_whole(k):
            n = 4 * core + k
            arrived(first.at[k], recv_first.at[k])
            whole[n] = chunk_product(last, first[k])

            @pl.when(is_mate)
            def _():
                mate_copy(k).start()

            @pl.when(holds_whole)
            def _():
                whole_on(k).start()

        chunks(one_whole)

        arrived(first_q, recv_vec.at[2])
        put_rows(whole_q, sum_rows(packed_matvec(last, rows_of(first_q)), rows_of(whole_q)))

        @pl.when(is_mate)
        def _():
            vec_copies[4].start()

    @pl.when(single_master)
    def _():
        take_whole()
        entry()
        apply(plain_a, x_in, whole_q, x_out)

        @pl.when(last_single)
        def _():
            pair_copy(x_out, 5).start()

        for j in (3, 2, 1, 0):
            next_copy(j).start()

    @pl.when(merges & (y == 3))
    def _():
        shared(left, 3)

        def one_before(k):
            before[4 * core + k] = chunk_product(left, first[k])

        chunks(one_before)
        share(before, 1).start()
        put_rows(before_q, sum_rows(packed_matvec(left, rows_of(first_q)), rows_of(left_q)))

    def inputs_sent():
        for b in range(4):
            @pl.when(jnp.logical_not(is_me(b)))
            def _():
                for src, dst, kind in small_pairs(b):
                    remote(src, dst, send_small.at[b, kind], recv_small.at[y, kind], target_of(b)).wait_send()

        def finish_chunk(q, carry):
            for b in range(4):
                @pl.when(jnp.logical_not(is_me(b)))
                def _():
                    for src, dst, kind in big_pairs(b, q):
                        remote(src, dst, send_in.at[b, kind, q], recv_in.at[y, kind, q], target_of(b)).wait_send()
            return carry

        lax.fori_loop(0, NCHUNK, finish_chunk, 0)

        @pl.when(holds)
        def _():
            for mine, others, dst, kind in obs_arrays:
                remote(others, dst, send_obs.at[kind], recv_obs.at[kind], sibling).wait_send()

    @pl.when(is_master)
    def _():
        take_whole()
        inputs_sent()

        def one_mate(k, slot, plain):
            arrived(mate.at[slot, 4 * core + k], recv_mate.at[slot, k])
            mate_on(k, slot).start()

            @pl.when(lax.rem(k, 2) == 1)
            def _():
                plain_pair(mate.at[slot], 2 * core + k // 2, plain)

        def both(k):
            one_mate(k, 0, plain_d)

            @pl.when(long_master)
            def _():
                one_mate(k, 1, plain_e)

        chunks(both)

    @pl.when(merges & (y > 0))
    def _():
        shared(before, 1)
        to_plain(before, plain_b)

    def take_mate(slot, plain):
        arrived(mate_q.at[slot], recv_vec.at[3 + slot])
        for k in range(4):
            arrived(mate.at[slot, 4 * other + k], recv_on.at[slot, k])
        for h in range(2):
            plain_pair(mate.at[slot], 2 * other + h, plain)

    @pl.when(jnp.logical_not(is_master))
    def _():
        inputs_sent()

    @pl.when(jnp.logical_not(single_master))
    def _():
        @pl.when(is_master)
        def _():
            take_mate(0, plain_d)

            @pl.when(long_master)
            def _():
                take_mate(1, plain_e)

        entry()

    @pl.when(is_master)
    def _():
        arrived(x_pair, recv_pair)
        apply(plain_d, x_pair, mate_q.at[0], x_mid)
        apply(plain_a, x_mid, whole_q, x_out)

        @pl.when(long_master)
        def _():
            apply(plain_e, x_out, mate_q.at[1], x_end)
            pair_copy(x_end, column + 3).start()
            for j in range(4):
                end_copy(j).start()

        for j in range(4):
            next_copy(j).start()
        for j in range(3):
            middle_copy(j).start()
        x_in[...] = x_mid[...]

    @pl.when(jnp.logical_and(grouped, jnp.logical_and(place == 1, y < 3)))
    def _():
        arrived(x_in, recv_x)

    enters = jnp.logical_or(first_column, y == 0)

    @pl.when(enters)
    def _():
        x_work[...] = x_in[...]

    @pl.when(jnp.logical_not(enters))
    def _():
        moved = matvec(block_of_plain(plain_b), rows_of(x_in))
        put_rows(x_work, [m + o for m, o in zip(moved, rows_of(before_q))])

    @pl.when(core == 1)
    def _():
        moved = matvec(block_of_plain(plain_c), rows_of(x_work))
        put_rows(x_work, [m + o for m, o in zip(moved, rows_of(maps_q.at[0]))])

    def sweep(s, carry):
        moved = matvec(block_of_plain(e_buf.at[s]), list(carry))
        rows = [m + o for m, o in zip(moved, rows_of(off_buf.at[s]))]
        for g in range(4):
            sweep_buf[g, pl.ds(s, 1), :] = rows[g]
        return tuple(rows)

    lax.fori_loop(0, STEPS, sweep, tuple(rows_of(x_work)))

    owner = first_tm + y // 2
    out_block = 2 * lax.rem(y, 2) + core
    here = pl.ds(8 * out_block, STEPS)

    def own_rows(g):
        return jnp.logical_and(owner == tm, g == y)

    for g in range(4):
        src, dst = sweep_buf.at[g], out_ref.at[here]

        @pl.when(jnp.logical_not(own_rows(g)))
        def _():
            remote(src, dst, send_out.at[g], recv_out.at[out_block], (owner, g)).start()

        @pl.when(own_rows(g))
        def _():
            pltpu.make_async_copy(src, dst, recv_out.at[out_block]).start()

    for b in range(4):
        arrived(out_ref.at[pl.ds(8 * b, STEPS)], recv_out.at[b])

    for g in range(4):
        @pl.when(jnp.logical_not(own_rows(g)))
        def _():
            remote(sweep_buf.at[g], out_ref.at[here], send_out.at[g], recv_out.at[out_block], (owner, g)).wait_send()

    map_copy.wait_send()
    q_copy.wait_send()

    @pl.when(merges & (y == 0))
    def _():
        chunks(lambda k: chip_before_copy(k).wait_send())
        vec_copies[0].wait_send()

    @pl.when(merges & (y == 1))
    def _():
        chunks(lambda k: first_copy(k).wait_send())
        first_before_copy.wait_send()
        vec_copies[2].wait_send()
        vec_copies[3].wait_send()

    @pl.when(merges & (y == 2))
    def _():
        chunks(lambda k: chip_left_copy(k).wait_send())
        vec_copies[1].wait_send()

    @pl.when(shares_chip)
    def _():
        share(chip, 0).wait_send()

    @pl.when(first_column)
    def _():
        @pl.when(y < 3)
        def _():
            along_copy.wait_send()

        @pl.when(y == 3)
        def _():
            for j in range(4):
                next_copy(j).wait_send()

    @pl.when(merges & (y > 0))
    def _():
        share(before, 1).wait_send()

    @pl.when(merges & (y == 3))
    def _():
        share(last, 2).wait_send()
        share(left, 3).wait_send()

    @pl.when(is_mate)
    def _():
        chunks(lambda k: mate_copy(k).wait_send())
        vec_copies[4].wait_send()

    @pl.when(jnp.logical_or(is_master, single_master))
    def _():
        chunks(lambda k: whole_on(k).wait_send())
        for j in range(4):
            next_copy(j).wait_send()

    @pl.when(is_master)
    def _():
        chunks(lambda k: mate_on(k, 0).wait_send())
        for j in range(3):
            middle_copy(j).wait_send()

    @pl.when(long_master)
    def _():
        chunks(lambda k: mate_on(k, 1).wait_send())
        for j in range(4):
            end_copy(j).wait_send()
        pair_copy(x_end, column + 3).wait_send()

    @pl.when(last_single)
    def _():
        pair_copy(x_out, 5).wait_send()


def body(dyn_cols, dyn_vals, obs_blocks, obs_op, obs_counts, obs_values, gain, sources, prior):
    count = dyn_vals.shape[0]
    columns_count = lax.axis_size("tm") // 2
    cols = jnp.transpose(dyn_cols, (2, 1, 0))
    blocks = jnp.transpose(obs_blocks, (1, 0))
    counts = obs_counts.reshape(1, count)
    prior_rows = prior.reshape(4, 128)
    vmem = pl.BlockSpec(memory_space=pltpu.VMEM)
    hbm = pl.BlockSpec(memory_space=pl.ANY)
    dma = pltpu.SemaphoreType.DMA
    a_map = (2, 2, NS, HALF)
    packed_map = (8, NS, 128)

    def call(*refs):
        kernel(columns_count, *refs)

    return pl.pallas_call(
        call,
        out_shape=pltpu.VMEM((count, 128), F32),
        in_specs=[hbm] * 9,
        out_specs=vmem,
        scratch_shapes=[
            pltpu.VMEM((count, 2, 64, 64), BF16),
            pltpu.VMEM((count, 64, 128), BF16),
            pltpu.VMEM((4, STEPS, 2, 64, 128), BF16),
            pltpu.VMEM((4, STEPS, 64, 128), BF16),
            pltpu.VMEM((4, STEPS, 128, 128), BF16),
            pltpu.VMEM((4, STEPS, 128), F32),
            pltpu.VMEM((4, *cols.shape), jnp.int32),
            pltpu.VMEM(blocks.shape, jnp.int32),
            pltpu.VMEM(counts.shape, jnp.int32),
            pltpu.SMEM((4, *cols.shape), jnp.int32),
            pltpu.SMEM(blocks.shape, jnp.int32),
            pltpu.SMEM(counts.shape, jnp.int32),
            pltpu.VMEM((STEPS, 64, 128), BF16),
            pltpu.VMEM((STEPS, 128), F32),
            pltpu.VMEM((8, 64, NS), F32),
            pltpu.VMEM((8, 64, NS), BF16),
            pltpu.VMEM((STEPS, NS, NS), BF16),
            pltpu.VMEM((STEPS, 4, 128), F32),
            pltpu.VMEM((2, *a_map), BF16),
            pltpu.VMEM((2, 4, 128), F32),
            pltpu.VMEM(packed_map, BF16),
            pltpu.VMEM((4, 128), F32),
            pltpu.VMEM(packed_map, BF16),
            pltpu.VMEM((4, 128), F32),
            pltpu.VMEM(packed_map, BF16),
            pltpu.VMEM((4, 128), F32),
            pltpu.VMEM((4, NS, 128), BF16),
            pltpu.VMEM((4, 128), F32),
            pltpu.VMEM(packed_map, BF16),
            pltpu.VMEM(packed_map, BF16),
            pltpu.VMEM((4, 128), F32),
            pltpu.VMEM((2, *packed_map), BF16),
            pltpu.VMEM((2, 4, 128), F32),
            pltpu.VMEM((NS, NS), F32),
            pltpu.VMEM((NS, NS), F32),
            pltpu.VMEM((NS, NS), F32),
            pltpu.VMEM((NS, NS), F32),
            pltpu.VMEM((NS, NS), F32),
            pltpu.VMEM((4, 128), F32),
            pltpu.VMEM((4, 128), F32),
            pltpu.VMEM((4, 128), F32),
            pltpu.VMEM((4, 128), F32),
            pltpu.VMEM((4, 128), F32),
            pltpu.VMEM((4, 128), F32),
            pltpu.VMEM((4, STEPS, 128), F32),
            dma((4, 3, NCHUNK)), dma((4, 3, NCHUNK)),
            dma((4, 2)), dma((4, 2)),
            dma((4,)), dma((4,)), dma((3,)),
            dma((2,)), dma((2,)), dma((5,)), dma((5,)), dma((4,)), dma((4,)), dma((4,)), dma((4,)),
            dma((4,)), dma((2, 4)), dma((5,)), dma((5,)), dma((5,)), dma((5,)), dma((2, 4)), dma((2, 4)),
            dma((9,)), dma, dma, dma((4,)), dma((4,)), dma, dma((4,)), dma, dma((4,)), dma((4,)),
        ],
        compiler_params=pltpu.CompilerParams(
            collective_id=0, has_side_effects=True, vmem_limit_bytes=58 * 1024 * 1024
        ),
        cost_estimate=pl.CostEstimate(flops=10_000_000_000, bytes_accessed=4_000_000, transcendentals=0),
    )(dyn_vals, gain, obs_op, cols, blocks, counts, obs_values, sources, prior_rows)


def solution(mesh):
    return jax.shard_map(
        body,
        mesh=mesh,
        in_specs=(
            P("tm", "state", None),
            P("tm", "state", None, None),
            P("tm", None),
            P("tm", None, None),
            P("tm"),
            P("tm", None),
            P("tm", "state", None),
            P("tm", "state"),
            P(),
        ),
        out_specs=P("tm", "state"),
        check_vma=False,
    )
```

```python
import jax
import jax.numpy as jnp
from jax import lax
from jax.experimental import pallas as pl
from jax.experimental.pallas import tpu as pltpu
from jax.sharding import PartitionSpec as P

MESH = pl.DeviceIdType.MESH
F32 = jnp.float32
BF16 = jnp.bfloat16
NS = 512
HALF = 256
STEPS = 8
CHUNK = 1
NCHUNK = STEPS // CHUNK


def split(value):
    high = value.astype(BF16)
    low = (value - high.astype(F32)).astype(BF16)
    return high, low


def column_to_row(column):
    rows = lax.broadcasted_iota(jnp.int32, (128, 128), 0)
    lanes = lax.broadcasted_iota(jnp.int32, (128, 128), 1)
    return jnp.sum(jnp.where(rows == lanes, column, 0.0), axis=0, keepdims=True)


def matvec(load, vector):
    out = []
    for g in range(4):
        total = load(g, 0) * vector[0]
        for j in range(1, 4):
            total = total + load(g, j) * vector[j]
        out.append(column_to_row(jnp.sum(total, axis=1, keepdims=True)))
    return out


def rows_of(ref):
    return [ref[g : g + 1, :] for g in range(4)]


def put_rows(ref, rows):
    for g in range(4):
        ref[g : g + 1, :] = rows[g]


def block_of_plain(ref):
    def load(g, j):
        return ref[pl.ds(g * 128, 128), pl.ds(j * 128, 128)].astype(F32)

    return load


def half_product(left, right, h):
    rows = pl.ds(h * HALF, HALF)
    total = None
    for a, b in ((0, 0), (0, 1), (1, 0)):
        term = jnp.dot(left[h, a], right[b, rows, :], preferred_element_type=F32)
        total = term if total is None else total + term
    return total


def half_map(maps_ref, out):
    for h in range(2):
        out[:, h * HALF : (h + 1) * HALF] = maps_ref[h, 0].astype(F32) + maps_ref[h, 1].astype(F32)


def left_lanes(shape):
    return lax.broadcasted_iota(jnp.int32, shape, 1) < 64


def pack_chunk(doubled):
    low = doubled - doubled.astype(BF16).astype(F32)
    return jnp.where(left_lanes(doubled.shape), doubled, low).astype(BF16)


def pack_pair(pair):
    turned = pltpu.roll(pair, 64, 1)
    left = left_lanes(pair.shape)
    return pack_chunk(jnp.where(left, pair, turned)), pack_chunk(jnp.where(left, turned, pair))


def chunk_product(left, right):
    rows = right.reshape(8, 64, 128)
    rows = jnp.concatenate([rows, rows], axis=1).reshape(2 * NS, 128)
    lanes = jnp.concatenate([left[n] for n in range(8)], axis=1)
    parts = jnp.dot(lanes, rows, preferred_element_type=F32)
    return pack_chunk(parts + pltpu.roll(parts, 64, 1))


def plain_pair(packed, n, out):
    first, second = packed[2 * n].astype(F32), packed[2 * n + 1].astype(F32)
    first, second = first + pltpu.roll(first, 64, 1), second + pltpu.roll(second, 64, 1)
    out[:, pl.ds(pl.multiple_of(n * 128, 128), 128)] = jnp.where(left_lanes(first.shape), first, second)


def to_plain(packed, out):
    for n in range(4):
        plain_pair(packed, n, out)


def packed_matvec(packed, vector):
    doubled = []
    for row in vector:
        doubled.append(jnp.concatenate([row[:, :64], row[:, :64]], axis=1))
        doubled.append(jnp.concatenate([row[:, 64:], row[:, 64:]], axis=1))
    out = []
    for g in range(4):
        total = None
        for n in range(8):
            term = packed[n, pl.ds(g * 128, 128), :].astype(F32) * doubled[n]
            total = term if total is None else total + term
        out.append(column_to_row(jnp.sum(total, axis=1, keepdims=True)))
    return out


def sum_rows(a, b):
    return [m + o for m, o in zip(a, b)]


def kernel(
    columns_count,
    vals_ref, gain_ref, obs_op_ref, cols_ref, blocks_ref, counts_ref, obs_values_ref, sources_ref, prior_ref,
    out_ref,
    third, packed, a_buf, b_buf, gain_buf, src_buf, cols_buf, blocks_buf, counts_buf,
    cols_smem, blocks_smem, counts_smem, op_buf, ov_buf,
    f_buf, fn_buf, e_buf, off_buf,
    maps, maps_q, chip, chip_q, before, before_q, left, left_q, first, first_q, last, whole, whole_q,
    mate, mate_q, plain_a, plain_b, plain_c, plain_d, plain_e, x_in, x_pair, x_mid, x_out, x_end, x_work, sweep_buf,
    send_in, recv_in, send_small, recv_small, send_obs, recv_obs, smem_sem,
    send_map, recv_map, send_before, recv_before, send_left, recv_left, send_first, recv_first,
    send_mate, recv_mate, send_vec, recv_vec, send_share, recv_share, send_on, recv_on,
    send_x, recv_x, recv_pair, send_out, recv_out, third_sem, send_end, prior_sem, send_whole, recv_whole,
):
    tm, y = lax.axis_index("tm"), lax.axis_index("state")
    core = lax.rem(tm, 2)
    column = tm // 2
    first_tm = tm - core
    other = 1 - core
    sibling = (first_tm + other, y)
    groups = (columns_count - 4) // 3
    single = column < 4
    grouped = jnp.logical_not(single)
    group = (column - 4) // 3
    place = column - 4 - 3 * group
    last_group = group == groups - 1

    def device(c, j):
        return 2 * c + core, j

    first_column = column == 0
    merges = column > 0
    at_last_chip = jnp.logical_and(y == 3, grouped)
    single_master = jnp.logical_and(y == 3, jnp.logical_and(single, merges))
    exits_first = jnp.logical_and(first_column, y == 3)
    is_master = jnp.logical_and(at_last_chip, place == 1)
    long_master = jnp.logical_and(is_master, jnp.logical_not(last_group))
    is_mate = jnp.logical_and(
        at_last_chip, jnp.logical_or(place == 0, jnp.logical_and(place == 2, jnp.logical_not(last_group)))
    )
    mate_slot = jnp.where(place == 2, 1, 0)
    partner = device(5 + 3 * group, 3)

    barrier = pltpu.get_barrier_semaphore()

    def greet(where):
        pl.semaphore_signal(barrier, inc=1, device_id=where, device_id_type=MESH)

    for c in range(2):
        for j in range(4):
            @pl.when(jnp.logical_or(c != core, j != y))
            def _():
                greet((first_tm + c, j))

    third_copy = pltpu.make_async_copy(vals_ref.at[:, :, :, pl.ds(128, 64)], third, third_sem)
    third_copy.start()
    prior_copy = pltpu.make_async_copy(prior_ref, x_in, prior_sem)
    starts = jnp.logical_and(column == 0, y == 0)

    @pl.when(starts)
    def _():
        prior_copy.start()


    from_before = jnp.logical_or(
        jnp.logical_and(column > 0, column <= 4), jnp.logical_and(grouped, place == 2)
    )
    from_earlier = jnp.logical_and(grouped, jnp.logical_and(place == 0, group > 0))
    earlier = device(jnp.where(group == 0, 3, 2 + 3 * group), 3)

    @pl.when(from_before)
    def _():
        greet(device(column - 1, 3))

    @pl.when(jnp.logical_or(from_earlier, is_master))
    def _():
        greet(earlier)

    @pl.when(is_master)
    def _():
        greet(device(column - 1, 3))

    @pl.when(long_master)
    def _():
        greet(device(column + 1, 3))

    last_single = jnp.logical_and(single_master, column == 3)
    peers = (
        7
        + jnp.where(jnp.logical_or(exits_first, jnp.logical_or(single_master, is_master)), 4, 0)
        + jnp.where(is_mate, 1, 0)
        + jnp.where(last_single, 1, 0)
        + jnp.where(long_master, 5, 0)
    )
    pl.semaphore_wait(barrier, peers)

    def target_of(b):
        return first_tm + b % 2, 2 * core + b // 2

    def is_me(b):
        dest_tm, dest_y = target_of(b)
        return jnp.logical_and(dest_tm == tm, dest_y == y)

    def remote(src, dst, send, recv, device):
        return pltpu.make_async_remote_copy(
            src_ref=src, dst_ref=dst, send_sem=send, recv_sem=recv, device_id=device, device_id_type=MESH
        )

    def small_pairs(b):
        start = pl.ds(8 * b, STEPS)
        return (
            (sources_ref.at[start], src_buf.at[y], 0),
            (cols_ref, cols_buf.at[y], 1),
        )

    def big_pairs(b, q):
        start, there = pl.ds(8 * b + CHUNK * q, CHUNK), pl.ds(CHUNK * q, CHUNK)
        return (
            (vals_ref.at[start, :, :, pl.ds(0, 128)], a_buf.at[y, there], 0),
            (packed.at[start], b_buf.at[y, there], 1),
            (gain_ref.at[start], gain_buf.at[y, there], 2),
        )

    def send_pair(b, src, dst, send, recv):
        @pl.when(jnp.logical_not(is_me(b)))
        def _():
            remote(src, dst, send, recv, target_of(b)).start()

        @pl.when(is_me(b))
        def _():
            pltpu.make_async_copy(src, dst, recv).start()

    for b in range(4):
        for src, dst, kind in small_pairs(b):
            send_pair(b, src, dst, send_small.at[b, kind], recv_small.at[y, kind])

    holds = core == y // 2
    first_step = 16 * lax.rem(y, 2) + 8 * core
    mine_at = pl.ds(first_step, STEPS)
    other_at = pl.ds(16 * lax.rem(y, 2) + 8 * other, STEPS)
    obs_arrays = (
        (obs_op_ref.at[mine_at], obs_op_ref.at[other_at], op_buf, 0),
        (obs_values_ref.at[mine_at], obs_values_ref.at[other_at], ov_buf, 1),
        (blocks_ref, blocks_ref, blocks_buf, 2),
        (counts_ref, counts_ref, counts_buf, 3),
    )

    @pl.when(holds)
    def _():
        for mine, others, dst, kind in obs_arrays:
            remote(others, dst, send_obs.at[kind], recv_obs.at[kind], sibling).start()
            pltpu.make_async_copy(mine, dst, recv_obs.at[kind]).start()

    def start_chunk(q, carry):
        for b in range(4):
            for src, dst, kind in big_pairs(b, q)[:1]:
                send_pair(b, src, dst, send_in.at[b, kind, q], recv_in.at[y, kind, q])

        @pl.when(q == 0)
        def _():
            third_copy.wait()

        for b in range(4):
            for t in range(CHUNK):
                at = 8 * b + CHUNK * q + t
                packed[at] = jnp.concatenate([third[at, 0], third[at, 1]], axis=1)
        for k in (1, 2):
            for b in range(4):
                src, dst, kind = big_pairs(b, q)[k]
                send_pair(b, src, dst, send_in.at[b, kind, q], recv_in.at[y, kind, q])
        return carry

    lax.fori_loop(0, NCHUNK, start_chunk, 0)

    def arrived(dst, sem):
        pltpu.make_async_copy(dst, dst, sem).wait()

    for j in range(4):
        arrived(src_buf.at[j], recv_small.at[j, 0])
        arrived(cols_buf.at[j], recv_small.at[j, 1])
    for _, _, dst, kind in obs_arrays:
        arrived(dst, recv_obs.at[kind])
    to_smem = [
        pltpu.make_async_copy(src, dst, smem_sem.at[k])
        for k, (src, dst) in enumerate(((cols_buf, cols_smem), (blocks_buf, blocks_smem), (counts_buf, counts_smem)))
    ]
    for copy in to_smem:
        copy.start()
    for copy in to_smem:
        copy.wait()

    lane64 = lax.broadcasted_iota(jnp.int32, (64, 128), 1)
    row64 = lax.broadcasted_iota(jnp.int32, (64, 128), 0)
    left64 = lane64 < 64
    half64 = lane64 // 64
    lane1 = lax.broadcasted_iota(jnp.int32, (1, 128), 1)

    maps_q[core] = jnp.zeros((4, 128), F32)

    def step(s, carry):
        at = first_step + s

        @pl.when(lax.rem(s, CHUNK) == 0)
        def _():
            q = s // CHUNK
            there = pl.ds(CHUNK * q, CHUNK)
            for j in range(4):
                arrived(a_buf.at[j, there], recv_in.at[j, 0, q])
                arrived(b_buf.at[j, there], recv_in.at[j, 1, q])

        for j in range(4):
            thirds = b_buf[j, s].astype(F32)
            thirds_turned = pltpu.roll(thirds, 64, 1)
            for il in range(2):
                i = 2 * j + il
                pair = a_buf[j, s, il].astype(F32)
                turned = pltpu.roll(pair, 64, 1)
                block0 = jnp.where(left64, pair, turned)
                block1 = jnp.where(left64, turned, pair)
                block2 = jnp.where(left64 if il == 0 else jnp.logical_not(left64), thirds, thirds_turned)
                col1 = cols_smem[j, 1, il, at]
                col2 = cols_smem[j, 2, il, at]
                for p in range(4):
                    index = half64 + 2 * p
                    value = jnp.where(index == col1, block1, jnp.where(index == col2, block2, 0.0))
                    if p == j:
                        value = jnp.where(half64 == il, block0, value)
                    f_buf[i, :, p * 128 : (p + 1) * 128] = value
                    fn_buf[i, :, p * 128 : (p + 1) * 128] = value.astype(BF16)

        operator = op_buf[s].astype(F32)
        turned_operator = operator.T.astype(BF16)
        count = counts_smem[0, at]
        images, source_columns = [], []
        for o in range(2):
            block = blocks_smem[o, at]
            selected = fn_buf[block]
            images.append(jnp.dot(turned_operator[64 * o : 64 * o + 64], selected, preferred_element_type=F32))
            source_row = src_buf[block // 2, pl.ds(s, 1), :]
            offset = lax.rem(block, 2) * 64
            source_columns.append(
                jnp.sum(jnp.where(lane64 == row64 + offset, source_row, 0.0), axis=1, keepdims=True)
            )
        image = jnp.concatenate(images, axis=0)
        slot = lax.broadcasted_iota(jnp.int32, (128, NS), 0)
        masked = jnp.where(slot < count, image, 0.0).astype(BF16)

        @pl.when(lax.rem(s, CHUNK) == 0)
        def _():
            q = s // CHUNK
            for j in range(4):
                arrived(gain_buf.at[j, pl.ds(CHUNK * q, CHUNK)], recv_in.at[j, 2, q])

        gains = gain_buf[:, s].reshape(NS, 128)
        correction = jnp.dot(gains, masked, preferred_element_type=F32)
        e_buf[s] = (f_buf[...].reshape(NS, NS) - correction).astype(BF16)

        source_image = jnp.sum(
            operator * jnp.where(left64, source_columns[0], source_columns[1]), axis=0, keepdims=True
        )
        source_image = source_image.astype(BF16).astype(F32)
        innovation = jnp.where(lane1 < count, ov_buf[pl.ds(s, 1), :] - source_image, 0.0)
        offsets = []
        for g in range(4):
            moved = jnp.sum(gain_buf[g, s].astype(F32) * innovation, axis=1, keepdims=True)
            offsets.append(column_to_row(moved) + src_buf[g, pl.ds(s, 1), :])
        put_rows(off_buf.at[s], offsets)

        moved = matvec(block_of_plain(e_buf.at[s]), rows_of(maps_q.at[core]))
        put_rows(maps_q.at[core], [m + o for m, o in zip(moved, offsets)])

        @pl.when(s == 0)
        def _():
            for h in range(2):
                maps[core, h, 0] = e_buf[s, :, h * HALF : (h + 1) * HALF]
                maps[core, h, 1] = jnp.zeros((NS, HALF), BF16)

        @pl.when(s > 0)
        def _():
            for h in range(2):
                matrix = e_buf[s]
                value = jnp.dot(matrix, maps[core, h, 0], preferred_element_type=F32)
                value = value + jnp.dot(matrix, maps[core, h, 1], preferred_element_type=F32)
                maps[core, h, 0], maps[core, h, 1] = split(value)

        return carry

    lax.fori_loop(0, STEPS, step, 0)

    def map_copy(h, k):
        return remote(maps.at[core, h], maps.at[core, h], send_map.at[k], recv_map.at[k], sibling)

    q_copy = remote(maps_q.at[core], maps_q.at[core], send_map.at[1], recv_map.at[1], sibling)
    map_copy(other, 0).start()
    map_copy(core, 2).start()
    q_copy.start()
    arrived(maps.at[other, core], recv_map.at[0])
    mine = pl.ds(4 * core, 4)
    theirs = pl.ds(4 * other, 4)

    def to_chip(j):
        return tm, j

    def share(ref, k):
        return remote(ref.at[mine], ref.at[mine], send_share.at[k], recv_share.at[k], sibling)

    def shared(ref, k):
        arrived(ref.at[theirs], recv_share.at[k])

    def chip_before_copy(k):
        n = 4 * core + k
        return remote(chip.at[n], before.at[n], send_before.at[k], recv_before.at[k], to_chip(1))

    def chip_left_copy(k):
        n = 4 * core + k
        return remote(chip.at[n], left.at[n], send_left.at[k], recv_left.at[k], to_chip(3))

    def first_copy(k):
        return remote(first.at[k], first.at[k], send_first.at[k], recv_first.at[k], to_chip(3))

    first_before_copy = remote(first, before.at[mine], send_before.at[4], recv_before.at[4], to_chip(2))

    def mate_copy(k):
        n = 4 * core + k
        return remote(whole.at[n], mate.at[mate_slot, n], send_mate.at[k], recv_mate.at[mate_slot, k], partner)

    holds_whole = jnp.logical_or(is_master, single_master)

    def whole_on(k):
        n = 4 * core + k
        return remote(whole.at[n], whole.at[n], send_whole.at[k], recv_whole.at[k], sibling)

    def take_whole():
        for h in range(2):
            plain_pair(whole, 2 * core + h, plain_a)
        for k in range(4):
            arrived(whole.at[4 * other + k], recv_whole.at[k])
        for h in range(2):
            plain_pair(whole, 2 * other + h, plain_a)

    def mate_on(k, slot):
        n = 4 * core + k
        return remote(mate.at[slot, n], mate.at[slot, n], send_on.at[slot, k], recv_on.at[slot, k], sibling)

    vec_copies = (
        remote(chip_q, before_q, send_vec.at[0], recv_vec.at[0], to_chip(1)),
        remote(chip_q, left_q, send_vec.at[1], recv_vec.at[1], to_chip(3)),
        remote(first_q, first_q, send_vec.at[2], recv_vec.at[2], to_chip(3)),
        remote(first_q, before_q, send_vec.at[3], recv_vec.at[0], to_chip(2)),
        remote(whole_q, mate_q.at[mate_slot], send_vec.at[4], recv_vec.at[3 + mate_slot], partner),
    )

    def chunks(step):
        def one(k, carry):
            step(k)
            return carry

        lax.fori_loop(0, 4, one, 0)

    def right(h):
        return maps.at[0, core, :, :, pl.ds(128 * h, 128)]

    for h in range(2):
        plain_c[:, h * 128 : (h + 1) * 128] = half_product(maps.at[1], right(h), 0)

    @pl.when(core == 0)
    def _():
        arrived(maps.at[other, other], recv_map.at[2])

    for h in range(2):
        total = plain_c[:, h * 128 : (h + 1) * 128] + half_product(maps.at[1], right(h), 1)
        chip[4 * core + 2 * h], chip[4 * core + 2 * h + 1] = pack_pair(total)
        for k in (2 * h, 2 * h + 1):
            @pl.when(jnp.logical_and(merges, y == 0))
            def _():
                chip_before_copy(k).start()

            @pl.when(jnp.logical_and(merges, y == 2))
            def _():
                chip_left_copy(k).start()

    shares_chip = jnp.logical_or(first_column, lax.rem(y, 2) == 1)

    @pl.when(shares_chip)
    def _():
        share(chip, 0).start()

    @pl.when(core == 1)
    def _():
        arrived(maps.at[other, other], recv_map.at[2])

    arrived(maps_q.at[other], recv_map.at[1])
    half_map(maps.at[0], plain_c)
    half_map(maps.at[1], plain_b)
    moved = matvec(block_of_plain(plain_b), rows_of(maps_q.at[0]))
    put_rows(chip_q, sum_rows(moved, rows_of(maps_q.at[1])))

    @pl.when(merges & (y == 0))
    def _():
        vec_copies[0].start()

    @pl.when(merges & (y == 2))
    def _():
        vec_copies[1].start()

    @pl.when(shares_chip)
    def _():
        shared(chip, 0)

    def entry():
        @pl.when(jnp.logical_or(from_before, from_earlier))
        def _():
            arrived(x_in, recv_x)

    def apply(plain, vector, shift, out):
        moved = matvec(block_of_plain(plain), rows_of(vector))
        put_rows(out, [m + o for m, o in zip(moved, rows_of(shift))])

    def pair_copy(source, there):
        return remote(source, x_pair, send_x.at[8], recv_pair, device(there, 3))

    def next_copy(j):
        return remote(x_out, x_in, send_x.at[j], recv_x, device(column + 1, j))

    def middle_copy(j):
        return remote(x_mid, x_in, send_x.at[4 + j], recv_x, device(column, j))

    def end_copy(j):
        return remote(x_end, x_in, send_end.at[j], recv_x, device(column + 2, j))

    along_copy = remote(x_out, x_in, send_end.at[0], recv_x, to_chip(lax.rem(y + 1, 4)))

    @pl.when(first_column)
    def _():
        @pl.when(y == 0)
        def _():
            prior_copy.wait()

        @pl.when(y > 0)
        def _():
            arrived(x_in, recv_x)

        put_rows(x_out, sum_rows(packed_matvec(chip, rows_of(x_in)), rows_of(chip_q)))

        @pl.when(y < 3)
        def _():
            along_copy.start()

        @pl.when(y == 3)
        def _():
            for j in (3, 2, 1, 0):
                next_copy(j).start()

    @pl.when(merges & (y == 1))
    def _():
        def one(k):
            n = 4 * core + k
            arrived(before.at[n], recv_before.at[k])
            first[k] = chunk_product(chip, before[n])
            first_copy(k).start()

        chunks(one)
        first_before_copy.start()
        share(before, 1).start()
        arrived(before_q, recv_vec.at[0])
        put_rows(first_q, sum_rows(packed_matvec(chip, rows_of(before_q)), rows_of(chip_q)))
        vec_copies[2].start()
        vec_copies[3].start()

    @pl.when(merges & (y == 2))
    def _():
        arrived(before.at[mine], recv_before.at[4])
        share(before, 1).start()
        arrived(before_q, recv_vec.at[0])

    @pl.when(merges & (y == 3))
    def _():
        def one_last(k):
            n = 4 * core + k
            arrived(left.at[n], recv_left.at[k])
            last[n] = chunk_product(chip, left[n])

        chunks(one_last)
        share(last, 2).start()
        share(left, 3).start()
        arrived(left_q, recv_vec.at[1])
        put_rows(whole_q, sum_rows(packed_matvec(chip, rows_of(left_q)), rows_of(chip_q)))
        shared(last, 2)

        def one_whole(k):
            n = 4 * core + k
            arrived(first.at[k], recv_first.at[k])
            whole[n] = chunk_product(last, first[k])

            @pl.when(is_mate)
            def _():
                mate_copy(k).start()

            @pl.when(holds_whole)
            def _():
                whole_on(k).start()

        chunks(one_whole)

        arrived(first_q, recv_vec.at[2])
        put_rows(whole_q, sum_rows(packed_matvec(last, rows_of(first_q)), rows_of(whole_q)))

        @pl.when(is_mate)
        def _():
            vec_copies[4].start()

    @pl.when(single_master)
    def _():
        take_whole()
        entry()
        apply(plain_a, x_in, whole_q, x_out)

        @pl.when(last_single)
        def _():
            pair_copy(x_out, 5).start()

        for j in (3, 2, 1, 0):
            next_copy(j).start()

    @pl.when(merges & (y == 3))
    def _():
        shared(left, 3)

        def one_before(k):
            before[4 * core + k] = chunk_product(left, first[k])

        chunks(one_before)
        share(before, 1).start()
        put_rows(before_q, sum_rows(packed_matvec(left, rows_of(first_q)), rows_of(left_q)))

    def inputs_sent():
        for b in range(4):
            @pl.when(jnp.logical_not(is_me(b)))
            def _():
                for src, dst, kind in small_pairs(b):
                    remote(src, dst, send_small.at[b, kind], recv_small.at[y, kind], target_of(b)).wait_send()

        def finish_chunk(q, carry):
            for b in range(4):
                @pl.when(jnp.logical_not(is_me(b)))
                def _():
                    for src, dst, kind in big_pairs(b, q):
                        remote(src, dst, send_in.at[b, kind, q], recv_in.at[y, kind, q], target_of(b)).wait_send()
            return carry

        lax.fori_loop(0, NCHUNK, finish_chunk, 0)

        @pl.when(holds)
        def _():
            for mine, others, dst, kind in obs_arrays:
                remote(others, dst, send_obs.at[kind], recv_obs.at[kind], sibling).wait_send()

    @pl.when(is_master)
    def _():
        take_whole()
        inputs_sent()

        def one_mate(k, slot, plain):
            arrived(mate.at[slot, 4 * core + k], recv_mate.at[slot, k])
            mate_on(k, slot).start()

            @pl.when(lax.rem(k, 2) == 1)
            def _():
                plain_pair(mate.at[slot], 2 * core + k // 2, plain)

        def both(k):
            one_mate(k, 0, plain_d)

            @pl.when(long_master)
            def _():
                one_mate(k, 1, plain_e)

        chunks(both)

    @pl.when(merges & (y > 0))
    def _():
        shared(before, 1)
        to_plain(before, plain_b)

    def take_mate(slot, plain):
        arrived(mate_q.at[slot], recv_vec.at[3 + slot])
        for k in range(4):
            arrived(mate.at[slot, 4 * other + k], recv_on.at[slot, k])
        for h in range(2):
            plain_pair(mate.at[slot], 2 * other + h, plain)

    @pl.when(jnp.logical_not(is_master))
    def _():
        inputs_sent()

    @pl.when(jnp.logical_not(single_master))
    def _():
        @pl.when(is_master)
        def _():
            take_mate(0, plain_d)

            @pl.when(long_master)
            def _():
                take_mate(1, plain_e)

        entry()

    @pl.when(is_master)
    def _():
        arrived(x_pair, recv_pair)
        apply(plain_d, x_pair, mate_q.at[0], x_mid)
        apply(plain_a, x_mid, whole_q, x_out)

        @pl.when(long_master)
        def _():
            apply(plain_e, x_out, mate_q.at[1], x_end)
            pair_copy(x_end, column + 3).start()
            for j in range(4):
                end_copy(j).start()

        for j in range(4):
            next_copy(j).start()
        for j in range(3):
            middle_copy(j).start()
        x_in[...] = x_mid[...]

    @pl.when(jnp.logical_and(grouped, jnp.logical_and(place == 1, y < 3)))
    def _():
        arrived(x_in, recv_x)

    enters = jnp.logical_or(first_column, y == 0)

    @pl.when(enters)
    def _():
        x_work[...] = x_in[...]

    @pl.when(jnp.logical_not(enters))
    def _():
        moved = matvec(block_of_plain(plain_b), rows_of(x_in))
        put_rows(x_work, [m + o for m, o in zip(moved, rows_of(before_q))])

    @pl.when(core == 1)
    def _():
        moved = matvec(block_of_plain(plain_c), rows_of(x_work))
        put_rows(x_work, [m + o for m, o in zip(moved, rows_of(maps_q.at[0]))])

    def sweep(s, carry):
        moved = matvec(block_of_plain(e_buf.at[s]), list(carry))
        rows = [m + o for m, o in zip(moved, rows_of(off_buf.at[s]))]
        for g in range(4):
            sweep_buf[g, pl.ds(s, 1), :] = rows[g]
        return tuple(rows)

    lax.fori_loop(0, STEPS, sweep, tuple(rows_of(x_work)))

    owner = first_tm + y // 2
    out_block = 2 * lax.rem(y, 2) + core
    here = pl.ds(8 * out_block, STEPS)

    def own_rows(g):
        return jnp.logical_and(owner == tm, g == y)

    for g in range(4):
        src, dst = sweep_buf.at[g], out_ref.at[here]

        @pl.when(jnp.logical_not(own_rows(g)))
        def _():
            remote(src, dst, send_out.at[g], recv_out.at[out_block], (owner, g)).start()

        @pl.when(own_rows(g))
        def _():
            pltpu.make_async_copy(src, dst, recv_out.at[out_block]).start()

    for b in range(4):
        arrived(out_ref.at[pl.ds(8 * b, STEPS)], recv_out.at[b])

    for g in range(4):
        @pl.when(jnp.logical_not(own_rows(g)))
        def _():
            remote(sweep_buf.at[g], out_ref.at[here], send_out.at[g], recv_out.at[out_block], (owner, g)).wait_send()

    map_copy(other, 0).wait_send()
    map_copy(core, 2).wait_send()
    q_copy.wait_send()

    @pl.when(merges & (y == 0))
    def _():
        chunks(lambda k: chip_before_copy(k).wait_send())
        vec_copies[0].wait_send()

    @pl.when(merges & (y == 1))
    def _():
        chunks(lambda k: first_copy(k).wait_send())
        first_before_copy.wait_send()
        vec_copies[2].wait_send()
        vec_copies[3].wait_send()

    @pl.when(merges & (y == 2))
    def _():
        chunks(lambda k: chip_left_copy(k).wait_send())
        vec_copies[1].wait_send()

    @pl.when(shares_chip)
    def _():
        share(chip, 0).wait_send()

    @pl.when(first_column)
    def _():
        @pl.when(y < 3)
        def _():
            along_copy.wait_send()

        @pl.when(y == 3)
        def _():
            for j in range(4):
                next_copy(j).wait_send()

    @pl.when(merges & (y > 0))
    def _():
        share(before, 1).wait_send()

    @pl.when(merges & (y == 3))
    def _():
        share(last, 2).wait_send()
        share(left, 3).wait_send()

    @pl.when(is_mate)
    def _():
        chunks(lambda k: mate_copy(k).wait_send())
        vec_copies[4].wait_send()

    @pl.when(jnp.logical_or(is_master, single_master))
    def _():
        chunks(lambda k: whole_on(k).wait_send())
        for j in range(4):
            next_copy(j).wait_send()

    @pl.when(is_master)
    def _():
        chunks(lambda k: mate_on(k, 0).wait_send())
        for j in range(3):
            middle_copy(j).wait_send()

    @pl.when(long_master)
    def _():
        chunks(lambda k: mate_on(k, 1).wait_send())
        for j in range(4):
            end_copy(j).wait_send()
        pair_copy(x_end, column + 3).wait_send()

    @pl.when(last_single)
    def _():
        pair_copy(x_out, 5).wait_send()


def body(dyn_cols, dyn_vals, obs_blocks, obs_op, obs_counts, obs_values, gain, sources, prior):
    count = dyn_vals.shape[0]
    columns_count = lax.axis_size("tm") // 2
    cols = jnp.transpose(dyn_cols, (2, 1, 0))
    blocks = jnp.transpose(obs_blocks, (1, 0))
    counts = obs_counts.reshape(1, count)
    prior_rows = prior.reshape(4, 128)
    vmem = pl.BlockSpec(memory_space=pltpu.VMEM)
    hbm = pl.BlockSpec(memory_space=pl.ANY)
    dma = pltpu.SemaphoreType.DMA
    a_map = (2, 2, NS, HALF)
    packed_map = (8, NS, 128)

    def call(*refs):
        kernel(columns_count, *refs)

    return pl.pallas_call(
        call,
        out_shape=pltpu.VMEM((count, 128), F32),
        in_specs=[hbm] * 9,
        out_specs=vmem,
        scratch_shapes=[
            pltpu.VMEM((count, 2, 64, 64), BF16),
            pltpu.VMEM((count, 64, 128), BF16),
            pltpu.VMEM((4, STEPS, 2, 64, 128), BF16),
            pltpu.VMEM((4, STEPS, 64, 128), BF16),
            pltpu.VMEM((4, STEPS, 128, 128), BF16),
            pltpu.VMEM((4, STEPS, 128), F32),
            pltpu.VMEM((4, *cols.shape), jnp.int32),
            pltpu.VMEM(blocks.shape, jnp.int32),
            pltpu.VMEM(counts.shape, jnp.int32),
            pltpu.SMEM((4, *cols.shape), jnp.int32),
            pltpu.SMEM(blocks.shape, jnp.int32),
            pltpu.SMEM(counts.shape, jnp.int32),
            pltpu.VMEM((STEPS, 64, 128), BF16),
            pltpu.VMEM((STEPS, 128), F32),
            pltpu.VMEM((8, 64, NS), F32),
            pltpu.VMEM((8, 64, NS), BF16),
            pltpu.VMEM((STEPS, NS, NS), BF16),
            pltpu.VMEM((STEPS, 4, 128), F32),
            pltpu.VMEM((2, *a_map), BF16),
            pltpu.VMEM((2, 4, 128), F32),
            pltpu.VMEM(packed_map, BF16),
            pltpu.VMEM((4, 128), F32),
            pltpu.VMEM(packed_map, BF16),
            pltpu.VMEM((4, 128), F32),
            pltpu.VMEM(packed_map, BF16),
            pltpu.VMEM((4, 128), F32),
            pltpu.VMEM((4, NS, 128), BF16),
            pltpu.VMEM((4, 128), F32),
            pltpu.VMEM(packed_map, BF16),
            pltpu.VMEM(packed_map, BF16),
            pltpu.VMEM((4, 128), F32),
            pltpu.VMEM((2, *packed_map), BF16),
            pltpu.VMEM((2, 4, 128), F32),
            pltpu.VMEM((NS, NS), F32),
            pltpu.VMEM((NS, NS), F32),
            pltpu.VMEM((NS, NS), F32),
            pltpu.VMEM((NS, NS), F32),
            pltpu.VMEM((NS, NS), F32),
            pltpu.VMEM((4, 128), F32),
            pltpu.VMEM((4, 128), F32),
            pltpu.VMEM((4, 128), F32),
            pltpu.VMEM((4, 128), F32),
            pltpu.VMEM((4, 128), F32),
            pltpu.VMEM((4, 128), F32),
            pltpu.VMEM((4, STEPS, 128), F32),
            dma((4, 3, NCHUNK)), dma((4, 3, NCHUNK)),
            dma((4, 2)), dma((4, 2)),
            dma((4,)), dma((4,)), dma((3,)),
            dma((3,)), dma((3,)), dma((5,)), dma((5,)), dma((4,)), dma((4,)), dma((4,)), dma((4,)),
            dma((4,)), dma((2, 4)), dma((5,)), dma((5,)), dma((5,)), dma((5,)), dma((2, 4)), dma((2, 4)),
            dma((9,)), dma, dma, dma((4,)), dma((4,)), dma, dma((4,)), dma, dma((4,)), dma((4,)),
        ],
        compiler_params=pltpu.CompilerParams(
            collective_id=0, has_side_effects=True, vmem_limit_bytes=58 * 1024 * 1024
        ),
        cost_estimate=pl.CostEstimate(flops=10_000_000_000, bytes_accessed=4_000_000, transcendentals=0),
    )(dyn_vals, gain, obs_op, cols, blocks, counts, obs_values, sources, prior_rows)


def solution(mesh):
    return jax.shard_map(
        body,
        mesh=mesh,
        in_specs=(
            P("tm", "state", None),
            P("tm", "state", None, None),
            P("tm", None),
            P("tm", None, None),
            P("tm"),
            P("tm", None),
            P("tm", "state", None),
            P("tm", "state"),
            P(),
        ),
        out_specs=P("tm", "state"),
        check_vma=False,
    )
```

```python
import jax
import jax.numpy as jnp
from jax import lax
from jax.experimental import pallas as pl
from jax.experimental.pallas import tpu as pltpu
from jax.sharding import PartitionSpec as P

MESH = pl.DeviceIdType.MESH
F32 = jnp.float32
BF16 = jnp.bfloat16
NS = 512
HALF = 256
STEPS = 8
CHUNK = 1
NCHUNK = STEPS // CHUNK


def split(value):
    high = value.astype(BF16)
    low = (value - high.astype(F32)).astype(BF16)
    return high, low


def column_to_row(column):
    rows = lax.broadcasted_iota(jnp.int32, (128, 128), 0)
    lanes = lax.broadcasted_iota(jnp.int32, (128, 128), 1)
    return jnp.sum(jnp.where(rows == lanes, column, 0.0), axis=0, keepdims=True)


def matvec(load, vector):
    out = []
    for g in range(4):
        total = load(g, 0) * vector[0]
        for j in range(1, 4):
            total = total + load(g, j) * vector[j]
        out.append(column_to_row(jnp.sum(total, axis=1, keepdims=True)))
    return out


def rows_of(ref):
    return [ref[g : g + 1, :] for g in range(4)]


def put_rows(ref, rows):
    for g in range(4):
        ref[g : g + 1, :] = rows[g]


def block_of_plain(ref):
    def load(g, j):
        return ref[pl.ds(g * 128, 128), pl.ds(j * 128, 128)].astype(F32)

    return load


def half_product(left, right, h):
    rows = pl.ds(h * HALF, HALF)
    total = None
    for a, b in ((0, 0), (0, 1), (1, 0)):
        term = jnp.dot(left[h, a], right[b, rows, :], preferred_element_type=F32)
        total = term if total is None else total + term
    return total


def half_map(maps_ref, out):
    for h in range(2):
        out[:, h * HALF : (h + 1) * HALF] = maps_ref[h, 0].astype(F32) + maps_ref[h, 1].astype(F32)


def left_lanes(shape):
    return lax.broadcasted_iota(jnp.int32, shape, 1) < 64


def pack_chunk(doubled):
    low = doubled - doubled.astype(BF16).astype(F32)
    return jnp.where(left_lanes(doubled.shape), doubled, low).astype(BF16)


def pack_pair(pair):
    turned = pltpu.roll(pair, 64, 1)
    left = left_lanes(pair.shape)
    return pack_chunk(jnp.where(left, pair, turned)), pack_chunk(jnp.where(left, turned, pair))


def chunk_product(left, right):
    rows = right.reshape(8, 64, 128)
    rows = jnp.concatenate([rows, rows], axis=1).reshape(2 * NS, 128)
    lanes = jnp.concatenate([left[n] for n in range(8)], axis=1)
    parts = jnp.dot(lanes, rows, preferred_element_type=F32)
    return pack_chunk(parts + pltpu.roll(parts, 64, 1))


def plain_pair(packed, n, out):
    first, second = packed[2 * n].astype(F32), packed[2 * n + 1].astype(F32)
    first, second = first + pltpu.roll(first, 64, 1), second + pltpu.roll(second, 64, 1)
    out[:, pl.ds(pl.multiple_of(n * 128, 128), 128)] = jnp.where(left_lanes(first.shape), first, second)


def to_plain(packed, out):
    for n in range(4):
        plain_pair(packed, n, out)


def packed_matvec(packed, vector):
    doubled = []
    for row in vector:
        doubled.append(jnp.concatenate([row[:, :64], row[:, :64]], axis=1))
        doubled.append(jnp.concatenate([row[:, 64:], row[:, 64:]], axis=1))
    out = []
    for g in range(4):
        total = None
        for n in range(8):
            term = packed[n, pl.ds(g * 128, 128), :].astype(F32) * doubled[n]
            total = term if total is None else total + term
        out.append(column_to_row(jnp.sum(total, axis=1, keepdims=True)))
    return out


def sum_rows(a, b):
    return [m + o for m, o in zip(a, b)]


def kernel(
    columns_count,
    vals_ref, gain_ref, obs_op_ref, cols_ref, blocks_ref, counts_ref, obs_values_ref, sources_ref, prior_ref,
    out_ref,
    third, packed, a_buf, b_buf, gain_buf, src_buf, cols_buf, blocks_buf, counts_buf,
    cols_smem, blocks_smem, counts_smem, op_buf, ov_buf,
    f_buf, fn_buf, e_buf, off_buf,
    maps, maps_q, chip, chip_q, before, before_q, left, left_q, first, first_q, last, whole, whole_q,
    mate, mate_q, plain_a, plain_b, plain_c, plain_d, plain_e, x_in, x_pair, x_mid, x_out, x_end, x_work, sweep_buf,
    send_in, recv_in, send_small, recv_small, send_obs, recv_obs, smem_sem,
    send_map, recv_map, send_before, recv_before, send_left, recv_left, send_first, recv_first,
    send_mate, recv_mate, send_vec, recv_vec, send_share, recv_share, send_on, recv_on,
    send_x, recv_x, recv_pair, send_out, recv_out, third_sem, send_end, prior_sem, send_whole, recv_whole,
):
    tm, y = lax.axis_index("tm"), lax.axis_index("state")
    core = lax.rem(tm, 2)
    column = tm // 2
    first_tm = tm - core
    other = 1 - core
    sibling = (first_tm + other, y)
    groups = (columns_count - 4) // 3
    single = column < 4
    grouped = jnp.logical_not(single)
    group = (column - 4) // 3
    place = column - 4 - 3 * group
    last_group = group == groups - 1

    def device(c, j):
        return 2 * c + core, j

    first_column = column == 0
    merges = column > 0
    at_last_chip = jnp.logical_and(y == 3, grouped)
    single_master = jnp.logical_and(y == 3, jnp.logical_and(single, merges))
    exits_first = jnp.logical_and(first_column, y == 3)
    is_master = jnp.logical_and(at_last_chip, place == 1)
    long_master = jnp.logical_and(is_master, jnp.logical_not(last_group))
    is_mate = jnp.logical_and(
        at_last_chip, jnp.logical_or(place == 0, jnp.logical_and(place == 2, jnp.logical_not(last_group)))
    )
    mate_slot = jnp.where(place == 2, 1, 0)
    partner = device(5 + 3 * group, 3)

    barrier = pltpu.get_barrier_semaphore()

    def greet(where):
        pl.semaphore_signal(barrier, inc=1, device_id=where, device_id_type=MESH)

    for c in range(2):
        for j in range(4):
            @pl.when(jnp.logical_or(c != core, j != y))
            def _():
                greet((first_tm + c, j))

    third_copy = pltpu.make_async_copy(vals_ref.at[:, :, :, pl.ds(128, 64)], third, third_sem)
    third_copy.start()
    prior_copy = pltpu.make_async_copy(prior_ref, x_in, prior_sem)
    starts = jnp.logical_and(column == 0, y == 0)

    @pl.when(starts)
    def _():
        prior_copy.start()


    from_before = jnp.logical_or(
        jnp.logical_and(column > 0, column <= 4), jnp.logical_and(grouped, place == 2)
    )
    from_earlier = jnp.logical_and(grouped, jnp.logical_and(place == 0, group > 0))
    earlier = device(jnp.where(group == 0, 3, 2 + 3 * group), 3)

    @pl.when(from_before)
    def _():
        greet(device(column - 1, 3))

    @pl.when(jnp.logical_or(from_earlier, is_master))
    def _():
        greet(earlier)

    @pl.when(is_master)
    def _():
        greet(device(column - 1, 3))

    @pl.when(long_master)
    def _():
        greet(device(column + 1, 3))

    last_single = jnp.logical_and(single_master, column == 3)
    peers = (
        7
        + jnp.where(jnp.logical_or(exits_first, jnp.logical_or(single_master, is_master)), 4, 0)
        + jnp.where(is_mate, 1, 0)
        + jnp.where(last_single, 1, 0)
        + jnp.where(long_master, 5, 0)
    )
    pl.semaphore_wait(barrier, peers)

    def target_of(b):
        return first_tm + b % 2, 2 * core + b // 2

    def is_me(b):
        dest_tm, dest_y = target_of(b)
        return jnp.logical_and(dest_tm == tm, dest_y == y)

    def remote(src, dst, send, recv, device):
        return pltpu.make_async_remote_copy(
            src_ref=src, dst_ref=dst, send_sem=send, recv_sem=recv, device_id=device, device_id_type=MESH
        )

    def small_pairs(b):
        start = pl.ds(8 * b, STEPS)
        return (
            (sources_ref.at[start], src_buf.at[y], 0),
            (cols_ref, cols_buf.at[y], 1),
        )

    def big_pairs(b, q):
        start, there = pl.ds(8 * b + CHUNK * q, CHUNK), pl.ds(CHUNK * q, CHUNK)
        return (
            (vals_ref.at[start, :, :, pl.ds(0, 128)], a_buf.at[y, there], 0),
            (packed.at[start], b_buf.at[y, there], 1),
            (gain_ref.at[start], gain_buf.at[y, there], 2),
        )

    def send_pair(b, src, dst, send, recv):
        @pl.when(jnp.logical_not(is_me(b)))
        def _():
            remote(src, dst, send, recv, target_of(b)).start()

        @pl.when(is_me(b))
        def _():
            pltpu.make_async_copy(src, dst, recv).start()

    for b in range(4):
        for src, dst, kind in small_pairs(b):
            send_pair(b, src, dst, send_small.at[b, kind], recv_small.at[y, kind])

    holds = core == y // 2
    first_step = 16 * lax.rem(y, 2) + 8 * core
    mine_at = pl.ds(first_step, STEPS)
    other_at = pl.ds(16 * lax.rem(y, 2) + 8 * other, STEPS)
    obs_arrays = (
        (obs_op_ref.at[mine_at], obs_op_ref.at[other_at], op_buf, 0),
        (obs_values_ref.at[mine_at], obs_values_ref.at[other_at], ov_buf, 1),
        (blocks_ref, blocks_ref, blocks_buf, 2),
        (counts_ref, counts_ref, counts_buf, 3),
    )

    @pl.when(holds)
    def _():
        for mine, others, dst, kind in obs_arrays:
            remote(others, dst, send_obs.at[kind], recv_obs.at[kind], sibling).start()
            pltpu.make_async_copy(mine, dst, recv_obs.at[kind]).start()

    def start_chunk(q, carry):
        for b in range(4):
            for src, dst, kind in big_pairs(b, q)[:1]:
                send_pair(b, src, dst, send_in.at[b, kind, q], recv_in.at[y, kind, q])

        @pl.when(q == 0)
        def _():
            third_copy.wait()

        for b in range(4):
            for t in range(CHUNK):
                at = 8 * b + CHUNK * q + t
                packed[at] = jnp.concatenate([third[at, 0], third[at, 1]], axis=1)
        for k in (1, 2):
            for b in range(4):
                src, dst, kind = big_pairs(b, q)[k]
                send_pair(b, src, dst, send_in.at[b, kind, q], recv_in.at[y, kind, q])
        return carry

    lax.fori_loop(0, NCHUNK, start_chunk, 0)

    def arrived(dst, sem):
        pltpu.make_async_copy(dst, dst, sem).wait()

    for j in range(4):
        arrived(src_buf.at[j], recv_small.at[j, 0])
        arrived(cols_buf.at[j], recv_small.at[j, 1])
    for _, _, dst, kind in obs_arrays:
        arrived(dst, recv_obs.at[kind])
    to_smem = [
        pltpu.make_async_copy(src, dst, smem_sem.at[k])
        for k, (src, dst) in enumerate(((cols_buf, cols_smem), (blocks_buf, blocks_smem), (counts_buf, counts_smem)))
    ]
    for copy in to_smem:
        copy.start()
    for copy in to_smem:
        copy.wait()

    lane64 = lax.broadcasted_iota(jnp.int32, (64, 128), 1)
    row64 = lax.broadcasted_iota(jnp.int32, (64, 128), 0)
    left64 = lane64 < 64
    half64 = lane64 // 64
    lane1 = lax.broadcasted_iota(jnp.int32, (1, 128), 1)

    maps_q[core] = jnp.zeros((4, 128), F32)

    def map_copy(h, k):
        return remote(maps.at[core, h], maps.at[core, h], send_map.at[k], recv_map.at[k], sibling)

    def step(s, carry):
        at = first_step + s

        @pl.when(lax.rem(s, CHUNK) == 0)
        def _():
            q = s // CHUNK
            there = pl.ds(CHUNK * q, CHUNK)
            for j in range(4):
                arrived(a_buf.at[j, there], recv_in.at[j, 0, q])
                arrived(b_buf.at[j, there], recv_in.at[j, 1, q])

        for j in range(4):
            thirds = b_buf[j, s].astype(F32)
            thirds_turned = pltpu.roll(thirds, 64, 1)
            for il in range(2):
                i = 2 * j + il
                pair = a_buf[j, s, il].astype(F32)
                turned = pltpu.roll(pair, 64, 1)
                block0 = jnp.where(left64, pair, turned)
                block1 = jnp.where(left64, turned, pair)
                block2 = jnp.where(left64 if il == 0 else jnp.logical_not(left64), thirds, thirds_turned)
                col1 = cols_smem[j, 1, il, at]
                col2 = cols_smem[j, 2, il, at]
                for p in range(4):
                    index = half64 + 2 * p
                    value = jnp.where(index == col1, block1, jnp.where(index == col2, block2, 0.0))
                    if p == j:
                        value = jnp.where(half64 == il, block0, value)
                    f_buf[i, :, p * 128 : (p + 1) * 128] = value
                    fn_buf[i, :, p * 128 : (p + 1) * 128] = value.astype(BF16)

        operator = op_buf[s].astype(F32)
        turned_operator = operator.T.astype(BF16)
        count = counts_smem[0, at]
        images, source_columns = [], []
        for o in range(2):
            block = blocks_smem[o, at]
            selected = fn_buf[block]
            images.append(jnp.dot(turned_operator[64 * o : 64 * o + 64], selected, preferred_element_type=F32))
            source_row = src_buf[block // 2, pl.ds(s, 1), :]
            offset = lax.rem(block, 2) * 64
            source_columns.append(
                jnp.sum(jnp.where(lane64 == row64 + offset, source_row, 0.0), axis=1, keepdims=True)
            )
        image = jnp.concatenate(images, axis=0)
        slot = lax.broadcasted_iota(jnp.int32, (128, NS), 0)
        masked = jnp.where(slot < count, image, 0.0).astype(BF16)

        @pl.when(lax.rem(s, CHUNK) == 0)
        def _():
            q = s // CHUNK
            for j in range(4):
                arrived(gain_buf.at[j, pl.ds(CHUNK * q, CHUNK)], recv_in.at[j, 2, q])

        gains = gain_buf[:, s].reshape(NS, 128)
        correction = jnp.dot(gains, masked, preferred_element_type=F32)
        e_buf[s] = (f_buf[...].reshape(NS, NS) - correction).astype(BF16)

        source_image = jnp.sum(
            operator * jnp.where(left64, source_columns[0], source_columns[1]), axis=0, keepdims=True
        )
        source_image = source_image.astype(BF16).astype(F32)
        innovation = jnp.where(lane1 < count, ov_buf[pl.ds(s, 1), :] - source_image, 0.0)
        offsets = []
        for g in range(4):
            moved = jnp.sum(gain_buf[g, s].astype(F32) * innovation, axis=1, keepdims=True)
            offsets.append(column_to_row(moved) + src_buf[g, pl.ds(s, 1), :])
        put_rows(off_buf.at[s], offsets)

        moved = matvec(block_of_plain(e_buf.at[s]), rows_of(maps_q.at[core]))
        put_rows(maps_q.at[core], [m + o for m, o in zip(moved, offsets)])

        @pl.when(s == 0)
        def _():
            for h in range(2):
                maps[core, h, 0] = e_buf[s, :, h * HALF : (h + 1) * HALF]
                maps[core, h, 1] = jnp.zeros((NS, HALF), BF16)

        @pl.when(s > 0)
        def _():
            for h, k in ((other, 0), (core, 2)):
                matrix = e_buf[s]
                value = jnp.dot(matrix, maps[core, h, 0], preferred_element_type=F32)
                value = value + jnp.dot(matrix, maps[core, h, 1], preferred_element_type=F32)
                maps[core, h, 0], maps[core, h, 1] = split(value)

                @pl.when(s == STEPS - 1)
                def _():
                    map_copy(h, k).start()

        return carry

    lax.fori_loop(0, STEPS, step, 0)

    q_copy = remote(maps_q.at[core], maps_q.at[core], send_map.at[1], recv_map.at[1], sibling)
    q_copy.start()
    arrived(maps.at[other, core], recv_map.at[0])
    mine = pl.ds(4 * core, 4)
    theirs = pl.ds(4 * other, 4)

    def to_chip(j):
        return tm, j

    def share(ref, k):
        return remote(ref.at[mine], ref.at[mine], send_share.at[k], recv_share.at[k], sibling)

    def shared(ref, k):
        arrived(ref.at[theirs], recv_share.at[k])

    def chip_before_copy(k):
        n = 4 * core + k
        return remote(chip.at[n], before.at[n], send_before.at[k], recv_before.at[k], to_chip(1))

    def chip_left_copy(k):
        n = 4 * core + k
        return remote(chip.at[n], left.at[n], send_left.at[k], recv_left.at[k], to_chip(3))

    def first_copy(k):
        return remote(first.at[k], first.at[k], send_first.at[k], recv_first.at[k], to_chip(3))

    first_before_copy = remote(first, before.at[mine], send_before.at[4], recv_before.at[4], to_chip(2))

    def mate_copy(k):
        n = 4 * core + k
        return remote(whole.at[n], mate.at[mate_slot, n], send_mate.at[k], recv_mate.at[mate_slot, k], partner)

    holds_whole = jnp.logical_or(is_master, single_master)

    def whole_on(k):
        n = 4 * core + k
        return remote(whole.at[n], whole.at[n], send_whole.at[k], recv_whole.at[k], sibling)

    def take_whole():
        for h in range(2):
            plain_pair(whole, 2 * core + h, plain_a)
        for k in range(4):
            arrived(whole.at[4 * other + k], recv_whole.at[k])
        for h in range(2):
            plain_pair(whole, 2 * other + h, plain_a)

    def mate_on(k, slot):
        n = 4 * core + k
        return remote(mate.at[slot, n], mate.at[slot, n], send_on.at[slot, k], recv_on.at[slot, k], sibling)

    vec_copies = (
        remote(chip_q, before_q, send_vec.at[0], recv_vec.at[0], to_chip(1)),
        remote(chip_q, left_q, send_vec.at[1], recv_vec.at[1], to_chip(3)),
        remote(first_q, first_q, send_vec.at[2], recv_vec.at[2], to_chip(3)),
        remote(first_q, before_q, send_vec.at[3], recv_vec.at[0], to_chip(2)),
        remote(whole_q, mate_q.at[mate_slot], send_vec.at[4], recv_vec.at[3 + mate_slot], partner),
    )

    def chunks(step):
        def one(k, carry):
            step(k)
            return carry

        lax.fori_loop(0, 4, one, 0)

    def right(h):
        return maps.at[0, core, :, :, pl.ds(128 * h, 128)]

    for h in range(2):
        plain_c[:, h * 128 : (h + 1) * 128] = half_product(maps.at[1], right(h), 0)

    @pl.when(core == 0)
    def _():
        arrived(maps.at[other, other], recv_map.at[2])

    for h in range(2):
        total = plain_c[:, h * 128 : (h + 1) * 128] + half_product(maps.at[1], right(h), 1)
        chip[4 * core + 2 * h], chip[4 * core + 2 * h + 1] = pack_pair(total)
        for k in (2 * h, 2 * h + 1):
            @pl.when(jnp.logical_and(merges, y == 0))
            def _():
                chip_before_copy(k).start()

            @pl.when(jnp.logical_and(merges, y == 2))
            def _():
                chip_left_copy(k).start()

    shares_chip = jnp.logical_or(first_column, lax.rem(y, 2) == 1)

    @pl.when(shares_chip)
    def _():
        share(chip, 0).start()

    @pl.when(core == 1)
    def _():
        arrived(maps.at[other, other], recv_map.at[2])

    arrived(maps_q.at[other], recv_map.at[1])
    half_map(maps.at[0], plain_c)
    half_map(maps.at[1], plain_b)
    moved = matvec(block_of_plain(plain_b), rows_of(maps_q.at[0]))
    put_rows(chip_q, sum_rows(moved, rows_of(maps_q.at[1])))

    @pl.when(merges & (y == 0))
    def _():
        vec_copies[0].start()

    @pl.when(merges & (y == 2))
    def _():
        vec_copies[1].start()

    @pl.when(shares_chip)
    def _():
        shared(chip, 0)

    def entry():
        @pl.when(jnp.logical_or(from_before, from_earlier))
        def _():
            arrived(x_in, recv_x)

    def apply(plain, vector, shift, out):
        moved = matvec(block_of_plain(plain), rows_of(vector))
        put_rows(out, [m + o for m, o in zip(moved, rows_of(shift))])

    def pair_copy(source, there):
        return remote(source, x_pair, send_x.at[8], recv_pair, device(there, 3))

    def next_copy(j):
        return remote(x_out, x_in, send_x.at[j], recv_x, device(column + 1, j))

    def middle_copy(j):
        return remote(x_mid, x_in, send_x.at[4 + j], recv_x, device(column, j))

    def end_copy(j):
        return remote(x_end, x_in, send_end.at[j], recv_x, device(column + 2, j))

    along_copy = remote(x_out, x_in, send_end.at[0], recv_x, to_chip(lax.rem(y + 1, 4)))

    @pl.when(first_column)
    def _():
        @pl.when(y == 0)
        def _():
            prior_copy.wait()

        @pl.when(y > 0)
        def _():
            arrived(x_in, recv_x)

        put_rows(x_out, sum_rows(packed_matvec(chip, rows_of(x_in)), rows_of(chip_q)))

        @pl.when(y < 3)
        def _():
            along_copy.start()

        @pl.when(y == 3)
        def _():
            for j in (3, 2, 1, 0):
                next_copy(j).start()

    @pl.when(merges & (y == 1))
    def _():
        def one(k):
            n = 4 * core + k
            arrived(before.at[n], recv_before.at[k])
            first[k] = chunk_product(chip, before[n])
            first_copy(k).start()

        chunks(one)
        first_before_copy.start()
        share(before, 1).start()
        arrived(before_q, recv_vec.at[0])
        put_rows(first_q, sum_rows(packed_matvec(chip, rows_of(before_q)), rows_of(chip_q)))
        vec_copies[2].start()
        vec_copies[3].start()

    @pl.when(merges & (y == 2))
    def _():
        arrived(before.at[mine], recv_before.at[4])
        share(before, 1).start()
        arrived(before_q, recv_vec.at[0])

    @pl.when(merges & (y == 3))
    def _():
        def one_last(k):
            n = 4 * core + k
            arrived(left.at[n], recv_left.at[k])
            last[n] = chunk_product(chip, left[n])

        chunks(one_last)
        share(last, 2).start()
        share(left, 3).start()
        arrived(left_q, recv_vec.at[1])
        put_rows(whole_q, sum_rows(packed_matvec(chip, rows_of(left_q)), rows_of(chip_q)))
        shared(last, 2)

        def one_whole(k):
            n = 4 * core + k
            arrived(first.at[k], recv_first.at[k])
            whole[n] = chunk_product(last, first[k])

            @pl.when(is_mate)
            def _():
                mate_copy(k).start()

            @pl.when(holds_whole)
            def _():
                whole_on(k).start()

        chunks(one_whole)

        arrived(first_q, recv_vec.at[2])
        put_rows(whole_q, sum_rows(packed_matvec(last, rows_of(first_q)), rows_of(whole_q)))

        @pl.when(is_mate)
        def _():
            vec_copies[4].start()

    @pl.when(single_master)
    def _():
        take_whole()
        entry()
        apply(plain_a, x_in, whole_q, x_out)

        @pl.when(last_single)
        def _():
            pair_copy(x_out, 5).start()

        for j in (3, 2, 1, 0):
            next_copy(j).start()

    @pl.when(merges & (y == 3))
    def _():
        shared(left, 3)

        def one_before(k):
            before[4 * core + k] = chunk_product(left, first[k])

        chunks(one_before)
        share(before, 1).start()
        put_rows(before_q, sum_rows(packed_matvec(left, rows_of(first_q)), rows_of(left_q)))

    def inputs_sent():
        for b in range(4):
            @pl.when(jnp.logical_not(is_me(b)))
            def _():
                for src, dst, kind in small_pairs(b):
                    remote(src, dst, send_small.at[b, kind], recv_small.at[y, kind], target_of(b)).wait_send()

        def finish_chunk(q, carry):
            for b in range(4):
                @pl.when(jnp.logical_not(is_me(b)))
                def _():
                    for src, dst, kind in big_pairs(b, q):
                        remote(src, dst, send_in.at[b, kind, q], recv_in.at[y, kind, q], target_of(b)).wait_send()
            return carry

        lax.fori_loop(0, NCHUNK, finish_chunk, 0)

        @pl.when(holds)
        def _():
            for mine, others, dst, kind in obs_arrays:
                remote(others, dst, send_obs.at[kind], recv_obs.at[kind], sibling).wait_send()

    @pl.when(is_master)
    def _():
        take_whole()
        inputs_sent()

        def one_mate(k, slot, plain):
            arrived(mate.at[slot, 4 * core + k], recv_mate.at[slot, k])
            mate_on(k, slot).start()

            @pl.when(lax.rem(k, 2) == 1)
            def _():
                plain_pair(mate.at[slot], 2 * core + k // 2, plain)

        def both(k):
            one_mate(k, 0, plain_d)

            @pl.when(long_master)
            def _():
                one_mate(k, 1, plain_e)

        chunks(both)

    @pl.when(merges & (y > 0))
    def _():
        shared(before, 1)
        to_plain(before, plain_b)

    def take_mate(slot, plain):
        arrived(mate_q.at[slot], recv_vec.at[3 + slot])
        for k in range(4):
            arrived(mate.at[slot, 4 * other + k], recv_on.at[slot, k])
        for h in range(2):
            plain_pair(mate.at[slot], 2 * other + h, plain)

    @pl.when(jnp.logical_not(is_master))
    def _():
        inputs_sent()

    @pl.when(jnp.logical_not(single_master))
    def _():
        @pl.when(is_master)
        def _():
            take_mate(0, plain_d)

            @pl.when(long_master)
            def _():
                take_mate(1, plain_e)

        entry()

    @pl.when(is_master)
    def _():
        arrived(x_pair, recv_pair)
        apply(plain_d, x_pair, mate_q.at[0], x_mid)
        apply(plain_a, x_mid, whole_q, x_out)

        @pl.when(long_master)
        def _():
            apply(plain_e, x_out, mate_q.at[1], x_end)
            pair_copy(x_end, column + 3).start()
            for j in range(4):
                end_copy(j).start()

        for j in range(4):
            next_copy(j).start()
        for j in range(3):
            middle_copy(j).start()
        x_in[...] = x_mid[...]

    @pl.when(jnp.logical_and(grouped, jnp.logical_and(place == 1, y < 3)))
    def _():
        arrived(x_in, recv_x)

    enters = jnp.logical_or(first_column, y == 0)

    @pl.when(enters)
    def _():
        x_work[...] = x_in[...]

    @pl.when(jnp.logical_not(enters))
    def _():
        moved = matvec(block_of_plain(plain_b), rows_of(x_in))
        put_rows(x_work, [m + o for m, o in zip(moved, rows_of(before_q))])

    @pl.when(core == 1)
    def _():
        moved = matvec(block_of_plain(plain_c), rows_of(x_work))
        put_rows(x_work, [m + o for m, o in zip(moved, rows_of(maps_q.at[0]))])

    def sweep(s, carry):
        moved = matvec(block_of_plain(e_buf.at[s]), list(carry))
        rows = [m + o for m, o in zip(moved, rows_of(off_buf.at[s]))]
        for g in range(4):
            sweep_buf[g, pl.ds(s, 1), :] = rows[g]
        return tuple(rows)

    lax.fori_loop(0, STEPS, sweep, tuple(rows_of(x_work)))

    owner = first_tm + y // 2
    out_block = 2 * lax.rem(y, 2) + core
    here = pl.ds(8 * out_block, STEPS)

    def own_rows(g):
        return jnp.logical_and(owner == tm, g == y)

    for g in range(4):
        src, dst = sweep_buf.at[g], out_ref.at[here]

        @pl.when(jnp.logical_not(own_rows(g)))
        def _():
            remote(src, dst, send_out.at[g], recv_out.at[out_block], (owner, g)).start()

        @pl.when(own_rows(g))
        def _():
            pltpu.make_async_copy(src, dst, recv_out.at[out_block]).start()

    for b in range(4):
        arrived(out_ref.at[pl.ds(8 * b, STEPS)], recv_out.at[b])

    for g in range(4):
        @pl.when(jnp.logical_not(own_rows(g)))
        def _():
            remote(sweep_buf.at[g], out_ref.at[here], send_out.at[g], recv_out.at[out_block], (owner, g)).wait_send()

    map_copy(other, 0).wait_send()
    map_copy(core, 2).wait_send()
    q_copy.wait_send()

    @pl.when(merges & (y == 0))
    def _():
        chunks(lambda k: chip_before_copy(k).wait_send())
        vec_copies[0].wait_send()

    @pl.when(merges & (y == 1))
    def _():
        chunks(lambda k: first_copy(k).wait_send())
        first_before_copy.wait_send()
        vec_copies[2].wait_send()
        vec_copies[3].wait_send()

    @pl.when(merges & (y == 2))
    def _():
        chunks(lambda k: chip_left_copy(k).wait_send())
        vec_copies[1].wait_send()

    @pl.when(shares_chip)
    def _():
        share(chip, 0).wait_send()

    @pl.when(first_column)
    def _():
        @pl.when(y < 3)
        def _():
            along_copy.wait_send()

        @pl.when(y == 3)
        def _():
            for j in range(4):
                next_copy(j).wait_send()

    @pl.when(merges & (y > 0))
    def _():
        share(before, 1).wait_send()

    @pl.when(merges & (y == 3))
    def _():
        share(last, 2).wait_send()
        share(left, 3).wait_send()

    @pl.when(is_mate)
    def _():
        chunks(lambda k: mate_copy(k).wait_send())
        vec_copies[4].wait_send()

    @pl.when(jnp.logical_or(is_master, single_master))
    def _():
        chunks(lambda k: whole_on(k).wait_send())
        for j in range(4):
            next_copy(j).wait_send()

    @pl.when(is_master)
    def _():
        chunks(lambda k: mate_on(k, 0).wait_send())
        for j in range(3):
            middle_copy(j).wait_send()

    @pl.when(long_master)
    def _():
        chunks(lambda k: mate_on(k, 1).wait_send())
        for j in range(4):
            end_copy(j).wait_send()
        pair_copy(x_end, column + 3).wait_send()

    @pl.when(last_single)
    def _():
        pair_copy(x_out, 5).wait_send()


def body(dyn_cols, dyn_vals, obs_blocks, obs_op, obs_counts, obs_values, gain, sources, prior):
    count = dyn_vals.shape[0]
    columns_count = lax.axis_size("tm") // 2
    cols = jnp.transpose(dyn_cols, (2, 1, 0))
    blocks = jnp.transpose(obs_blocks, (1, 0))
    counts = obs_counts.reshape(1, count)
    prior_rows = prior.reshape(4, 128)
    vmem = pl.BlockSpec(memory_space=pltpu.VMEM)
    hbm = pl.BlockSpec(memory_space=pl.ANY)
    dma = pltpu.SemaphoreType.DMA
    a_map = (2, 2, NS, HALF)
    packed_map = (8, NS, 128)

    def call(*refs):
        kernel(columns_count, *refs)

    return pl.pallas_call(
        call,
        out_shape=pltpu.VMEM((count, 128), F32),
        in_specs=[hbm] * 9,
        out_specs=vmem,
        scratch_shapes=[
            pltpu.VMEM((count, 2, 64, 64), BF16),
            pltpu.VMEM((count, 64, 128), BF16),
            pltpu.VMEM((4, STEPS, 2, 64, 128), BF16),
            pltpu.VMEM((4, STEPS, 64, 128), BF16),
            pltpu.VMEM((4, STEPS, 128, 128), BF16),
            pltpu.VMEM((4, STEPS, 128), F32),
            pltpu.VMEM((4, *cols.shape), jnp.int32),
            pltpu.VMEM(blocks.shape, jnp.int32),
            pltpu.VMEM(counts.shape, jnp.int32),
            pltpu.SMEM((4, *cols.shape), jnp.int32),
            pltpu.SMEM(blocks.shape, jnp.int32),
            pltpu.SMEM(counts.shape, jnp.int32),
            pltpu.VMEM((STEPS, 64, 128), BF16),
            pltpu.VMEM((STEPS, 128), F32),
            pltpu.VMEM((8, 64, NS), F32),
            pltpu.VMEM((8, 64, NS), BF16),
            pltpu.VMEM((STEPS, NS, NS), BF16),
            pltpu.VMEM((STEPS, 4, 128), F32),
            pltpu.VMEM((2, *a_map), BF16),
            pltpu.VMEM((2, 4, 128), F32),
            pltpu.VMEM(packed_map, BF16),
            pltpu.VMEM((4, 128), F32),
            pltpu.VMEM(packed_map, BF16),
            pltpu.VMEM((4, 128), F32),
            pltpu.VMEM(packed_map, BF16),
            pltpu.VMEM((4, 128), F32),
            pltpu.VMEM((4, NS, 128), BF16),
            pltpu.VMEM((4, 128), F32),
            pltpu.VMEM(packed_map, BF16),
            pltpu.VMEM(packed_map, BF16),
            pltpu.VMEM((4, 128), F32),
            pltpu.VMEM((2, *packed_map), BF16),
            pltpu.VMEM((2, 4, 128), F32),
            pltpu.VMEM((NS, NS), F32),
            pltpu.VMEM((NS, NS), F32),
            pltpu.VMEM((NS, NS), F32),
            pltpu.VMEM((NS, NS), F32),
            pltpu.VMEM((NS, NS), F32),
            pltpu.VMEM((4, 128), F32),
            pltpu.VMEM((4, 128), F32),
            pltpu.VMEM((4, 128), F32),
            pltpu.VMEM((4, 128), F32),
            pltpu.VMEM((4, 128), F32),
            pltpu.VMEM((4, 128), F32),
            pltpu.VMEM((4, STEPS, 128), F32),
            dma((4, 3, NCHUNK)), dma((4, 3, NCHUNK)),
            dma((4, 2)), dma((4, 2)),
            dma((4,)), dma((4,)), dma((3,)),
            dma((3,)), dma((3,)), dma((5,)), dma((5,)), dma((4,)), dma((4,)), dma((4,)), dma((4,)),
            dma((4,)), dma((2, 4)), dma((5,)), dma((5,)), dma((5,)), dma((5,)), dma((2, 4)), dma((2, 4)),
            dma((9,)), dma, dma, dma((4,)), dma((4,)), dma, dma((4,)), dma, dma((4,)), dma((4,)),
        ],
        compiler_params=pltpu.CompilerParams(
            collective_id=0, has_side_effects=True, vmem_limit_bytes=58 * 1024 * 1024
        ),
        cost_estimate=pl.CostEstimate(flops=10_000_000_000, bytes_accessed=4_000_000, transcendentals=0),
    )(dyn_vals, gain, obs_op, cols, blocks, counts, obs_values, sources, prior_rows)


def solution(mesh):
    return jax.shard_map(
        body,
        mesh=mesh,
        in_specs=(
            P("tm", "state", None),
            P("tm", "state", None, None),
            P("tm", None),
            P("tm", None, None),
            P("tm"),
            P("tm", None),
            P("tm", "state", None),
            P("tm", "state"),
            P(),
        ),
        out_specs=P("tm", "state"),
        check_vma=False,
    )
```
